512 devices in a mesh: grid: 32 (over y, x, core), head: 16 (over z).
Axes of the slice: x: 4, y: 4, z: 16, core: 2. Of those that a mesh axis runs over, the one named last changes fastest.
Arguments:
- grid_feat: bfloat16 [32768, 1024], P('grid'), may hold values from -6 to 6
- mesh_feat: bfloat16 [8192, 1024], P('grid'), may hold values from -6 to 6
- query_weight: bfloat16 [1024, 1024], P(None, 'head'), may hold values from -0.1875 to 0.1875
- key_weight: bfloat16 [1024, 1024], P(None, 'head'), may hold values from -0.1875 to 0.1875
- value_weight: bfloat16 [1024, 1024], P(None, 'head'), may hold values from -0.1875 to 0.1875
- enc_out_weight: bfloat16 [1024, 1024], P('head'), may hold values from -0.75 to 0.75
- layer_query: bfloat16 [1024, 1024], P(None, 'head'), may hold values from -0.1875 to 0.1875
- layer_key: bfloat16 [1024, 1024], P(None, 'head'), may hold values from -0.1875 to 0.1875
- layer_value: bfloat16 [1024, 1024], P(None, 'head'), may hold values from -0.1875 to 0.1875
- layer_out_weight: bfloat16 [1024, 1024], P('head'), may hold values from -0.75 to 0.75
- enc_bias: float32 [64, 30, 16], P('grid', None, 'head'), may hold values from -4 to 360
- layer_bias: float32 [64, 3, 16], P('grid', None, 'head'), may hold values from -4 to 360
- send_list: int32 [32, 32], P('grid'), may hold values from 0 to 7
- edge_slot: int32 [64, 30], P('grid'), may hold values from 0 to 39, as said below
- edge_count: int32 [64], P('grid'), may hold values from 2 to 30, as said below
- cotangent: bfloat16 [8192, 1024], P(('grid', 'head')), may hold values from -6 to 6
Outputs:
- mesh_out: bfloat16 [8192, 1024], P(('grid', 'head'))
- key_grad: float32 [1024, 1024], P('grid', 'head')
- value_grad: float32 [1024, 1024], P('grid', 'head')
The draws below stay inside these ranges and needn't reach their ends.
Inputs may be any that keep to these rules, and one draw needn't show every extreme that they name: `edge_slot`: row m lists the grid blocks read by mesh block m of grid shard s = m // 2: an entry below 8 is a block of shard s, an entry 8 + p is the block that shard p (never s) sends to s. The first edge_count[m] entries are live and distinct, the others are 0. Over the 2 mesh blocks of a shard, each of its 8 blocks and each of the other shards' blocks is read exactly once. `edge_count`: the counts of the 2 mesh blocks of a grid shard sum to 39, and one of them equals 30. `send_list`: entry [s, p] is the block of grid shard s, counted within that shard, that s sends to shard p; diagonal entries are not read.
All inputs are finite; a program needn't handle non-finite values.
Results may differ from the reference program's by a relative error of at most 0.029.
Values may be sent and summed in bfloat16 or wider, within the bound.
No kernel may reach another device: no remote copies, remote signals or barrier semaphores. Data moves between devices by JAX's collectives and lax.ppermute only.
A program may use at most 64 MiB of HBM per device.

```python
import jax
import jax.numpy as jnp
from jax import lax

C = 1024
HEADS = 16
HEAD_DIM = 64
BLOCK = 128
GB = 8
MB = 2
GRID = 32768
MESH = 8192
CAND = 39
EDGES = 30
N_GRID = 32


def edge_tables(key):
    key = jax.random.fold_in(key, 11)
    shard_keys = jax.random.split(key, N_GRID)

    def one_shard(shard_key, shard_index):
        order_key, full_key, split_key = jax.random.split(shard_key, 3)
        others = GB + (shard_index + 1 + jnp.arange(N_GRID - 1, dtype=jnp.int32)) % N_GRID
        candidates = jnp.concatenate([jnp.arange(GB, dtype=jnp.int32), others.astype(jnp.int32)])
        shuffled = jax.random.permutation(order_key, candidates)
        full_block = jax.random.randint(full_key, (), 0, MB, dtype=jnp.int32)
        block_ids = jnp.arange(MB, dtype=jnp.int32)
        is_full = block_ids == full_block
        share_weights = jnp.where(is_full, 0, jax.random.randint(split_key, (MB,), 1, 4, dtype=jnp.int32))
        spare_room = CAND - EDGES - 2 * (MB - 1)
        lengths = jnp.where(is_full, 0, 2 + spare_room * share_weights // jnp.maximum(jnp.sum(share_weights), 1))
        leftover = CAND - EDGES - jnp.sum(lengths)
        first_other = jnp.where(full_block == 0, 1, 0)
        lengths = lengths + jnp.where(block_ids == first_other, leftover, 0)
        lengths = jnp.where(is_full, EDGES, lengths).astype(jnp.int32)
        starts = jnp.cumsum(lengths) - lengths
        position = starts[:, None] + jnp.arange(EDGES, dtype=jnp.int32)[None, :]
        live_edges = jnp.arange(EDGES, dtype=jnp.int32)[None, :] < lengths[:, None]
        slot_table = jnp.where(live_edges, shuffled[jnp.minimum(position, CAND - 1)], 0)
        return (slot_table.astype(jnp.int32), lengths)
    slot_table, lengths = jax.vmap(one_shard)(shard_keys, jnp.arange(N_GRID, dtype=jnp.int32))
    return (slot_table.reshape(MB * N_GRID, EDGES), lengths.reshape(MB * N_GRID))


def bias_values(key, edge_total, boost_share):
    base_key, pick_key, level_key, gap_key = jax.random.split(key, 4)
    base = jax.random.uniform(base_key, (MB * N_GRID, edge_total, HEADS), jnp.float32, -4.0, 4.0)
    chosen = jax.random.uniform(pick_key, (MB * N_GRID, 1, HEADS), jnp.float32) < boost_share
    level = 120.0 * jax.random.randint(level_key, (MB * N_GRID, 1, HEADS), 1, 4).astype(jnp.float32)
    spacing = jax.random.uniform(gap_key, (MB * N_GRID, 1, HEADS), jnp.float32, 1.0, 3.0)
    position = jnp.arange(edge_total, dtype=jnp.int32)[None, :, None]
    boosted = jnp.where(position == 0, level, jnp.where(position == 1, level - spacing, base))
    return jnp.where(chosen, boosted, base)


def draw_edge_slot(key, part):
    return edge_tables(key)[0]


def draw_edge_count(key, part):
    return edge_tables(key)[1]


def draw_enc_bias(key, part):
    key = jax.random.fold_in(key, 23)
    boost_share = 0.0
    return bias_values(key, EDGES, boost_share)


def draw_layer_bias(key, part):
    key = jax.random.fold_in(key, 37)
    boost_share = 0.0
    return bias_values(key, 3, boost_share)


def set_ends(result, key, least, high):
    longest = result.shape.index(max(result.shape))
    spots = []
    for shift in (0, 1):
        where = [jax.random.randint(jax.random.fold_in(key, axis), (), 0, length) for axis, length in enumerate(result.shape)]
        where[longest] = (where[longest] + shift) % result.shape[longest]
        spots.append(tuple(where))
    return result.at[spots[0]].set(least).at[spots[1]].set(high)


def shard_levels(stream_key, dims, shards, least, top_value):
    factor_of = 1.0
    for axis_at, blocks in shards:
        steps = jax.random.uniform(jax.random.fold_in(jax.random.fold_in(stream_key, 6), axis_at), (blocks,), jnp.float32, least / len(shards), top_value / len(shards))
        factor_of = factor_of * jnp.repeat(jnp.exp(steps), dims[axis_at] // blocks).reshape((-1,) + (1,) * (len(dims) - 1 - axis_at))
    return factor_of


def gaussian(own_key, dims, spread, bound, cuts=(), held_as=jnp.bfloat16):
    factor_of = shard_levels(own_key, dims, cuts, -0.22, 0.18) if cuts else 1.0
    drawn = jax.random.normal(own_key, dims, jnp.float32) * spread * factor_of
    return jnp.minimum(jnp.maximum(drawn, -bound), bound).astype(held_as)


def setup_inputs(seed: int = 0) -> dict:
    splits = jax.random.split(jax.random.key(seed), 17)
    grid_feat = gaussian(splits[0], (GRID, C), 1.0, 6.0, ((0, 32),))
    mesh_feat = gaussian(splits[1], (MESH, C), 1.0, 6.0, ((0, 32),))
    query_weight = gaussian(splits[2], (C, C), C ** -0.5, 0.1875, ((1, 16),))
    key_weight = gaussian(splits[3], (C, C), C ** -0.5, 0.1875, ((1, 16),))
    value_weight = gaussian(splits[4], (C, C), C ** -0.5, 0.1875, ((1, 16),))
    enc_out_weight = gaussian(splits[5], (C, C), HEAD_DIM ** -0.5, 0.75, ((0, 16),))
    layer_query = gaussian(splits[6], (C, C), C ** -0.5, 0.1875, ((1, 16),))
    layer_key = gaussian(splits[7], (C, C), C ** -0.5, 0.1875, ((1, 16),))
    layer_value = gaussian(splits[8], (C, C), C ** -0.5, 0.1875, ((1, 16),))
    layer_out_weight = gaussian(splits[9], (C, C), HEAD_DIM ** -0.5, 0.75, ((0, 16),))
    enc_bias = draw_enc_bias(jax.random.fold_in(splits[16], 71), 0)
    layer_bias = draw_layer_bias(jax.random.fold_in(splits[16], 71), 0)
    send_list = set_ends(jax.random.randint(splits[12], (N_GRID, N_GRID), 0, GB), jax.random.fold_in(splits[12], 1), 0, GB - 1).astype(jnp.int32)
    edge_slot = draw_edge_slot(jax.random.fold_in(splits[16], 71), 0)
    edge_count = draw_edge_count(jax.random.fold_in(splits[16], 71), 0)
    cotangent = gaussian(splits[15], (MESH, C), 1.0, 6.0, ((0, 512),))
    return {"grid_feat": grid_feat, "mesh_feat": mesh_feat, "query_weight": query_weight, "key_weight": key_weight, "value_weight": value_weight, "enc_out_weight": enc_out_weight, "layer_query": layer_query, "layer_key": layer_key, "layer_value": layer_value, "layer_out_weight": layer_out_weight, "enc_bias": enc_bias, "layer_bias": layer_bias, "send_list": send_list, "edge_slot": edge_slot, "edge_count": edge_count, "cotangent": cotangent}


epsilon = 1e-05
score_scale = 0.125

def normalize(matrix):
    values = matrix.astype(jnp.float32)
    center = values - lax.optimization_barrier(jnp.mean(values, axis=-1, keepdims=True))
    inverse = lax.rsqrt(lax.optimization_barrier(jnp.mean(center * center, axis=-1, keepdims=True)) + epsilon)
    return (center * inverse, inverse)

def norm_back(grad_unit, unit_rows, inverse):
    mean_grad = lax.optimization_barrier(jnp.mean(grad_unit, axis=-1, keepdims=True))
    mean_both = lax.optimization_barrier(jnp.mean(grad_unit * unit_rows, axis=-1, keepdims=True))
    return inverse * (grad_unit - mean_grad - unit_rows * mean_both)

def widened(array):
    return lax.optimization_barrier(array.astype(jnp.bfloat16)).astype(jnp.float32)

def dot_right(left_rows, right_rows):
    return lax.dot_general(left_rows, right_rows, (((1,), (1,)), ((), ())), preferred_element_type=jnp.float32)

def dot_left(left_rows, right_rows):
    return lax.dot_general(left_rows, right_rows, (((0,), (0,)), ((), ())), preferred_element_type=jnp.float32)

def probabilities(query_rows, key_rows, bias_table, live_edges):
    scores = jnp.einsum('rhd,shd->hrs', query_rows.astype(jnp.float32), key_rows.astype(jnp.float32))
    heads_here, row_total, key_total = scores.shape
    edge_total = bias_table.shape[1]
    scores = scores.reshape(heads_here, row_total, edge_total, key_total // edge_total) * score_scale
    scores = scores + bias_table[:, None, :, None]
    scores = jnp.where(live_edges[None, None, :, None], scores, -jnp.inf)
    scores = scores.reshape(heads_here, row_total, key_total)
    highest = lax.optimization_barrier(jnp.max(scores, axis=-1, keepdims=True))
    raised = jnp.exp(scores - highest)
    return raised / lax.optimization_barrier(jnp.sum(raised, axis=-1, keepdims=True))

def combine(soft_weights, value_rows):
    mixed_rows = jnp.einsum('hrs,shd->rhd', widened(soft_weights), value_rows.astype(jnp.float32))
    return mixed_rows.astype(jnp.bfloat16)

def attend_back(query_rows, key_rows, value_rows, soft_weights, grad_rows, with_query):
    grad_wide = grad_rows.astype(jnp.float32)
    grad_soft = jnp.einsum('rhd,shd->hrs', grad_wide, value_rows.astype(jnp.float32))
    inner_sum = lax.optimization_barrier(jnp.sum(soft_weights * grad_soft, axis=-1, keepdims=True))
    grad_scores = widened(soft_weights * (grad_soft - inner_sum) * score_scale)
    grad_keys = jnp.einsum('hrs,rhd->shd', grad_scores, query_rows.astype(jnp.float32))
    grad_values = jnp.einsum('hrs,rhd->shd', widened(soft_weights), grad_wide)
    if with_query:
        grad_query = jnp.einsum('hrs,shd->rhd', grad_scores, key_rows.astype(jnp.float32))
        return (grad_query, grad_keys, grad_values)
    return (None, grad_keys, grad_values)

def reference(grid_feat, mesh_feat, query_weight, key_weight, value_weight, enc_out_weight, layer_query, layer_key, layer_value, layer_out_weight, enc_bias, layer_bias, send_list, edge_slot, edge_count, cotangent):
    mesh_blocks = MB * N_GRID
    grid_blocks = GB * N_GRID
    grid_unit, unused_scale = normalize(grid_feat)
    grid_norm = grid_unit.astype(jnp.bfloat16)
    grid_keys = jnp.dot(grid_norm, key_weight, preferred_element_type=jnp.float32).astype(jnp.bfloat16)
    grid_values = jnp.dot(grid_norm, value_weight, preferred_element_type=jnp.float32).astype(jnp.bfloat16)
    mesh_unit, unused_scale = normalize(mesh_feat)
    queries = jnp.dot(mesh_unit.astype(jnp.bfloat16), query_weight, preferred_element_type=jnp.float32).astype(jnp.bfloat16)
    shard_of = (jnp.arange(mesh_blocks, dtype=jnp.int32) // MB)[:, None]
    peer_of = jnp.clip(edge_slot - GB, 0, N_GRID - 1).astype(jnp.int32)
    remote_block = send_list[peer_of, shard_of]
    source = jnp.where(edge_slot < GB, shard_of * GB + edge_slot, peer_of * GB + remote_block).astype(jnp.int32)
    live_table = jnp.arange(EDGES, dtype=jnp.int32)[None, :] < edge_count[:, None]
    key_blocks = grid_keys.reshape(grid_blocks, BLOCK, HEADS, HEAD_DIM)
    value_blocks = grid_values.reshape(grid_blocks, BLOCK, HEADS, HEAD_DIM)
    query_blocks = queries.reshape(mesh_blocks, BLOCK, HEADS, HEAD_DIM)
    block_ids = jnp.arange(mesh_blocks, dtype=jnp.int32)

    def enc_sources(block_index):
        picked = source[block_index]
        key_rows = key_blocks[picked].reshape(EDGES * BLOCK, HEADS, HEAD_DIM)
        value_rows = value_blocks[picked].reshape(EDGES * BLOCK, HEADS, HEAD_DIM)
        return (key_rows, value_rows)

    def enc_weights(block_index, key_rows):
        return probabilities(query_blocks[block_index], key_rows, enc_bias[block_index].T, live_table[block_index])

    def enc_forward(block_index):
        key_rows, value_rows = enc_sources(block_index)
        return combine(enc_weights(block_index, key_rows), value_rows)
    enc_heads = lax.map(enc_forward, block_ids).reshape(MESH, C)
    encoded = mesh_feat.astype(jnp.float32) + jnp.dot(enc_heads, enc_out_weight, preferred_element_type=jnp.float32)
    enc_unit, enc_inverse = normalize(encoded)
    layer_in = enc_unit.astype(jnp.bfloat16)
    layer_q = jnp.dot(layer_in, layer_query, preferred_element_type=jnp.float32).astype(jnp.bfloat16).reshape(mesh_blocks, BLOCK, HEADS, HEAD_DIM)
    layer_k = jnp.dot(layer_in, layer_key, preferred_element_type=jnp.float32).astype(jnp.bfloat16).reshape(mesh_blocks, BLOCK, HEADS, HEAD_DIM)
    layer_v = jnp.dot(layer_in, layer_value, preferred_element_type=jnp.float32).astype(jnp.bfloat16).reshape(mesh_blocks, BLOCK, HEADS, HEAD_DIM)
    offsets = jnp.arange(3, dtype=jnp.int32) - 1
    all_live = jnp.ones((3,), dtype=jnp.bool_)

    def layer_sources(block_index):
        beside_all = (block_index + offsets) % mesh_blocks
        key_rows = layer_k[beside_all].reshape(3 * BLOCK, HEADS, HEAD_DIM)
        value_rows = layer_v[beside_all].reshape(3 * BLOCK, HEADS, HEAD_DIM)
        return (beside_all, key_rows, value_rows)

    def layer_soft_of(block_index, key_rows):
        return probabilities(layer_q[block_index], key_rows, layer_bias[block_index].T, all_live)

    def layer_forward(block_index):
        beside_all, key_rows, value_rows = layer_sources(block_index)
        return combine(layer_soft_of(block_index, key_rows), value_rows)
    layer_heads = lax.map(layer_forward, block_ids).reshape(MESH, C)
    mixed_rows = encoded + jnp.dot(layer_heads, layer_out_weight, preferred_element_type=jnp.float32)
    mesh_out = mixed_rows.astype(jnp.bfloat16)
    grad_layer = dot_right(cotangent, layer_out_weight).astype(jnp.bfloat16).reshape(mesh_blocks, BLOCK, HEADS, HEAD_DIM)

    def layer_back(running, block_index):
        grad_key_total, grad_value_total = running
        beside_all, key_rows, value_rows = layer_sources(block_index)
        soft_weights = layer_soft_of(block_index, key_rows)
        grad_query, grad_keys, grad_values = attend_back(layer_q[block_index], key_rows, value_rows, soft_weights, grad_layer[block_index], True)
        grad_key_total = grad_key_total.at[beside_all].add(grad_keys.reshape(3, BLOCK, C))
        grad_value_total = grad_value_total.at[beside_all].add(grad_values.reshape(3, BLOCK, C))
        return ((grad_key_total, grad_value_total), grad_query.reshape(BLOCK, C))
    empty_mesh = jnp.zeros((mesh_blocks, BLOCK, C), jnp.float32)
    (grad_layer_keys, grad_layer_values), grad_layer_queries = lax.scan(layer_back, (empty_mesh, empty_mesh), block_ids)
    grad_y = dot_right(grad_layer_queries.reshape(MESH, C).astype(jnp.bfloat16), layer_query)
    grad_y = grad_y + dot_right(grad_layer_keys.reshape(MESH, C).astype(jnp.bfloat16), layer_key)
    grad_y = grad_y + dot_right(grad_layer_values.reshape(MESH, C).astype(jnp.bfloat16), layer_value)
    grad_enc = cotangent.astype(jnp.float32) + norm_back(grad_y, enc_unit, enc_inverse)
    grad_heads = dot_right(grad_enc.astype(jnp.bfloat16), enc_out_weight).astype(jnp.bfloat16).reshape(mesh_blocks, BLOCK, HEADS, HEAD_DIM)

    def enc_back(running, block_index):
        grad_key_total, grad_value_total = running
        key_rows, value_rows = enc_sources(block_index)
        soft_weights = enc_weights(block_index, key_rows)
        unused_query, grad_keys, grad_values = attend_back(query_blocks[block_index], key_rows, value_rows, soft_weights, grad_heads[block_index], False)
        picked = source[block_index]
        grad_key_total = grad_key_total.at[picked].add(grad_keys.reshape(EDGES, BLOCK, C))
        grad_value_total = grad_value_total.at[picked].add(grad_values.reshape(EDGES, BLOCK, C))
        return ((grad_key_total, grad_value_total), None)
    empty_grid = jnp.zeros((grid_blocks, BLOCK, C), jnp.float32)
    (grad_grid_keys, grad_grid_values), unused_rows = lax.scan(enc_back, (empty_grid, empty_grid), block_ids)
    key_grad = dot_left(grid_norm, grad_grid_keys.reshape(GRID, C).astype(jnp.bfloat16))
    value_grad = dot_left(grid_norm, grad_grid_values.reshape(GRID, C).astype(jnp.bfloat16))
    return (mesh_out, key_grad, value_grad)
```

```python
import jax
import jax.numpy as jnp
from jax import lax
from jax.experimental import pallas as pl
from jax.experimental.pallas import tpu as pltpu
from jax.sharding import PartitionSpec as P

D = 64
B = 128
C = 1024
FULL = 30
REST = 9
epsilon = 1e-05
score_scale = 0.125

f32 = jnp.float32
bf16 = jnp.bfloat16

NN = (((1,), (0,)), ((), ()))
NT = (((1,), (1,)), ((), ()))
TN = (((0,), (0,)), ((), ()))

VMEM = pl.BlockSpec(memory_space=pltpu.VMEM)
SMEM = pl.BlockSpec(memory_space=pltpu.SMEM)


def dot(left, right, dims=NN):
    return lax.dot_general(left, right, dims, preferred_element_type=f32)


def struct(shape, dtype):
    return jax.ShapeDtypeStruct(shape, dtype)


def call(body, outs, specs, scratch=(), mib=40, flops=1 << 26, data=1 << 22, name=None, **extra):
    return pl.pallas_call(
        body,
        out_shape=outs,
        in_specs=specs,
        scratch_shapes=list(scratch),
        compiler_params=pltpu.CompilerParams(vmem_limit_bytes=mib << 20),
        cost_estimate=pl.CostEstimate(flops=flops, bytes_accessed=data, transcendentals=0),
        name=name,
        **extra,
    )


def normalize(values):
    center = values - jnp.mean(values, axis=-1, keepdims=True)
    inverse = lax.rsqrt(jnp.mean(center * center, axis=-1, keepdims=True) + epsilon)
    return center * inverse, inverse


def grid_kernel(send_ref, feat_ref, wk_ref, wv_ref, norm_ref, kv_ref, out_ref):
    step = pl.program_id(0)
    unit, _ = normalize(feat_ref[...].astype(f32))
    rows = unit.astype(bf16)
    norm_ref[...] = rows
    keys = dot(rows, wk_ref[...]).astype(bf16)
    values = dot(rows, wv_ref[...]).astype(bf16)
    both = jnp.concatenate([keys, values], axis=1)
    per = both.shape[0] // B
    for i in range(per):
        kv_ref[step * per + i] = both[i * B : (i + 1) * B]

    @pl.when(step == pl.num_programs(0) - 1)
    def _():
        for i in range(out_ref.shape[0]):
            out_ref[i] = kv_ref[send_ref[i]]


def grid_part(send, feat, wk, wv, shards):
    rows = feat.shape[0]
    steps = 4
    return pl.pallas_call(
        grid_kernel,
        grid=(steps,),
        out_shape=(
            struct((rows, C), bf16),
            struct((rows // B, B, 2 * D), bf16),
            struct((shards, B, 2 * D), bf16),
        ),
        in_specs=[
            SMEM,
            pl.BlockSpec((rows // steps, C), lambda i: (i, 0)),
            pl.BlockSpec((C, D), lambda i: (0, 0)),
            pl.BlockSpec((C, D), lambda i: (0, 0)),
        ],
        out_specs=(
            pl.BlockSpec((rows // steps, C), lambda i: (i, 0)),
            pl.BlockSpec((rows // B, B, 2 * D), lambda i: (0, 0, 0)),
            pl.BlockSpec((shards, B, 2 * D), lambda i: (0, 0, 0)),
        ),
        compiler_params=pltpu.CompilerParams(vmem_limit_bytes=40 << 20),
        cost_estimate=pl.CostEstimate(
            flops=1 << 28, bytes_accessed=6 << 20, transcendentals=0
        ),
        name="grid_part",
    )(send, feat, wk, wv)


def query_kernel(mesh_ref, wq_ref, out_ref):
    for b in range(out_ref.shape[0]):
        unit, _ = normalize(mesh_ref[b * B : (b + 1) * B].astype(f32))
        rows = dot(unit.astype(bf16), wq_ref[...]).astype(bf16).astype(f32) * score_scale
        out_ref[b] = rows.T.astype(bf16)


def fill_pool(pool_ref, own_ref, arrived_ref):
    own = own_ref.shape[0]
    for i in range(own):
        pool_ref[i] = own_ref[i]
    for i in range(arrived_ref.shape[0]):
        pool_ref[own + i] = arrived_ref[i]


def folded(op, values):
    parts = [values[i * 8 : (i + 1) * 8] for i in range(values.shape[0] // 8)]
    while len(parts) > 1:
        parts = [
            op(parts[i], parts[i + 1]) if i + 1 < len(parts) else parts[i]
            for i in range(0, len(parts), 2)
        ]
    return parts[0]


def encoder_kernel(
    slot_ref, count_ref, bias_ref, own_ref, arrived_ref, query_ref,
    wide_ref, out_ref, lse_ref, pool_ref, score_ref,
):
    fill_pool(pool_ref, own_ref, arrived_ref)
    full = jnp.where(count_ref[0] == FULL, 0, 1)
    for m, total in ((full, FULL), (1 - full, REST)):
        stack = jnp.concatenate([query_ref[m], jnp.zeros((D, B), bf16)], axis=0)

        def scores(e, top, m=m, stack=stack):
            value = dot(pool_ref[slot_ref[m, e]], stack) + bias_ref[m, e]
            score_ref[e] = value
            return jnp.maximum(top, folded(jnp.maximum, value))

        top = lax.fori_loop(0, total, scores, jnp.full((8, B), -jnp.inf, f32), unroll=3)
        top = jnp.max(top, axis=0, keepdims=True)

        def mix(e, carry, m=m, top=top):
            low, acc = carry
            raised = jnp.exp(score_ref[e] - top)
            acc = acc + dot(pool_ref[slot_ref[m, e]], raised.astype(bf16), TN)
            return low + folded(jnp.add, raised), acc

        low, acc = lax.fori_loop(
            0, total, mix, (jnp.zeros((8, B), f32), jnp.zeros((2 * D, B), f32)), unroll=3
        )
        low = jnp.sum(low, axis=0, keepdims=True)
        rows = acc[D:] / low
        wide_ref[m] = rows
        out_ref[m] = rows.astype(bf16)
        lse_ref[m] = jnp.broadcast_to(top + jnp.log(low), (8, B))


def middle_kernel(
    heads_ref, gathered_ref, mesh_ref, wq_ref, wk_ref, wv_ref, wl_ref,
    pack_ref, enc_ref, unit_ref, inv_ref,
):
    parts = heads_ref.shape[0]
    w_out = gathered_ref[:, 0:D, :].reshape(parts * D, C)
    half = parts // 2
    queries, grads = [], []
    for b in range(2):
        rows = slice(b * B, (b + 1) * B)
        heads = heads_ref[:, b].reshape(parts * D, B)
        enc = mesh_ref[rows].astype(f32) + dot(heads, w_out, TN)
        enc_ref[rows] = enc
        unit, inverse = normalize(enc)
        unit = unit.astype(bf16)
        unit_ref[rows] = unit
        inv_ref[rows] = jnp.broadcast_to(inverse, (B, 128))
        queries.append((dot(unit, wq_ref[...]).astype(bf16).astype(f32) * score_scale).astype(bf16))
        keys = dot(unit, wk_ref[...]).astype(bf16)
        values = dot(unit, wv_ref[...]).astype(bf16)
        pack_ref[rows] = jnp.concatenate([keys, values], axis=1)
        cot = gathered_ref[half * b : half * (b + 1), D:, :].reshape(B, C)
        grads.append(dot(cot, wl_ref[...], NT).astype(bf16))
    pack_ref[2 * B : 3 * B] = jnp.concatenate(queries, axis=1)
    pack_ref[3 * B : 4 * B] = jnp.concatenate(grads, axis=1)


def side_kernel(gathered_ref, unit_ref, inv_ref, wo_ref, cot_ref, unit_out_ref, inv_out_ref, sum_ref):
    half = gathered_ref.shape[0] // 2
    weight = wo_ref[...]
    for b in range(2):
        rows = slice(b * B, (b + 1) * B)
        cot = gathered_ref[half * b : half * (b + 1), D:, :].reshape(B, C)
        cot_ref[b] = dot(weight, cot, NT)
        unit_out_ref[b] = dot(weight, unit_ref[rows], NT)
        inv_out_ref[b] = inv_ref[rows].T[0:8]
    sum_ref[...] = jnp.broadcast_to(
        jnp.sum(weight.astype(f32), axis=1, keepdims=True), sum_ref.shape
    )


def layer_kernel(
    bias_ref, left_bias_ref, right_bias_ref, own_ref, left_ref, right_ref, unit_ref,
    wq_ref, wk_ref, wv_ref, gathered_ref, send_ref, heads_ref,
):
    zero = jnp.zeros((B, D), bf16)

    def block(ref, b):
        return ref[b * B : (b + 1) * B]

    def stacked(ref, b):
        lanes = slice(b * D, (b + 1) * D)
        query = ref[2 * B : 3 * B][:, lanes]
        grad = ref[3 * B : 4 * B][:, lanes]
        return jnp.concatenate(
            [jnp.concatenate([query, zero], axis=1), jnp.concatenate([zero, grad], axis=1)], axis=0
        )

    kv = [block(ref, b) for ref in (left_ref, own_ref, right_ref) for b in range(2)]
    queries = [(left_ref, 1, left_bias_ref), (own_ref, 0, bias_ref), (own_ref, 1, bias_ref)]
    queries.append((right_ref, 0, right_bias_ref))
    grad_kv = [jnp.zeros((B, 2 * D), f32), jnp.zeros((B, 2 * D), f32)]
    grad_q = []
    for j, (ref, b, table) in enumerate(queries):
        pair = stacked(ref, b)
        window = kv[j : j + 3]
        both = [dot(rows, pair, NT) for rows in window]
        scores = [both[n][:, :B] + table[b, n] for n in range(3)]
        top = folded(jnp.maximum, jnp.concatenate(scores, axis=0))
        top = jnp.max(top, axis=0, keepdims=True)
        raised = [jnp.exp(s - top) for s in scores]
        low = sum(folded(jnp.add, r) for r in raised)
        scale = 1.0 / jnp.sum(low, axis=0, keepdims=True)
        soft = [r * scale for r in raised]
        inner = sum(folded(jnp.add, soft[n] * both[n][:, B:]) for n in range(3))
        inner = jnp.sum(inner, axis=0, keepdims=True)
        mixed = [
            jnp.concatenate(
                [(soft[n] * (both[n][:, B:] - inner)).astype(bf16), soft[n].astype(bf16)], axis=1
            )
            for n in range(3)
        ]
        for n in range(3):
            own = j + n - 2
            if 0 <= own < 2:
                grad_kv[own] = grad_kv[own] + dot(mixed[n], pair)
        if 1 <= j <= 2:
            back = sum(dot(mixed[n], window[n], TN) for n in range(3))
            grad_q.append((back[:B, :D] * score_scale).astype(bf16))
            heads_ref[b * B : (b + 1) * B] = back[B:, D:].astype(bf16)
    parts = gathered_ref.shape[0]
    totals, stats = [], []
    lane = lax.broadcasted_iota(jnp.int32, (B, 128), 1)
    for b in range(2):
        grad = grad_kv[b].astype(bf16)
        total = (
            dot(grad_q[b], wq_ref[...], NT)
            + dot(grad[:, :D], wk_ref[...], NT)
            + dot(grad[:, D:], wv_ref[...], NT)
        )
        first = jnp.mean(total, axis=1, keepdims=True)
        second = jnp.mean(total * unit_ref[b * B : (b + 1) * B].astype(f32), axis=1, keepdims=True)
        table = jnp.where(lane == 0, first, jnp.where(lane == 1, second, 0.0)).T[0:8]
        high = table.astype(bf16).astype(f32)
        stats.append(jnp.concatenate([high, table - high], axis=0).astype(bf16))
        totals.append(total.astype(bf16))
    total = jnp.concatenate(totals, axis=0)
    for z in range(parts):
        piece = dot(gathered_ref[z, 0:D, :], total, NT).astype(bf16)
        for b in range(2):
            send_ref[z, b, 0:D] = piece[:, b * B : (b + 1) * B]
            send_ref[z, b, D : D + 16] = stats[b]


def back_kernel(
    slot_ref, count_ref, bias_ref, me_ref, arrived_grad_ref, cot_ref, unit_ref, inv_ref, sum_ref,
    wide_ref, lse_ref, query_ref, own_ref, arrived_ref,
    own_out_ref, send_ref, pool_ref, grad_ref, pair_ref, inner_ref,
):
    fill_pool(pool_ref, own_ref, arrived_ref)
    zero = jnp.zeros((D, B), bf16)
    for b in range(2):
        total = arrived_grad_ref[0, b].astype(f32)
        for z in range(1, arrived_grad_ref.shape[0]):
            total = total + arrived_grad_ref[z, b].astype(f32)
        stats = total[D : D + 8] + total[D + 8 : D + 16]
        inside = total[:D] - stats[0:1] * sum_ref[...] - stats[1:2] * unit_ref[b]
        grad = (cot_ref[b] + inv_ref[b][0:1] * inside).astype(bf16)
        inner = jnp.sum(grad.astype(f32) * wide_ref[b], axis=0, keepdims=True)
        inner_ref[b] = jnp.broadcast_to(inner, (8, B))
        pair_ref[b] = jnp.concatenate(
            [
                jnp.concatenate([query_ref[b], zero], axis=1),
                jnp.concatenate([zero, grad], axis=1),
            ],
            axis=0,
        )
    own = own_ref.shape[0]
    grad_ref[own + me_ref[0]] = jnp.zeros((B, 2 * D), f32)
    full = jnp.where(count_ref[0] == FULL, 0, 1)
    for m, total in ((full, FULL), (1 - full, REST)):
        pair = pair_ref[m]
        lse = lse_ref[m][0:1]
        inner = inner_ref[m][0:1]

        def step(e, carry, m=m, pair=pair, lse=lse, inner=inner):
            slot = slot_ref[m, e]
            both = dot(pool_ref[slot], pair)
            soft = jnp.exp(both[:, :B] + (bias_ref[m, e] - lse))
            mixed = jnp.concatenate(
                [(soft * (both[:, B:] - inner)).astype(bf16), soft.astype(bf16)], axis=1
            )
            grad_ref[slot] = dot(mixed, pair, NT)
            return carry

        lax.fori_loop(0, total, step, 0, unroll=3)
    for i in range(own):
        own_out_ref[i] = grad_ref[i]
    for i in range(send_ref.shape[0]):
        send_ref[i] = grad_ref[own + i].astype(bf16)


def final_kernel(send_ref, norm_ref, own_ref, back_ref, out_ref, acc_ref):
    for i in range(own_ref.shape[0]):
        acc_ref[i] = own_ref[i]

    def add(i, carry):
        slot = send_ref[i]
        acc_ref[slot] = acc_ref[slot] + back_ref[i].astype(f32)
        return carry

    lax.fori_loop(0, back_ref.shape[0], add, 0, unroll=2)
    rows = acc_ref[...].reshape(norm_ref.shape[0], 2 * D).astype(bf16)
    shards, height = out_ref.shape[0], out_ref.shape[1]
    tile = 256
    for c in range(C // tile):
        part = dot(rows, norm_ref[:, c * tile : (c + 1) * tile], TN).T
        per = tile // height
        out_ref[c * per : (c + 1) * per] = part.astype(bf16).reshape(per, height, 2 * D)


def output_kernel(at_ref, heads_ref, weight_ref, enc_ref, out_ref):
    height = out_ref.shape[0]
    total = enc_ref[pl.ds(pl.multiple_of(at_ref[0] * height, height), height), :]
    for h in range(heads_ref.shape[0]):
        total = total + dot(heads_ref[h], weight_ref[h * D : (h + 1) * D])
    out_ref[...] = total.astype(bf16)


def sum_kernel(parts_ref, key_ref, value_ref):
    total = parts_ref[0].astype(f32)
    for i in range(1, parts_ref.shape[0]):
        total = total + parts_ref[i].astype(f32)
    key_ref[...] = total[:, :D]
    value_ref[...] = total[:, D:]


def exchange(array, axis):
    return lax.all_to_all(array, axis, split_axis=0, concat_axis=0, tiled=True)


def on_device(
    grid_feat,
    mesh_feat,
    query_weight,
    key_weight,
    value_weight,
    enc_out_weight,
    layer_query,
    layer_key,
    layer_value,
    layer_out_weight,
    enc_bias,
    layer_bias,
    send_list,
    edge_slot,
    edge_count,
    cotangent,
):
    shards = lax.axis_size("grid")
    parts = lax.axis_size("head")
    own = grid_feat.shape[0] // B
    share = cotangent.shape[0]
    send = send_list[0]
    enc_table = enc_bias[:, :, 0]
    layer_table = layer_bias[:, :, 0]
    shard_at = lax.axis_index("grid").astype(jnp.int32)[None]
    head_at = lax.axis_index("head").astype(jnp.int32)[None]
    forward = [(i, (i + 1) % shards) for i in range(shards)]
    backward = [(t, s) for s, t in forward]

    gathered = lax.all_gather(
        jnp.concatenate([enc_out_weight, cotangent], axis=0), "head", axis=0, tiled=False
    )
    layer_out_all = lax.all_gather(layer_out_weight, "head", axis=0, tiled=True)

    grid_norm, own_kv, outgoing = grid_part(send, grid_feat, key_weight, value_weight, shards)
    arrived_kv = exchange(outgoing, "grid")
    left_bias = lax.ppermute(layer_table, "grid", forward)
    right_bias = lax.ppermute(layer_table, "grid", backward)
    queries = call(
        query_kernel, struct((2, D, B), bf16), [VMEM] * 2, name="query_part", data=1 << 20
    )(mesh_feat, query_weight)
    wide_heads, enc_heads, lse = call(
        encoder_kernel,
        (struct((2, D, B), f32), struct((2, D, B), bf16), struct((2, 8, B), f32)),
        [SMEM] * 3 + [VMEM] * 3,
        [pltpu.VMEM((own + shards, B, 2 * D), bf16), pltpu.VMEM((FULL, B, B), f32)],
        name="encoder_part",
    )(edge_slot, edge_count, enc_table, own_kv, arrived_kv, queries)
    all_heads = lax.all_gather(enc_heads, "head", axis=0, tiled=False)
    pack, encoded, unit, inverse = call(
        middle_kernel,
        (
            struct((4 * B, 2 * D), bf16),
            struct((2 * B, C), f32),
            struct((2 * B, C), bf16),
            struct((2 * B, 128), f32),
        ),
        [VMEM] * 7,
        name="middle_part",
    )(
        all_heads, gathered, mesh_feat, layer_query, layer_key, layer_value, layer_out_weight
    )
    left = lax.ppermute(pack, "grid", forward)
    right = lax.ppermute(pack, "grid", backward)
    cot_part, unit_part, inverse_row, weight_sum = call(
        side_kernel,
        (
            struct((2, D, B), f32),
            struct((2, D, B), f32),
            struct((2, 8, B), f32),
            struct((D, B), f32),
        ),
        [VMEM] * 4,
        name="side_part",
    )(gathered, unit, inverse, enc_out_weight)
    mixed, layer_heads = call(
        layer_kernel,
        (struct((parts, 2, D + 16, B), bf16), struct((2 * B, D), bf16)),
        [SMEM] * 3 + [VMEM] * 8,
        name="layer_part",
    )(
        layer_table, left_bias, right_bias, pack, left, right, unit,
        layer_query, layer_key, layer_value, gathered,
    )
    arrived_grad = exchange(mixed, "head")
    own_grad, send_grad = call(
        back_kernel,
        (struct((own, B, 2 * D), f32), struct((shards, B, 2 * D), bf16)),
        [SMEM] * 4 + [VMEM] * 10,
        [
            pltpu.VMEM((own + shards, B, 2 * D), bf16),
            pltpu.VMEM((own + shards, B, 2 * D), f32),
            pltpu.VMEM((2, 2 * D, 2 * B), bf16),
            pltpu.VMEM((2, 8, B), f32),
        ],
        name="back_part",
    )(
        edge_slot, edge_count, enc_table, shard_at, arrived_grad, cot_part, unit_part,
        inverse_row, weight_sum, wide_heads, lse, queries, own_kv, arrived_kv,
    )
    back_grad = exchange(send_grad, "grid")
    row_heads = exchange(layer_heads.reshape(parts, share, D), "head")
    product = call(
        final_kernel,
        struct((shards, C // shards, 2 * D), bf16),
        [SMEM] + [VMEM] * 3,
        [pltpu.VMEM((own, B, 2 * D), f32)],
        name="final_part",
    )(send, grid_norm, own_grad, back_grad)
    pieces = exchange(product, "grid")
    mesh_out = call(
        output_kernel,
        struct((share, C), bf16),
        [SMEM] + [VMEM] * 3,
        name="output_part",
    )(head_at, row_heads, layer_out_all, encoded)
    key_grad, value_grad = call(
        sum_kernel,
        (struct((C // shards, D), f32), struct((C // shards, D), f32)),
        [VMEM],
        name="sum_part",
    )(pieces)
    return mesh_out, key_grad, value_grad


def solution(mesh):
    in_specs = (
        P("grid", None),
        P("grid", None),
        P(None, "head"),
        P(None, "head"),
        P(None, "head"),
        P("head", None),
        P(None, "head"),
        P(None, "head"),
        P(None, "head"),
        P("head", None),
        P("grid", None, "head"),
        P("grid", None, "head"),
        P("grid", None),
        P("grid", None),
        P("grid"),
        P(("grid", "head"), None),
    )
    out_specs = (P(("grid", "head"), None), P("grid", "head"), P("grid", "head"))
    return jax.shard_map(
        on_device, mesh=mesh, in_specs=in_specs, out_specs=out_specs, check_vma=False
    )
```

```python
import jax
import jax.numpy as jnp
from jax import lax
from jax.experimental import pallas as pl
from jax.experimental.pallas import tpu as pltpu
from jax.sharding import PartitionSpec as P

D = 64
B = 128
C = 1024
FULL = 30
REST = 9
epsilon = 1e-05
score_scale = 0.125

f32 = jnp.float32
bf16 = jnp.bfloat16

NN = (((1,), (0,)), ((), ()))
NT = (((1,), (1,)), ((), ()))
TN = (((0,), (0,)), ((), ()))

VMEM = pl.BlockSpec(memory_space=pltpu.VMEM)
SMEM = pl.BlockSpec(memory_space=pltpu.SMEM)


def dot(left, right, dims=NN):
    return lax.dot_general(left, right, dims, preferred_element_type=f32)


def struct(shape, dtype):
    return jax.ShapeDtypeStruct(shape, dtype)


def call(body, outs, specs, scratch=(), mib=60, flops=1 << 26, data=1 << 22, name=None, **extra):
    return pl.pallas_call(
        body,
        out_shape=outs,
        in_specs=specs,
        scratch_shapes=list(scratch),
        compiler_params=pltpu.CompilerParams(vmem_limit_bytes=mib << 20),
        cost_estimate=pl.CostEstimate(flops=flops, bytes_accessed=data, transcendentals=0),
        name=name,
        **extra,
    )


def normalize(values):
    center = values - jnp.mean(values, axis=-1, keepdims=True)
    inverse = lax.rsqrt(jnp.mean(center * center, axis=-1, keepdims=True) + epsilon)
    return center * inverse, inverse


def grid_kernel(send_ref, feat_ref, wk_ref, wv_ref, norm_ref, kv_ref, out_ref):
    step = pl.program_id(0)
    unit, _ = normalize(feat_ref[...].astype(f32))
    rows = unit.astype(bf16)
    norm_ref[...] = rows
    weight = jnp.concatenate([wk_ref[...], wv_ref[...]], axis=0)
    both = dot(rows, weight, NT).astype(bf16)
    per = both.shape[0] // B
    for i in range(per):
        kv_ref[step * per + i] = both[i * B : (i + 1) * B]

    @pl.when(step == pl.num_programs(0) - 1)
    def _():
        for i in range(out_ref.shape[0]):
            out_ref[i] = kv_ref[send_ref[i]]


def grid_part(send, feat, wk, wv, shards):
    rows = feat.shape[0]
    steps = 4
    return pl.pallas_call(
        grid_kernel,
        grid=(steps,),
        out_shape=(
            struct((rows, C), bf16),
            struct((rows // B, B, 2 * D), bf16),
            struct((shards, B, 2 * D), bf16),
        ),
        in_specs=[
            SMEM,
            pl.BlockSpec((rows // steps, C), lambda i: (i, 0)),
            pl.BlockSpec((D, C), lambda i: (0, 0)),
            pl.BlockSpec((D, C), lambda i: (0, 0)),
        ],
        out_specs=(
            pl.BlockSpec((rows // steps, C), lambda i: (i, 0)),
            pl.BlockSpec((rows // B, B, 2 * D), lambda i: (0, 0, 0)),
            pl.BlockSpec((shards, B, 2 * D), lambda i: (0, 0, 0)),
        ),
        compiler_params=pltpu.CompilerParams(vmem_limit_bytes=60 << 20),
        cost_estimate=pl.CostEstimate(
            flops=1 << 28, bytes_accessed=6 << 20, transcendentals=0
        ),
        name="grid_part",
    )(send, feat, wk, wv)


def query_kernel(mesh_ref, wq_ref, out_ref):
    for b in range(out_ref.shape[0]):
        unit, _ = normalize(mesh_ref[b * B : (b + 1) * B].astype(f32))
        rows = dot(wq_ref[...], unit.astype(bf16), NT).astype(bf16).astype(f32) * score_scale
        out_ref[b] = rows.astype(bf16)


def fill_pool(pool_ref, own_ref, arrived_ref):
    own = own_ref.shape[0]
    for i in range(own):
        pool_ref[i] = own_ref[i]
    for i in range(arrived_ref.shape[0]):
        pool_ref[own + i] = arrived_ref[i]


def folded(op, values):
    parts = [values[i * 8 : (i + 1) * 8] for i in range(values.shape[0] // 8)]
    while len(parts) > 1:
        parts = [
            op(parts[i], parts[i + 1]) if i + 1 < len(parts) else parts[i]
            for i in range(0, len(parts), 2)
        ]
    return parts[0]


def encoder_kernel(
    slot_ref, count_ref, bias_ref, own_ref, arrived_ref, query_ref,
    wide_ref, out_ref, lse_ref, pool_ref, score_ref,
):
    fill_pool(pool_ref, own_ref, arrived_ref)
    full = jnp.where(count_ref[0] == FULL, 0, 1)
    for m, total in ((full, FULL), (1 - full, REST)):
        stack = jnp.concatenate([query_ref[m], jnp.zeros((D, B), bf16)], axis=0)

        def scores(e, top, m=m, stack=stack):
            value = dot(pool_ref[slot_ref[m, e]], stack) + bias_ref[m, e]
            score_ref[e] = value
            return jnp.maximum(top, folded(jnp.maximum, value))

        top = lax.fori_loop(0, total, scores, jnp.full((8, B), -jnp.inf, f32), unroll=3)
        top = jnp.max(top, axis=0, keepdims=True)

        def mix(e, carry, m=m, top=top):
            low, acc = carry
            raised = jnp.exp(score_ref[e] - top)
            acc = acc + dot(pool_ref[slot_ref[m, e]], raised.astype(bf16), TN)
            return low + folded(jnp.add, raised), acc

        low, acc = lax.fori_loop(
            0, total, mix, (jnp.zeros((8, B), f32), jnp.zeros((2 * D, B), f32)), unroll=3
        )
        low = jnp.sum(low, axis=0, keepdims=True)
        rows = acc[D:] / low
        wide_ref[m] = rows
        out_ref[m] = rows.astype(bf16)
        lse_ref[m] = jnp.broadcast_to(top + jnp.log(low), (8, B))


def middle_kernel(
    bias_ref, heads_ref, gathered_ref, mesh_ref, wq_ref, wk_ref, wv_ref, wl_ref,
    pack_ref, enc_ref, unit_ref, inv_ref,
):
    parts = heads_ref.shape[0]
    w_out = gathered_ref[:, 0:D, :].reshape(parts * D, C)
    w_layer = jnp.concatenate([wk_ref[...], wv_ref[...], wq_ref[...]], axis=0)
    half = parts // 2
    queries, grads = [], []
    for b in range(2):
        rows = slice(b * B, (b + 1) * B)
        heads = heads_ref[:, b].reshape(parts * D, B)
        enc = mesh_ref[rows].astype(f32) + dot(heads, w_out, TN)
        enc_ref[rows] = enc
        unit, inverse = normalize(enc)
        unit = unit.astype(bf16)
        unit_ref[rows] = unit
        inv_ref[rows] = jnp.broadcast_to(inverse, (B, 128))
        both = dot(unit, w_layer, NT).astype(bf16)
        pack_ref[rows] = both[:, : 2 * D]
        queries.append((both[:, 2 * D :].astype(f32) * score_scale).astype(bf16))
        cot = gathered_ref[half * b : half * (b + 1), 2 * D :, :].reshape(B, C)
        grads.append(dot(cot, wl_ref[...], NT).astype(bf16))
    pack_ref[2 * B : 3 * B] = jnp.concatenate(queries, axis=1)
    pack_ref[3 * B : 4 * B] = jnp.concatenate(grads, axis=1)
    row = lax.broadcasted_iota(jnp.int32, (8, 128), 0)
    table = jnp.zeros((8, 128), f32)
    for b in range(2):
        for n in range(3):
            table = jnp.where(row == 3 * b + n, bias_ref[b, n], table)
    high = table.astype(bf16).astype(f32)
    rest = table - high
    middle = rest.astype(bf16).astype(f32)
    tail = [high, middle, rest - middle, jnp.zeros((8, 128), f32)]
    pack_ref[4 * B : 4 * B + 32] = jnp.concatenate(tail, axis=0).astype(bf16)


def side_kernel(gathered_ref, unit_ref, inv_ref, wo_ref, cot_ref, unit_out_ref, inv_out_ref, sum_ref):
    half = gathered_ref.shape[0] // 2
    weight = wo_ref[...]
    for b in range(2):
        rows = slice(b * B, (b + 1) * B)
        cot = gathered_ref[half * b : half * (b + 1), 2 * D :, :].reshape(B, C)
        cot_ref[b] = dot(weight, cot, NT)
        unit_out_ref[b] = dot(weight, unit_ref[rows], NT)
        inv_out_ref[b] = inv_ref[rows].T[0:8]
    sum_ref[...] = jnp.broadcast_to(
        jnp.sum(weight.astype(f32), axis=1, keepdims=True), sum_ref.shape
    )


def layer_kernel(
    own_ref, left_ref, right_ref, unit_ref, wq_ref, wk_ref, wv_ref, gathered_ref, send_ref
):
    zero = jnp.zeros((B, D), bf16)

    def block(ref, b):
        return ref[b * B : (b + 1) * B]

    def stacked(ref, b):
        lanes = slice(b * D, (b + 1) * D)
        query = ref[2 * B : 3 * B][:, lanes]
        grad = ref[3 * B : 4 * B][:, lanes]
        return jnp.concatenate(
            [jnp.concatenate([query, zero], axis=1), jnp.concatenate([zero, grad], axis=1)], axis=0
        )

    def table(ref):
        tail = ref[4 * B : 4 * B + 32].astype(f32)
        return tail[0:8] + tail[8:16] + tail[16:24]

    kv = [block(ref, b) for ref in (left_ref, own_ref, right_ref) for b in range(2)]
    own_bias = table(own_ref)
    queries = [(left_ref, 1, table(left_ref)), (own_ref, 0, own_bias), (own_ref, 1, own_bias)]
    queries.append((right_ref, 0, table(right_ref)))
    heads = []
    grad_kv = [jnp.zeros((B, 2 * D), f32), jnp.zeros((B, 2 * D), f32)]
    grad_q = []
    for j, (ref, b, bias) in enumerate(queries):
        pair = stacked(ref, b)
        window = kv[j : j + 3]
        both = [dot(rows, pair, NT) for rows in window]
        scores = [both[n][:, :B] + bias[3 * b + n : 3 * b + n + 1] for n in range(3)]
        top = folded(jnp.maximum, jnp.concatenate(scores, axis=0))
        top = jnp.max(top, axis=0, keepdims=True)
        raised = [jnp.exp(s - top) for s in scores]
        low = sum(folded(jnp.add, r) for r in raised)
        scale = 1.0 / jnp.sum(low, axis=0, keepdims=True)
        soft = [r * scale for r in raised]
        inner = sum(folded(jnp.add, soft[n] * both[n][:, B:]) for n in range(3))
        inner = jnp.sum(inner, axis=0, keepdims=True)
        mixed = [
            jnp.concatenate(
                [(soft[n] * (both[n][:, B:] - inner)).astype(bf16), soft[n].astype(bf16)], axis=1
            )
            for n in range(3)
        ]
        for n in range(3):
            own = j + n - 2
            if 0 <= own < 2:
                grad_kv[own] = grad_kv[own] + dot(mixed[n], pair)
        if 1 <= j <= 2:
            back = sum(dot(mixed[n], window[n], TN) for n in range(3))
            grad_q.append((back[:B, :D] * score_scale).astype(bf16))
            heads.append(back[B:, D:].astype(bf16))
    parts = gathered_ref.shape[0]
    w_layer = jnp.concatenate([wk_ref[...], wv_ref[...], wq_ref[...]], axis=0)
    totals, stats = [], jnp.zeros((8, 128), f32)
    lane = lax.broadcasted_iota(jnp.int32, (B, 128), 1)
    for b in range(2):
        grad = jnp.concatenate([grad_kv[b].astype(bf16), grad_q[b]], axis=1)
        total = dot(grad, w_layer)
        first = jnp.mean(total, axis=1, keepdims=True)
        second = jnp.mean(total * unit_ref[b * B : (b + 1) * B].astype(f32), axis=1, keepdims=True)
        first_high = first.astype(bf16).astype(f32)
        second_high = second.astype(bf16).astype(f32)
        columns = (first_high, second_high, first - first_high, second - second_high)
        table_b = jnp.zeros((B, 128), f32)
        for k, column in enumerate(columns):
            table_b = jnp.where(lane == 4 * b + k, column, table_b)
        stats = stats + table_b.T[0:8]
        totals.append(total.astype(bf16))
    stats = jnp.concatenate([stats[:, :D], stats[:, D:]], axis=0).astype(bf16)
    total = jnp.concatenate(totals, axis=0)
    heads = jnp.concatenate(heads, axis=0)
    share = heads.shape[0] // parts
    for z in range(parts):
        piece = dot(gathered_ref[z, 0:D, :], total, NT).astype(bf16)
        for b in range(2):
            send_ref[z, b * D : (b + 1) * D] = piece[:, b * B : (b + 1) * B]
        rows = heads[z * share : (z + 1) * share]
        send_ref[z, 2 * D :] = jnp.concatenate([rows, stats], axis=1)


def back_kernel(
    slot_ref, count_ref, bias_ref, me_ref, arrived_grad_ref, cot_ref, unit_ref, inv_ref, sum_ref,
    wide_ref, lse_ref, query_ref, own_ref, arrived_ref,
    own_out_ref, send_ref, pool_ref, grad_ref, pair_ref, inner_ref,
):
    fill_pool(pool_ref, own_ref, arrived_ref)
    zero = jnp.zeros((D, B), bf16)
    total = arrived_grad_ref[0].astype(f32)
    for z in range(1, arrived_grad_ref.shape[0]):
        total = total + arrived_grad_ref[z].astype(f32)
    stats = total[2 * D :, D:]
    stats = jnp.concatenate([stats[0:8], stats[8:16]], axis=1)
    for b in range(2):
        first = stats[4 * b : 4 * b + 1] + stats[4 * b + 2 : 4 * b + 3]
        second = stats[4 * b + 1 : 4 * b + 2] + stats[4 * b + 3 : 4 * b + 4]
        inside = total[b * D : (b + 1) * D] - first * sum_ref[...] - second * unit_ref[b]
        grad = (cot_ref[b] + inv_ref[b][0:1] * inside).astype(bf16)
        inner = jnp.sum(grad.astype(f32) * wide_ref[b], axis=0, keepdims=True)
        inner_ref[b] = jnp.broadcast_to(inner, (8, B))
        pair_ref[b] = jnp.concatenate(
            [
                jnp.concatenate([query_ref[b], zero], axis=1),
                jnp.concatenate([zero, grad], axis=1),
            ],
            axis=0,
        )
    own = own_ref.shape[0]
    grad_ref[own + me_ref[0]] = jnp.zeros((B, 2 * D), f32)
    full = jnp.where(count_ref[0] == FULL, 0, 1)
    for m, total in ((full, FULL), (1 - full, REST)):
        pair = pair_ref[m]
        lse = lse_ref[m][0:1]
        inner = inner_ref[m][0:1]

        def step(e, carry, m=m, pair=pair, lse=lse, inner=inner):
            slot = slot_ref[m, e]
            both = dot(pool_ref[slot], pair)
            soft = jnp.exp(both[:, :B] + (bias_ref[m, e] - lse))
            mixed = jnp.concatenate(
                [(soft * (both[:, B:] - inner)).astype(bf16), soft.astype(bf16)], axis=1
            )
            grad_ref[slot] = dot(mixed, pair, NT)
            return carry

        lax.fori_loop(0, total, step, 0, unroll=3)
    for i in range(own):
        own_out_ref[i] = grad_ref[i]
    for i in range(send_ref.shape[0]):
        send_ref[i] = grad_ref[own + i].astype(bf16)


def final_kernel(send_ref, norm_ref, own_ref, back_ref, out_ref, acc_ref):
    for i in range(own_ref.shape[0]):
        acc_ref[i] = own_ref[i]

    def add(i, carry):
        slot = send_ref[i]
        acc_ref[slot] = acc_ref[slot] + back_ref[i].astype(f32)
        return carry

    lax.fori_loop(0, back_ref.shape[0], add, 0, unroll=2)
    rows = acc_ref[...].reshape(norm_ref.shape[0], 2 * D).astype(bf16)
    shards, height = out_ref.shape[0], out_ref.shape[1]
    tile = 256
    for c in range(C // tile):
        part = dot(rows, norm_ref[:, c * tile : (c + 1) * tile], TN).T
        per = tile // height
        out_ref[c * per : (c + 1) * per] = part.astype(bf16).reshape(per, height, 2 * D)


def output_kernel(at_ref, heads_ref, weight_ref, enc_ref, out_ref):
    height = out_ref.shape[0]
    total = enc_ref[pl.ds(pl.multiple_of(at_ref[0] * height, height), height), :]
    for h in range(heads_ref.shape[0]):
        total = total + dot(heads_ref[h, 2 * D :][:, :D], weight_ref[h, D : 2 * D])
    out_ref[...] = total.astype(bf16)


def sum_kernel(parts_ref, key_ref, value_ref):
    total = parts_ref[0].astype(f32)
    for i in range(1, parts_ref.shape[0]):
        total = total + parts_ref[i].astype(f32)
    key_ref[...] = total[:, :D]
    value_ref[...] = total[:, D:]


def exchange(array, axis):
    return lax.all_to_all(array, axis, split_axis=0, concat_axis=0, tiled=True)


def on_device(
    grid_feat,
    mesh_feat,
    query_weight,
    key_weight,
    value_weight,
    enc_out_weight,
    layer_query,
    layer_key,
    layer_value,
    layer_out_weight,
    enc_bias,
    layer_bias,
    send_list,
    edge_slot,
    edge_count,
    cotangent,
):
    shards = lax.axis_size("grid")
    parts = lax.axis_size("head")
    own = grid_feat.shape[0] // B
    share = cotangent.shape[0]
    send = send_list[0]
    enc_table = enc_bias[:, :, 0]
    layer_table = layer_bias[:, :, 0]
    shard_at = lax.axis_index("grid").astype(jnp.int32)[None]
    head_at = lax.axis_index("head").astype(jnp.int32)[None]
    forward = [(i, (i + 1) % shards) for i in range(shards)]
    backward = [(t, s) for s, t in forward]

    gathered = lax.all_gather(
        jnp.concatenate([enc_out_weight, layer_out_weight, cotangent], axis=0),
        "head",
        axis=0,
        tiled=False,
    )
    query_weight, key_weight, value_weight, layer_query, layer_key, layer_value = (
        weight.T
        for weight in (query_weight, key_weight, value_weight, layer_query, layer_key, layer_value)
    )

    grid_norm, own_kv, outgoing = grid_part(send, grid_feat, key_weight, value_weight, shards)
    arrived_kv = exchange(outgoing, "grid")
    queries = call(
        query_kernel, struct((2, D, B), bf16), [VMEM] * 2, name="query_part", data=1 << 20
    )(mesh_feat, query_weight)
    wide_heads, enc_heads, lse = call(
        encoder_kernel,
        (struct((2, D, B), f32), struct((2, D, B), bf16), struct((2, 8, B), f32)),
        [SMEM] * 3 + [VMEM] * 3,
        [pltpu.VMEM((own + shards, B, 2 * D), bf16), pltpu.VMEM((FULL, B, B), f32)],
        name="encoder_part",
    )(edge_slot, edge_count, enc_table, own_kv, arrived_kv, queries)
    all_heads = lax.all_gather(enc_heads, "head", axis=0, tiled=False)
    pack, encoded, unit, inverse = call(
        middle_kernel,
        (
            struct((4 * B + 32, 2 * D), bf16),
            struct((2 * B, C), f32),
            struct((2 * B, C), bf16),
            struct((2 * B, 128), f32),
        ),
        [SMEM] + [VMEM] * 7,
        name="middle_part",
    )(
        layer_table, all_heads, gathered, mesh_feat, layer_query, layer_key, layer_value, layer_out_weight
    )
    left = lax.ppermute(pack, "grid", forward)
    right = lax.ppermute(pack, "grid", backward)
    cot_part, unit_part, inverse_row, weight_sum = call(
        side_kernel,
        (
            struct((2, D, B), f32),
            struct((2, D, B), f32),
            struct((2, 8, B), f32),
            struct((D, B), f32),
        ),
        [VMEM] * 4,
        name="side_part",
    )(gathered, unit, inverse, enc_out_weight)
    mixed = call(
        layer_kernel, struct((parts, 2 * D + share, B), bf16), [VMEM] * 8, name="layer_part"
    )(pack, left, right, unit, layer_query, layer_key, layer_value, gathered)
    arrived_grad = exchange(mixed, "head")
    own_grad, send_grad = call(
        back_kernel,
        (struct((own, B, 2 * D), f32), struct((shards, B, 2 * D), bf16)),
        [SMEM] * 4 + [VMEM] * 10,
        [
            pltpu.VMEM((own + shards, B, 2 * D), bf16),
            pltpu.VMEM((own + shards, B, 2 * D), f32),
            pltpu.VMEM((2, 2 * D, 2 * B), bf16),
            pltpu.VMEM((2, 8, B), f32),
        ],
        name="back_part",
    )(
        edge_slot, edge_count, enc_table, shard_at, arrived_grad, cot_part, unit_part,
        inverse_row, weight_sum, wide_heads, lse, queries, own_kv, arrived_kv,
    )
    back_grad = exchange(send_grad, "grid")
    product = call(
        final_kernel,
        struct((shards, C // shards, 2 * D), bf16),
        [SMEM] + [VMEM] * 3,
        [pltpu.VMEM((own, B, 2 * D), f32)],
        name="final_part",
    )(send, grid_norm, own_grad, back_grad)
    pieces = exchange(product, "grid")
    mesh_out = call(
        output_kernel,
        struct((share, C), bf16),
        [SMEM] + [VMEM] * 3,
        name="output_part",
    )(head_at, arrived_grad, gathered, encoded)
    key_grad, value_grad = call(
        sum_kernel,
        (struct((C // shards, D), f32), struct((C // shards, D), f32)),
        [VMEM],
        name="sum_part",
    )(pieces)
    return mesh_out, key_grad, value_grad


def solution(mesh):
    in_specs = (
        P("grid", None),
        P("grid", None),
        P(None, "head"),
        P(None, "head"),
        P(None, "head"),
        P("head", None),
        P(None, "head"),
        P(None, "head"),
        P(None, "head"),
        P("head", None),
        P("grid", None, "head"),
        P("grid", None, "head"),
        P("grid", None),
        P("grid", None),
        P("grid"),
        P(("grid", "head"), None),
    )
    out_specs = (P(("grid", "head"), None), P("grid", "head"), P("grid", "head"))
    return jax.shard_map(
        on_device, mesh=mesh, in_specs=in_specs, out_specs=out_specs, check_vma=False
    )
```

```python
import jax
import jax.numpy as jnp
from jax import lax
from jax.experimental import pallas as pl
from jax.experimental.pallas import tpu as pltpu
from jax.sharding import PartitionSpec as P

D = 64
B = 128
C = 1024
FULL = 30
REST = 9
epsilon = 1e-05
score_scale = 0.125

f32 = jnp.float32
bf16 = jnp.bfloat16

NN = (((1,), (0,)), ((), ()))
NT = (((1,), (1,)), ((), ()))
TN = (((0,), (0,)), ((), ()))

VMEM = pl.BlockSpec(memory_space=pltpu.VMEM)
SMEM = pl.BlockSpec(memory_space=pltpu.SMEM)


def dot(left, right, dims=NN):
    return lax.dot_general(left, right, dims, preferred_element_type=f32)


def struct(shape, dtype):
    return jax.ShapeDtypeStruct(shape, dtype)


def call(body, outs, specs, scratch=(), mib=16, flops=1 << 26, data=1 << 22, name=None, **extra):
    return pl.pallas_call(
        body,
        out_shape=outs,
        in_specs=specs,
        scratch_shapes=list(scratch),
        compiler_params=pltpu.CompilerParams(vmem_limit_bytes=mib << 20),
        cost_estimate=pl.CostEstimate(flops=flops, bytes_accessed=data, transcendentals=0),
        name=name,
        **extra,
    )


def normalize(values):
    center = values - jnp.mean(values, axis=-1, keepdims=True)
    inverse = lax.rsqrt(jnp.mean(center * center, axis=-1, keepdims=True) + epsilon)
    return center * inverse, inverse


def grid_kernel(send_ref, feat_ref, wk_ref, wv_ref, norm_ref, kv_ref, out_ref):
    step = pl.program_id(0)
    unit, _ = normalize(feat_ref[...].astype(f32))
    rows = unit.astype(bf16)
    norm_ref[...] = rows
    weight = jnp.concatenate([wk_ref[...], wv_ref[...]], axis=0)
    both = dot(rows, weight, NT).astype(bf16)
    per = both.shape[0] // B
    for i in range(per):
        kv_ref[step * per + i] = both[i * B : (i + 1) * B]

    @pl.when(step == pl.num_programs(0) - 1)
    def _():
        for i in range(out_ref.shape[0]):
            out_ref[i] = kv_ref[send_ref[i]]


def grid_part(send, feat, wk, wv, shards):
    rows = feat.shape[0]
    steps = 4
    return pl.pallas_call(
        grid_kernel,
        grid=(steps,),
        out_shape=(
            struct((rows, C), bf16),
            struct((rows // B, B, 2 * D), bf16),
            struct((shards, B, 2 * D), bf16),
        ),
        in_specs=[
            SMEM,
            pl.BlockSpec((rows // steps, C), lambda i: (i, 0)),
            pl.BlockSpec((D, C), lambda i: (0, 0)),
            pl.BlockSpec((D, C), lambda i: (0, 0)),
        ],
        out_specs=(
            pl.BlockSpec((rows // steps, C), lambda i: (i, 0)),
            pl.BlockSpec((rows // B, B, 2 * D), lambda i: (0, 0, 0)),
            pl.BlockSpec((shards, B, 2 * D), lambda i: (0, 0, 0)),
        ),
        compiler_params=pltpu.CompilerParams(vmem_limit_bytes=60 << 20),
        cost_estimate=pl.CostEstimate(
            flops=1 << 28, bytes_accessed=6 << 20, transcendentals=0
        ),
        name="grid_part",
    )(send, feat, wk, wv)


def query_kernel(mesh_ref, wq_ref, out_ref):
    for b in range(out_ref.shape[0]):
        unit, _ = normalize(mesh_ref[b * B : (b + 1) * B].astype(f32))
        rows = dot(wq_ref[...], unit.astype(bf16), NT).astype(bf16).astype(f32) * score_scale
        out_ref[b] = rows.astype(bf16)


def fill_pool(pool_ref, own_ref, arrived_ref):
    own = own_ref.shape[0]
    for i in range(own):
        pool_ref[i] = own_ref[i]
    for i in range(arrived_ref.shape[0]):
        pool_ref[own + i] = arrived_ref[i]


def folded(op, values):
    parts = [values[i * 8 : (i + 1) * 8] for i in range(values.shape[0] // 8)]
    while len(parts) > 1:
        parts = [
            op(parts[i], parts[i + 1]) if i + 1 < len(parts) else parts[i]
            for i in range(0, len(parts), 2)
        ]
    return parts[0]


def encoder_kernel(
    slot_ref, count_ref, bias_ref, own_ref, arrived_ref, query_ref,
    wide_ref, out_ref, lse_ref, pool_ref, score_ref,
):
    fill_pool(pool_ref, own_ref, arrived_ref)
    full = jnp.where(count_ref[0] == FULL, 0, 1)
    for m, total in ((full, FULL), (1 - full, REST)):
        stack = jnp.concatenate([query_ref[m], jnp.zeros((D, B), bf16)], axis=0)

        def scores(e, top, m=m, stack=stack):
            value = dot(pool_ref[slot_ref[m, e]], stack) + bias_ref[m, e]
            score_ref[e] = value
            return jnp.maximum(top, folded(jnp.maximum, value))

        top = lax.fori_loop(0, total, scores, jnp.full((8, B), -jnp.inf, f32), unroll=3)
        top = jnp.max(top, axis=0, keepdims=True)

        def mix(e, carry, m=m, top=top):
            low, acc = carry
            raised = jnp.exp(score_ref[e] - top)
            acc = acc + dot(pool_ref[slot_ref[m, e]], raised.astype(bf16), TN)
            return low + folded(jnp.add, raised), acc

        low, acc = lax.fori_loop(
            0, total, mix, (jnp.zeros((8, B), f32), jnp.zeros((2 * D, B), f32)), unroll=3
        )
        low = jnp.sum(low, axis=0, keepdims=True)
        rows = acc[D:] / low
        wide_ref[m] = rows
        out_ref[m] = rows.astype(bf16)
        lse_ref[m] = jnp.broadcast_to(top + jnp.log(low), (8, B))


def middle_kernel(
    at_ref, bias_ref, heads_ref, gathered_ref, mesh_ref, wq_ref, wk_ref, wv_ref, wl_ref,
    pack_ref, tail_ref, unit_ref, enc_ref,
):
    parts = heads_ref.shape[0]
    w_out = gathered_ref[:, 0:D, :].reshape(parts * D, C)
    w_layer = jnp.concatenate([wk_ref[...], wv_ref[...], wq_ref[...]], axis=0)
    half = parts // 2
    height = 2 * B // parts
    tail_ref[height:] = jnp.zeros((8, C), f32)
    queries, grads = [], []
    for b in range(2):
        rows = slice(b * B, (b + 1) * B)
        heads = heads_ref[:, b].reshape(parts * D, B)
        enc = mesh_ref[rows].astype(f32) + dot(heads, w_out, TN)
        enc_ref[rows] = enc
        unit, inverse = normalize(enc)
        unit = unit.astype(bf16)
        unit_ref[rows] = unit
        tail_ref[height:, b * B : (b + 1) * B] = jnp.broadcast_to(inverse, (B, 128)).T[0:8]
        both = dot(unit, w_layer, NT).astype(bf16)
        pack_ref[rows] = both[:, : 2 * D]
        queries.append((both[:, 2 * D :].astype(f32) * score_scale).astype(bf16))
        cot = gathered_ref[half * b : half * (b + 1), 2 * D :, :].reshape(B, C)
        grads.append(dot(cot, wl_ref[...], NT).astype(bf16))
    tail_ref[:height] = enc_ref[pl.ds(pl.multiple_of(at_ref[0] * height, height), height), :]
    pack_ref[2 * B : 3 * B] = jnp.concatenate(queries, axis=1)
    pack_ref[3 * B : 4 * B] = jnp.concatenate(grads, axis=1)
    row = lax.broadcasted_iota(jnp.int32, (8, 128), 0)
    table = jnp.zeros((8, 128), f32)
    for b in range(2):
        for n in range(3):
            table = jnp.where(row == 3 * b + n, bias_ref[b, n], table)
    high = table.astype(bf16).astype(f32)
    rest = table - high
    middle = rest.astype(bf16).astype(f32)
    tail = [high, middle, rest - middle, jnp.zeros((8, 128), f32)]
    pack_ref[4 * B : 4 * B + 32] = jnp.concatenate(tail, axis=0).astype(bf16)


def side_kernel(gathered_ref, unit_ref, tail_ref, wo_ref, cot_ref, unit_out_ref, inv_out_ref, sum_ref):
    half = gathered_ref.shape[0] // 2
    weight = wo_ref[...]
    for b in range(2):
        rows = slice(b * B, (b + 1) * B)
        cot = gathered_ref[half * b : half * (b + 1), 2 * D :, :].reshape(B, C)
        cot_ref[b] = dot(weight, cot, NT)
        unit_out_ref[b] = dot(weight, unit_ref[rows], NT)
        inv_out_ref[b] = tail_ref[tail_ref.shape[0] - 8 :, b * B : (b + 1) * B]
    sum_ref[...] = jnp.broadcast_to(
        jnp.sum(weight.astype(f32), axis=1, keepdims=True), sum_ref.shape
    )


def layer_kernel(
    own_ref, left_ref, right_ref, unit_ref, wq_ref, wk_ref, wv_ref, gathered_ref, send_ref
):
    zero = jnp.zeros((B, D), bf16)

    def block(ref, b):
        return ref[b * B : (b + 1) * B]

    def stacked(ref, b):
        lanes = slice(b * D, (b + 1) * D)
        query = ref[2 * B : 3 * B][:, lanes]
        grad = ref[3 * B : 4 * B][:, lanes]
        return jnp.concatenate(
            [jnp.concatenate([query, zero], axis=1), jnp.concatenate([zero, grad], axis=1)], axis=0
        )

    def table(ref):
        tail = ref[4 * B : 4 * B + 32].astype(f32)
        return tail[0:8] + tail[8:16] + tail[16:24]

    kv = [block(ref, b) for ref in (left_ref, own_ref, right_ref) for b in range(2)]
    own_bias = table(own_ref)
    queries = [(left_ref, 1, table(left_ref)), (own_ref, 0, own_bias), (own_ref, 1, own_bias)]
    queries.append((right_ref, 0, table(right_ref)))
    heads = []
    grad_kv = [jnp.zeros((B, 2 * D), f32), jnp.zeros((B, 2 * D), f32)]
    grad_q = []
    for j, (ref, b, bias) in enumerate(queries):
        pair = stacked(ref, b)
        window = kv[j : j + 3]
        both = [dot(rows, pair, NT) for rows in window]
        scores = [both[n][:, :B] + bias[3 * b + n : 3 * b + n + 1] for n in range(3)]
        top = folded(jnp.maximum, jnp.concatenate(scores, axis=0))
        top = jnp.max(top, axis=0, keepdims=True)
        raised = [jnp.exp(s - top) for s in scores]
        low = sum(folded(jnp.add, r) for r in raised)
        scale = 1.0 / jnp.sum(low, axis=0, keepdims=True)
        soft = [r * scale for r in raised]
        inner = sum(folded(jnp.add, soft[n] * both[n][:, B:]) for n in range(3))
        inner = jnp.sum(inner, axis=0, keepdims=True)
        mixed = [
            jnp.concatenate(
                [(soft[n] * (both[n][:, B:] - inner)).astype(bf16), soft[n].astype(bf16)], axis=1
            )
            for n in range(3)
        ]
        for n in range(3):
            own = j + n - 2
            if 0 <= own < 2:
                grad_kv[own] = grad_kv[own] + dot(mixed[n], pair)
        if 1 <= j <= 2:
            back = sum(dot(mixed[n], window[n], TN) for n in range(3))
            grad_q.append((back[:B, :D] * score_scale).astype(bf16))
            heads.append(back[B:, D:].astype(bf16))
    parts = gathered_ref.shape[0]
    w_layer = jnp.concatenate([wk_ref[...], wv_ref[...], wq_ref[...]], axis=0)
    totals, stats = [], jnp.zeros((8, 128), f32)
    lane = lax.broadcasted_iota(jnp.int32, (B, 128), 1)
    for b in range(2):
        grad = jnp.concatenate([grad_kv[b].astype(bf16), grad_q[b]], axis=1)
        total = dot(grad, w_layer)
        first = jnp.mean(total, axis=1, keepdims=True)
        second = jnp.mean(total * unit_ref[b * B : (b + 1) * B].astype(f32), axis=1, keepdims=True)
        first_high = first.astype(bf16).astype(f32)
        second_high = second.astype(bf16).astype(f32)
        columns = (first_high, second_high, first - first_high, second - second_high)
        table_b = jnp.zeros((B, 128), f32)
        for k, column in enumerate(columns):
            table_b = jnp.where(lane == 4 * b + k, column, table_b)
        stats = stats + table_b.T[0:8]
        totals.append(total.astype(bf16))
    stats = jnp.concatenate([stats[:, :D], stats[:, D:]], axis=0).astype(bf16)
    total = jnp.concatenate(totals, axis=0)
    heads = jnp.concatenate(heads, axis=0)
    share = heads.shape[0] // parts
    for z in range(parts):
        piece = dot(gathered_ref[z, 0:D, :], total, NT).astype(bf16)
        for b in range(2):
            send_ref[z, b * D : (b + 1) * D] = piece[:, b * B : (b + 1) * B]
        rows = heads[z * share : (z + 1) * share]
        send_ref[z, 2 * D :] = jnp.concatenate([rows, stats], axis=1)


def back_kernel(
    slot_ref, count_ref, bias_ref, me_ref, arrived_grad_ref, cot_ref, unit_ref, inv_ref, sum_ref,
    wide_ref, lse_ref, query_ref, own_ref, arrived_ref,
    own_out_ref, send_ref, pool_ref, grad_ref, pair_ref, inner_ref,
):
    fill_pool(pool_ref, own_ref, arrived_ref)
    zero = jnp.zeros((D, B), bf16)
    total = arrived_grad_ref[0].astype(f32)
    for z in range(1, arrived_grad_ref.shape[0]):
        total = total + arrived_grad_ref[z].astype(f32)
    stats = total[2 * D :, D:]
    stats = jnp.concatenate([stats[0:8], stats[8:16]], axis=1)
    for b in range(2):
        first = stats[4 * b : 4 * b + 1] + stats[4 * b + 2 : 4 * b + 3]
        second = stats[4 * b + 1 : 4 * b + 2] + stats[4 * b + 3 : 4 * b + 4]
        inside = total[b * D : (b + 1) * D] - first * sum_ref[...] - second * unit_ref[b]
        grad = (cot_ref[b] + inv_ref[b][0:1] * inside).astype(bf16)
        inner = jnp.sum(grad.astype(f32) * wide_ref[b], axis=0, keepdims=True)
        inner_ref[b] = jnp.broadcast_to(inner, (8, B))
        pair_ref[b] = jnp.concatenate(
            [
                jnp.concatenate([query_ref[b], zero], axis=1),
                jnp.concatenate([zero, grad], axis=1),
            ],
            axis=0,
        )
    own = own_ref.shape[0]
    grad_ref[own + me_ref[0]] = jnp.zeros((B, 2 * D), f32)
    full = jnp.where(count_ref[0] == FULL, 0, 1)
    for m, total in ((full, FULL), (1 - full, REST)):
        pair = pair_ref[m]
        lse = lse_ref[m][0:1]
        inner = inner_ref[m][0:1]

        def step(e, carry, m=m, pair=pair, lse=lse, inner=inner):
            slot = slot_ref[m, e]
            both = dot(pool_ref[slot], pair)
            soft = jnp.exp(both[:, :B] + (bias_ref[m, e] - lse))
            mixed = jnp.concatenate(
                [(soft * (both[:, B:] - inner)).astype(bf16), soft.astype(bf16)], axis=1
            )
            grad_ref[slot] = dot(mixed, pair, NT)
            return carry

        lax.fori_loop(0, total, step, 0, unroll=3)
    for i in range(own):
        own_out_ref[i] = grad_ref[i]
    for i in range(send_ref.shape[0]):
        send_ref[i] = grad_ref[own + i].astype(bf16)


def final_kernel(send_ref, norm_ref, own_ref, back_ref, out_ref, acc_ref):
    for i in range(own_ref.shape[0]):
        acc_ref[i] = own_ref[i]

    def add(i, carry):
        slot = send_ref[i]
        acc_ref[slot] = acc_ref[slot] + back_ref[i].astype(f32)
        return carry

    lax.fori_loop(0, back_ref.shape[0], add, 0, unroll=2)
    rows = acc_ref[...].reshape(norm_ref.shape[0], 2 * D).astype(bf16)
    shards, height = out_ref.shape[0], out_ref.shape[1]
    tile = 256
    for c in range(C // tile):
        part = dot(rows, norm_ref[:, c * tile : (c + 1) * tile], TN).T
        per = tile // height
        out_ref[c * per : (c + 1) * per] = part.astype(bf16).reshape(per, height, 2 * D)


def output_kernel(heads_ref, weight_ref, tail_ref, out_ref):
    total = tail_ref[: out_ref.shape[0]]
    for h in range(heads_ref.shape[0]):
        total = total + dot(heads_ref[h, 2 * D :][:, :D], weight_ref[h, D : 2 * D])
    out_ref[...] = total.astype(bf16)


def sum_kernel(parts_ref, key_ref, value_ref):
    total = parts_ref[0].astype(f32)
    for i in range(1, parts_ref.shape[0]):
        total = total + parts_ref[i].astype(f32)
    key_ref[...] = total[:, :D]
    value_ref[...] = total[:, D:]


def exchange(array, axis):
    return lax.all_to_all(array, axis, split_axis=0, concat_axis=0, tiled=True)


def on_device(
    grid_feat,
    mesh_feat,
    query_weight,
    key_weight,
    value_weight,
    enc_out_weight,
    layer_query,
    layer_key,
    layer_value,
    layer_out_weight,
    enc_bias,
    layer_bias,
    send_list,
    edge_slot,
    edge_count,
    cotangent,
):
    shards = lax.axis_size("grid")
    parts = lax.axis_size("head")
    own = grid_feat.shape[0] // B
    share = cotangent.shape[0]
    send = send_list[0]
    enc_table = enc_bias[:, :, 0]
    layer_table = layer_bias[:, :, 0]
    shard_at = lax.axis_index("grid").astype(jnp.int32)[None]
    head_at = lax.axis_index("head").astype(jnp.int32)[None]
    forward = [(i, (i + 1) % shards) for i in range(shards)]
    backward = [(t, s) for s, t in forward]

    gathered = lax.all_gather(
        jnp.concatenate([enc_out_weight, layer_out_weight, cotangent], axis=0),
        "head",
        axis=0,
        tiled=False,
    )
    query_weight, key_weight, value_weight, layer_query, layer_key, layer_value = (
        weight.T
        for weight in (query_weight, key_weight, value_weight, layer_query, layer_key, layer_value)
    )

    grid_norm, own_kv, outgoing = grid_part(send, grid_feat, key_weight, value_weight, shards)
    arrived_kv = exchange(outgoing, "grid")
    queries = call(
        query_kernel, struct((2, D, B), bf16), [VMEM] * 2, name="query_part", data=1 << 20
    )(mesh_feat, query_weight)
    wide_heads, enc_heads, lse = call(
        encoder_kernel,
        (struct((2, D, B), f32), struct((2, D, B), bf16), struct((2, 8, B), f32)),
        [SMEM] * 3 + [VMEM] * 3,
        [pltpu.VMEM((own + shards, B, 2 * D), bf16), pltpu.VMEM((FULL, B, B), f32)],
        name="encoder_part",
    )(edge_slot, edge_count, enc_table, own_kv, arrived_kv, queries)
    all_heads = lax.all_gather(enc_heads, "head", axis=0, tiled=False)
    pack, tail, unit = call(
        middle_kernel,
        (
            struct((4 * B + 32, 2 * D), bf16),
            struct((share + 8, C), f32),
            struct((2 * B, C), bf16),
        ),
        [SMEM] * 2 + [VMEM] * 7,
        [pltpu.VMEM((2 * B, C), f32)],
        name="middle_part",
    )(
        head_at, layer_table, all_heads, gathered, mesh_feat, layer_query, layer_key, layer_value, layer_out_weight
    )
    left = lax.ppermute(pack, "grid", forward)
    right = lax.ppermute(pack, "grid", backward)
    cot_part, unit_part, inverse_row, weight_sum = call(
        side_kernel,
        (
            struct((2, D, B), f32),
            struct((2, D, B), f32),
            struct((2, 8, B), f32),
            struct((D, B), f32),
        ),
        [VMEM] * 4,
        name="side_part",
    )(gathered, unit, tail, enc_out_weight)
    mixed = call(
        layer_kernel, struct((parts, 2 * D + share, B), bf16), [VMEM] * 8, name="layer_part"
    )(pack, left, right, unit, layer_query, layer_key, layer_value, gathered)
    arrived_grad = exchange(mixed, "head")
    own_grad, send_grad = call(
        back_kernel,
        (struct((own, B, 2 * D), f32), struct((shards, B, 2 * D), bf16)),
        [SMEM] * 4 + [VMEM] * 10,
        [
            pltpu.VMEM((own + shards, B, 2 * D), bf16),
            pltpu.VMEM((own + shards, B, 2 * D), f32),
            pltpu.VMEM((2, 2 * D, 2 * B), bf16),
            pltpu.VMEM((2, 8, B), f32),
        ],
        name="back_part",
    )(
        edge_slot, edge_count, enc_table, shard_at, arrived_grad, cot_part, unit_part,
        inverse_row, weight_sum, wide_heads, lse, queries, own_kv, arrived_kv,
    )
    back_grad = exchange(send_grad, "grid")
    product = call(
        final_kernel,
        struct((shards, C // shards, 2 * D), bf16),
        [SMEM] + [VMEM] * 3,
        [pltpu.VMEM((own, B, 2 * D), f32)],
        name="final_part",
    )(send, grid_norm, own_grad, back_grad)
    pieces = exchange(product, "grid")
    mesh_out = call(
        output_kernel,
        struct((share, C), bf16),
        [VMEM] * 3,
        name="output_part",
    )(arrived_grad, gathered, tail)
    key_grad, value_grad = call(
        sum_kernel,
        (struct((C // shards, D), f32), struct((C // shards, D), f32)),
        [VMEM],
        name="sum_part",
    )(pieces)
    return mesh_out, key_grad, value_grad


def solution(mesh):
    in_specs = (
        P("grid", None),
        P("grid", None),
        P(None, "head"),
        P(None, "head"),
        P(None, "head"),
        P("head", None),
        P(None, "head"),
        P(None, "head"),
        P(None, "head"),
        P("head", None),
        P("grid", None, "head"),
        P("grid", None, "head"),
        P("grid", None),
        P("grid", None),
        P("grid"),
        P(("grid", "head"), None),
    )
    out_specs = (P(("grid", "head"), None), P("grid", "head"), P("grid", "head"))
    return jax.shard_map(
        on_device, mesh=mesh, in_specs=in_specs, out_specs=out_specs, check_vma=False
    )
```

```python
import jax
import jax.numpy as jnp
from jax import lax
from jax.experimental import pallas as pl
from jax.experimental.pallas import tpu as pltpu
from jax.sharding import PartitionSpec as P

D = 64
B = 128
C = 1024
FULL = 30
REST = 9
epsilon = 1e-05
score_scale = 0.125

f32 = jnp.float32
bf16 = jnp.bfloat16

NN = (((1,), (0,)), ((), ()))
NT = (((1,), (1,)), ((), ()))
TN = (((0,), (0,)), ((), ()))

VMEM = pl.BlockSpec(memory_space=pltpu.VMEM)
SMEM = pl.BlockSpec(memory_space=pltpu.SMEM)
HBM = pl.BlockSpec(memory_space=pltpu.HBM)


def dot(left, right, dims=NN):
    return lax.dot_general(left, right, dims, preferred_element_type=f32)


def struct(shape, dtype):
    return jax.ShapeDtypeStruct(shape, dtype)


def call(body, outs, specs, scratch=(), mib=16, flops=1 << 26, data=1 << 22, name=None, **extra):
    return pl.pallas_call(
        body,
        out_shape=outs,
        in_specs=specs,
        scratch_shapes=list(scratch),
        compiler_params=pltpu.CompilerParams(vmem_limit_bytes=mib << 20),
        cost_estimate=pl.CostEstimate(flops=flops, bytes_accessed=data, transcendentals=0),
        name=name,
        **extra,
    )


def normalize(values):
    center = values - jnp.mean(values, axis=-1, keepdims=True)
    inverse = lax.rsqrt(jnp.mean(center * center, axis=-1, keepdims=True) + epsilon)
    return center * inverse, inverse


def grid_kernel(send_ref, feat_ref, wk_ref, wv_ref, norm_ref, kv_ref, out_ref):
    step = pl.program_id(0)
    unit, _ = normalize(feat_ref[...].astype(f32))
    rows = unit.astype(bf16)
    norm_ref[...] = rows
    weight = jnp.concatenate([wk_ref[...], wv_ref[...]], axis=0)
    both = dot(rows, weight, NT).astype(bf16)
    per = both.shape[0] // B
    for i in range(per):
        kv_ref[step * per + i] = both[i * B : (i + 1) * B]

    @pl.when(step == pl.num_programs(0) - 1)
    def _():
        for i in range(out_ref.shape[0]):
            out_ref[i] = kv_ref[send_ref[i]]


def grid_part(send, feat, wk, wv, shards):
    rows = feat.shape[0]
    steps = 4
    return pl.pallas_call(
        grid_kernel,
        grid=(steps,),
        out_shape=(
            struct((rows, C), bf16),
            struct((rows // B, B, 2 * D), bf16),
            struct((shards, B, 2 * D), bf16),
        ),
        in_specs=[
            SMEM,
            pl.BlockSpec((rows // steps, C), lambda i: (i, 0)),
            pl.BlockSpec((D, C), lambda i: (0, 0)),
            pl.BlockSpec((D, C), lambda i: (0, 0)),
        ],
        out_specs=(
            pl.BlockSpec((rows // steps, C), lambda i: (i, 0)),
            pl.BlockSpec((rows // B, B, 2 * D), lambda i: (0, 0, 0)),
            pl.BlockSpec((shards, B, 2 * D), lambda i: (0, 0, 0)),
        ),
        compiler_params=pltpu.CompilerParams(vmem_limit_bytes=60 << 20),
        cost_estimate=pl.CostEstimate(
            flops=1 << 28, bytes_accessed=6 << 20, transcendentals=0
        ),
        name="grid_part",
    )(send, feat, wk, wv)


def rows_kernel(wo_ref, wl_ref, cot_ref, out_ref, sem_ref):
    half = D // 2
    start = pl.multiple_of(lax.rem(lax.axis_index("grid"), 2) * half, half)
    copies = [
        pltpu.make_async_copy(wo_ref, out_ref.at[0:D], sem_ref.at[0]),
        pltpu.make_async_copy(
            wl_ref.at[pl.ds(start, half)], out_ref.at[D : D + half], sem_ref.at[1]
        ),
        pltpu.make_async_copy(cot_ref, out_ref.at[D + half :], sem_ref.at[2]),
    ]
    for copy in copies:
        copy.start()
    for copy in copies:
        copy.wait()


def query_kernel(mesh_ref, wq_ref, out_ref):
    for b in range(out_ref.shape[0]):
        unit, _ = normalize(mesh_ref[b * B : (b + 1) * B].astype(f32))
        rows = dot(wq_ref[...], unit.astype(bf16), NT).astype(bf16).astype(f32) * score_scale
        out_ref[b] = rows.astype(bf16)


def fill_pool(pool_ref, own_ref, arrived_ref):
    own = own_ref.shape[0]
    for i in range(own):
        pool_ref[i] = own_ref[i]
    for i in range(arrived_ref.shape[0]):
        pool_ref[own + i] = arrived_ref[i]


def folded(op, values):
    parts = [values[i * 8 : (i + 1) * 8] for i in range(values.shape[0] // 8)]
    while len(parts) > 1:
        parts = [
            op(parts[i], parts[i + 1]) if i + 1 < len(parts) else parts[i]
            for i in range(0, len(parts), 2)
        ]
    return parts[0]


def fill_tables(slot_ref, bias_ref, full, reader_ref, edge_ref):
    for i in range(reader_ref.shape[0]):
        reader_ref[i] = 0
        edge_ref[i] = 0.0
    for m, total in ((full, FULL), (1 - full, REST)):

        def put(e, carry, m=m):
            slot = slot_ref[m, e]
            reader_ref[slot] = m
            edge_ref[slot] = bias_ref[m, e]
            return carry

        lax.fori_loop(0, total, put, 0, unroll=3)


def encoder_kernel(
    slot_ref, count_ref, bias_ref, me_ref, own_ref, arrived_ref, query_ref,
    out_ref, lse_ref, early_ref, pool_ref, score_ref, reader_ref, edge_ref,
):
    fill_pool(pool_ref, own_ref, arrived_ref)
    full = jnp.where(count_ref[0] == FULL, 0, 1)
    fill_tables(slot_ref, bias_ref, full, reader_ref, edge_ref)
    for m, total in ((full, FULL), (1 - full, REST)):
        stack = jnp.concatenate([query_ref[m], jnp.zeros((D, B), bf16)], axis=0)

        def scores(e, top, m=m, stack=stack):
            value = dot(pool_ref[slot_ref[m, e]], stack) + bias_ref[m, e]
            score_ref[e] = value
            return jnp.maximum(top, folded(jnp.maximum, value))

        top = lax.fori_loop(0, total, scores, jnp.full((8, B), -jnp.inf, f32), unroll=3)
        top = jnp.max(top, axis=0, keepdims=True)

        def mix(e, carry, m=m, top=top):
            low, acc = carry
            raised = jnp.exp(score_ref[e] - top)
            acc = acc + dot(pool_ref[slot_ref[m, e]], raised.astype(bf16), TN)
            return low + folded(jnp.add, raised), acc

        low, acc = lax.fori_loop(
            0, total, mix, (jnp.zeros((8, B), f32), jnp.zeros((2 * D, B), f32)), unroll=3
        )
        low = jnp.sum(low, axis=0, keepdims=True)
        out_ref[m] = (acc[D:] / low).astype(bf16)
        lse_ref[m] = jnp.broadcast_to(top + jnp.log(low), (8, B))
    own = own_ref.shape[0]
    row = lax.broadcasted_iota(jnp.int32, (16, B), 0)
    for p in range(early_ref.shape[0]):
        m = reader_ref[own + p]
        other = me_ref[0] != p
        early_ref[p, 0:D] = jnp.where(other, query_ref[m], jnp.zeros((D, B), bf16))
        early_ref[p, D : 2 * D] = jnp.where(other, out_ref[m], jnp.zeros((D, B), bf16))
        shift = jnp.concatenate([lse_ref[m], lse_ref[m]], axis=0) - edge_ref[own + p]
        shift = jnp.where(other, shift, 0.0)
        high = shift.astype(bf16).astype(f32)
        middle = (shift - high).astype(bf16).astype(f32)
        rest = shift - high - middle
        tail = jnp.where(row == 0, high, jnp.where(row == 1, middle, jnp.where(row == 2, rest, 0.0)))
        early_ref[p, 2 * D :] = tail.astype(bf16)


def middle_kernel(
    at_ref, bias_ref, heads_ref, gathered_ref, mesh_ref, wq_ref, wk_ref, wv_ref, wl_ref,
    pack_ref, tail_ref, unit_ref, enc_ref, w_out_ref, cot_ref, sem_ref,
):
    parts = heads_ref.shape[0]
    first = parts // 2
    copies = [
        pltpu.make_async_copy(
            gathered_ref.at[0:first, 0:D, :], w_out_ref.at[0:first], sem_ref.at[0]
        ),
        pltpu.make_async_copy(
            gathered_ref.at[first:parts, 0:D, :], w_out_ref.at[first:parts], sem_ref.at[1]
        ),
        pltpu.make_async_copy(
            gathered_ref.at[:, D + D // 2 :, :], cot_ref, sem_ref.at[2]
        ),
    ]
    for copy in copies:
        copy.start()
    copies[0].wait()
    for b in range(2):
        rows = slice(b * B, (b + 1) * B)
        heads = heads_ref[0:first, b].reshape(first * D, B)
        w_out = w_out_ref[0:first].reshape(first * D, C)
        enc_ref[rows] = mesh_ref[rows].astype(f32) + dot(heads, w_out, TN)
    copies[1].wait()
    copies[2].wait()
    w_layer = jnp.concatenate([wk_ref[...], wv_ref[...], wq_ref[...]], axis=0)
    half = parts // 2
    height = 2 * B // parts
    tail_ref[height:] = jnp.zeros((8, C), f32)
    queries, grads = [], []
    for b in range(2):
        rows = slice(b * B, (b + 1) * B)
        heads = heads_ref[first:, b].reshape((parts - first) * D, B)
        w_out = w_out_ref[first:].reshape((parts - first) * D, C)
        enc = enc_ref[rows] + dot(heads, w_out, TN)
        enc_ref[rows] = enc
        unit, inverse = normalize(enc)
        unit = unit.astype(bf16)
        unit_ref[rows] = unit
        tail_ref[height:, b * B : (b + 1) * B] = jnp.broadcast_to(inverse, (B, 128)).T[0:8]
        both = dot(unit, w_layer, NT).astype(bf16)
        pack_ref[rows] = both[:, : 2 * D]
        queries.append((both[:, 2 * D :].astype(f32) * score_scale).astype(bf16))
        cot = cot_ref[half * b : half * (b + 1)].reshape(B, C)
        grads.append(dot(cot, wl_ref[...], NT).astype(bf16))
    tail_ref[:height] = enc_ref[pl.ds(pl.multiple_of(at_ref[0] * height, height), height), :]
    pack_ref[2 * B : 3 * B] = jnp.concatenate(queries, axis=1)
    pack_ref[3 * B : 4 * B] = jnp.concatenate(grads, axis=1)
    row = lax.broadcasted_iota(jnp.int32, (8, 128), 0)
    table = jnp.zeros((8, 128), f32)
    for b in range(2):
        for n in range(3):
            table = jnp.where(row == 3 * b + n, bias_ref[b, n], table)
    high = table.astype(bf16).astype(f32)
    rest = table - high
    middle = rest.astype(bf16).astype(f32)
    tail = [high, middle, rest - middle, jnp.zeros((8, 128), f32)]
    pack_ref[4 * B : 4 * B + 32] = jnp.concatenate(tail, axis=0).astype(bf16)


def side_kernel(gathered_ref, unit_ref, tail_ref, wo_ref, cot_ref, unit_out_ref, inv_out_ref, sum_ref, half_ref):
    half = gathered_ref.shape[0] // 2
    weight = wo_ref[...]
    for b in range(2):
        rows = slice(b * B, (b + 1) * B)
        cot = gathered_ref[half * b : half * (b + 1), D + D // 2 :, :].reshape(B, C)
        cot_ref[b] = dot(weight, cot, NT)
        unit_out_ref[b] = dot(weight, unit_ref[rows], NT)
        inv_out_ref[b] = tail_ref[tail_ref.shape[0] - 8 :, b * B : (b + 1) * B]
    sum_ref[...] = jnp.broadcast_to(
        jnp.sum(weight.astype(f32), axis=1, keepdims=True), sum_ref.shape
    )
    half_ref[...] = gathered_ref[:, D : D + D // 2, :]


def layer_kernel(
    own_ref, left_ref, right_ref, unit_ref, wq_ref, wk_ref, wv_ref, gathered_ref, send_ref,
    w_out_ref, sem_ref,
):
    copy = pltpu.make_async_copy(gathered_ref.at[:, 0:D, :], w_out_ref, sem_ref)
    copy.start()
    zero = jnp.zeros((B, D), bf16)

    def block(ref, b):
        return ref[b * B : (b + 1) * B]

    def stacked(ref, b):
        lanes = slice(b * D, (b + 1) * D)
        query = ref[2 * B : 3 * B][:, lanes]
        grad = ref[3 * B : 4 * B][:, lanes]
        return jnp.concatenate(
            [jnp.concatenate([query, zero], axis=1), jnp.concatenate([zero, grad], axis=1)], axis=0
        )

    def table(ref):
        tail = ref[4 * B : 4 * B + 32].astype(f32)
        return tail[0:8] + tail[8:16] + tail[16:24]

    kv = [block(ref, b) for ref in (left_ref, own_ref, right_ref) for b in range(2)]
    own_bias = table(own_ref)
    queries = [(left_ref, 1, table(left_ref)), (own_ref, 0, own_bias), (own_ref, 1, own_bias)]
    queries.append((right_ref, 0, table(right_ref)))
    heads = []
    grad_kv = [jnp.zeros((B, 2 * D), f32), jnp.zeros((B, 2 * D), f32)]
    grad_q = []
    for j, (ref, b, bias) in enumerate(queries):
        pair = stacked(ref, b)
        window = kv[j : j + 3]
        both = [dot(rows, pair, NT) for rows in window]
        scores = [both[n][:, :B] + bias[3 * b + n : 3 * b + n + 1] for n in range(3)]
        top = folded(jnp.maximum, jnp.concatenate(scores, axis=0))
        top = jnp.max(top, axis=0, keepdims=True)
        raised = [jnp.exp(s - top) for s in scores]
        low = sum(folded(jnp.add, r) for r in raised)
        scale = 1.0 / jnp.sum(low, axis=0, keepdims=True)
        soft = [r * scale for r in raised]
        inner = sum(folded(jnp.add, soft[n] * both[n][:, B:]) for n in range(3))
        inner = jnp.sum(inner, axis=0, keepdims=True)
        mixed = [
            jnp.concatenate(
                [(soft[n] * (both[n][:, B:] - inner)).astype(bf16), soft[n].astype(bf16)], axis=1
            )
            for n in range(3)
        ]
        for n in range(3):
            own = j + n - 2
            if 0 <= own < 2:
                grad_kv[own] = grad_kv[own] + dot(mixed[n], pair)
        if 1 <= j <= 2:
            back = sum(dot(mixed[n], window[n], TN) for n in range(3))
            grad_q.append((back[:B, :D] * score_scale).astype(bf16))
            heads.append(back[B:, D:].astype(bf16))
    parts = gathered_ref.shape[0]
    w_layer = jnp.concatenate([wk_ref[...], wv_ref[...], wq_ref[...]], axis=0)
    totals, stats = [], jnp.zeros((8, 128), f32)
    lane = lax.broadcasted_iota(jnp.int32, (B, 128), 1)
    for b in range(2):
        grad = jnp.concatenate([grad_kv[b].astype(bf16), grad_q[b]], axis=1)
        total = dot(grad, w_layer)
        first = jnp.mean(total, axis=1, keepdims=True)
        second = jnp.mean(total * unit_ref[b * B : (b + 1) * B].astype(f32), axis=1, keepdims=True)
        first_high = first.astype(bf16).astype(f32)
        second_high = second.astype(bf16).astype(f32)
        columns = (first_high, second_high, first - first_high, second - second_high)
        table_b = jnp.zeros((B, 128), f32)
        for k, column in enumerate(columns):
            table_b = jnp.where(lane == 4 * b + k, column, table_b)
        stats = stats + table_b.T[0:8]
        totals.append(total.astype(bf16))
    stats = jnp.concatenate([stats[:, :D], stats[:, D:]], axis=0).astype(bf16)
    total = jnp.concatenate(totals, axis=0)
    heads = jnp.concatenate(heads, axis=0)
    share = heads.shape[0] // parts
    copy.wait()
    for z in range(parts):
        piece = dot(w_out_ref[z], total, NT).astype(bf16)
        for b in range(2):
            send_ref[z, b * D : (b + 1) * D] = piece[:, b * B : (b + 1) * B]
        rows = heads[z * share : (z + 1) * share]
        send_ref[z, 2 * D :] = jnp.concatenate([rows, stats], axis=1)


def grad_kernel(
    slot_ref, count_ref, bias_ref, me_ref, arrived_ref, cot_ref, unit_ref, inv_ref, sum_ref,
    grad_ref, send_ref, reader_ref, edge_ref,
):
    full = jnp.where(count_ref[0] == FULL, 0, 1)
    fill_tables(slot_ref, bias_ref, full, reader_ref, edge_ref)
    total = arrived_ref[0].astype(f32)
    for z in range(1, arrived_ref.shape[0]):
        total = total + arrived_ref[z].astype(f32)
    stats = total[2 * D :, D:]
    stats = jnp.concatenate([stats[0:8], stats[8:16]], axis=1)
    for b in range(2):
        first = stats[4 * b : 4 * b + 1] + stats[4 * b + 2 : 4 * b + 3]
        second = stats[4 * b + 1 : 4 * b + 2] + stats[4 * b + 3 : 4 * b + 4]
        inside = total[b * D : (b + 1) * D] - first * sum_ref[...] - second * unit_ref[b]
        grad_ref[b] = (cot_ref[b] + inv_ref[b][0:1] * inside).astype(bf16)
    shards = send_ref.shape[0]
    own = reader_ref.shape[0] - shards
    for p in range(shards):
        block = grad_ref[reader_ref[own + p]]
        send_ref[p] = jnp.where(me_ref[0] != p, block, jnp.zeros((D, B), bf16))


def final_kernel(
    send_ref, slot_ref, count_ref, bias_ref, norm_ref, kv_ref, early_ref, grads_ref,
    query_ref, heads_ref, lse_ref, grad_ref, out_ref, acc_ref, reader_ref, edge_ref,
    held_ref, sem_ref,
):
    copy = pltpu.make_async_copy(norm_ref, held_ref, sem_ref)
    copy.start()
    full = jnp.where(count_ref[0] == FULL, 0, 1)
    fill_tables(slot_ref, bias_ref, full, reader_ref, edge_ref)
    zero = jnp.zeros((D, B), bf16)

    def back(keys, query, heads, shift, grad):
        inner = jnp.sum(grad.astype(f32) * heads.astype(f32), axis=0, keepdims=True)
        pair = jnp.concatenate(
            [jnp.concatenate([query, zero], axis=1), jnp.concatenate([zero, grad], axis=1)], axis=0
        )
        both = dot(keys, pair)
        soft = jnp.exp(both[:, :B] - shift)
        mixed = jnp.concatenate(
            [(soft * (both[:, B:] - inner)).astype(bf16), soft.astype(bf16)], axis=1
        )
        return dot(mixed, pair, NT)

    def own_step(v, carry):
        m = reader_ref[v]
        shift = lse_ref[m][0:1] - edge_ref[v]
        acc_ref[v] = back(kv_ref[v], query_ref[m], heads_ref[m], shift, grad_ref[m])
        return carry

    lax.fori_loop(0, kv_ref.shape[0], own_step, 0, unroll=4)

    def sent_step(r, carry):
        slot = send_ref[r]
        block = early_ref[r]
        tail = block[2 * D :].astype(f32)
        shift = tail[0:1] + tail[1:2] + tail[2:3]
        part = back(kv_ref[slot], block[:D], block[D : 2 * D], shift, grads_ref[r])
        acc_ref[slot] = acc_ref[slot] + part
        return carry

    lax.fori_loop(0, early_ref.shape[0], sent_step, 0, unroll=4)
    rows = acc_ref[...].reshape(norm_ref.shape[0], 2 * D).astype(bf16)
    copy.wait()
    shards, height = out_ref.shape[0], out_ref.shape[1]
    tile = 256
    for c in range(C // tile):
        part = dot(rows, held_ref[:, c * tile : (c + 1) * tile], TN).T
        per = tile // height
        out_ref[c * per : (c + 1) * per] = part.astype(bf16).reshape(per, height, 2 * D)


def output_kernel(me_ref, heads_ref, mine_ref, other_ref, tail_ref, out_ref):
    total = tail_ref[: out_ref.shape[0]]
    even = lax.rem(me_ref[0], 2) == 0
    half = D // 2
    for h in range(heads_ref.shape[0]):
        rows = heads_ref[h, 2 * D :][:, :D]
        low = jnp.where(even, mine_ref[h], other_ref[h])
        high = jnp.where(even, other_ref[h], mine_ref[h])
        total = total + dot(rows[:, :half], low) + dot(rows[:, half:], high)
    out_ref[...] = total.astype(bf16)


def sum_kernel(parts_ref, key_ref, value_ref):
    total = parts_ref[0].astype(f32)
    for i in range(1, parts_ref.shape[0]):
        total = total + parts_ref[i].astype(f32)
    key_ref[...] = total[:, :D]
    value_ref[...] = total[:, D:]


def exchange(array, axis):
    return lax.all_to_all(array, axis, split_axis=0, concat_axis=0, tiled=True)


def on_device(
    grid_feat,
    mesh_feat,
    query_weight,
    key_weight,
    value_weight,
    enc_out_weight,
    layer_query,
    layer_key,
    layer_value,
    layer_out_weight,
    enc_bias,
    layer_bias,
    send_list,
    edge_slot,
    edge_count,
    cotangent,
):
    shards = lax.axis_size("grid")
    parts = lax.axis_size("head")
    own = grid_feat.shape[0] // B
    share = cotangent.shape[0]
    send = send_list[0]
    enc_table = enc_bias[:, :, 0]
    layer_table = layer_bias[:, :, 0]
    shard_at = lax.axis_index("grid").astype(jnp.int32)[None]
    head_at = lax.axis_index("head").astype(jnp.int32)[None]
    forward = [(i, (i + 1) % shards) for i in range(shards)]
    backward = [(t, s) for s, t in forward]

    half = D // 2
    shared_rows = call(
        rows_kernel,
        struct((D + half + share, C), bf16),
        [HBM] * 3,
        [pltpu.SemaphoreType.DMA((3,))],
        name="rows_part",
        mib=61,
        out_specs=HBM,
    )(enc_out_weight, layer_out_weight, cotangent)
    gathered = lax.all_gather(shared_rows, "head", axis=0, tiled=False)
    query_weight, key_weight, value_weight, layer_query, layer_key, layer_value = (
        weight.T
        for weight in (query_weight, key_weight, value_weight, layer_query, layer_key, layer_value)
    )

    grid_norm, own_kv, outgoing = grid_part(send, grid_feat, key_weight, value_weight, shards)
    arrived_kv = exchange(outgoing, "grid")
    queries = call(
        query_kernel, struct((2, D, B), bf16), [VMEM] * 2, name="query_part", data=1 << 20
    )(mesh_feat, query_weight)
    tables = [pltpu.SMEM((own + shards,), jnp.int32), pltpu.SMEM((own + shards,), f32)]
    enc_heads, lse, early = call(
        encoder_kernel,
        (
            struct((2, D, B), bf16),
            struct((2, 8, B), f32),
            struct((shards, 2 * D + 16, B), bf16),
        ),
        [SMEM] * 4 + [VMEM] * 3,
        [pltpu.VMEM((own + shards, B, 2 * D), bf16), pltpu.VMEM((FULL, B, B), f32)] + tables,
        name="encoder_part",
    )(edge_slot, edge_count, enc_table, shard_at, own_kv, arrived_kv, queries)
    arrived_early = exchange(early, "grid")
    all_heads = lax.all_gather(enc_heads, "head", axis=0, tiled=False)
    pack, tail, unit = call(
        middle_kernel,
        (
            struct((4 * B + 32, 2 * D), bf16),
            struct((share + 8, C), f32),
            struct((2 * B, C), bf16),
        ),
        [SMEM] * 2 + [VMEM, HBM] + [VMEM] * 5,
        [
            pltpu.VMEM((2 * B, C), f32),
            pltpu.VMEM((parts, D, C), bf16),
            pltpu.VMEM((parts, share, C), bf16),
            pltpu.SemaphoreType.DMA((3,)),
        ],
        name="middle_part",
        mib=61,
    )(
        head_at, layer_table, all_heads, gathered, mesh_feat, layer_query, layer_key, layer_value, layer_out_weight
    )
    left = lax.ppermute(pack, "grid", forward)
    right = lax.ppermute(pack, "grid", backward)
    arrived_early, left, right = lax.optimization_barrier((arrived_early, left, right))
    cot_part, unit_part, inverse_row, weight_sum, half_mine = call(
        side_kernel,
        (
            struct((2, D, B), f32),
            struct((2, D, B), f32),
            struct((2, 8, B), f32),
            struct((D, B), f32),
            struct((parts, half, C), bf16),
        ),
        [VMEM] * 4,
        name="side_part",
    )(gathered, unit, tail, enc_out_weight)
    half_other = lax.ppermute(half_mine, "grid", [(i, i ^ 1) for i in range(shards)])
    mixed = call(
        layer_kernel,
        struct((parts, 2 * D + share, B), bf16),
        [VMEM] * 7 + [HBM],
        [pltpu.VMEM((parts, D, C), bf16), pltpu.SemaphoreType.DMA],
        name="layer_part",
        mib=61,
    )(pack, left, right, unit, layer_query, layer_key, layer_value, gathered)
    arrived_grad = exchange(mixed, "head")
    grads, send_grads = call(
        grad_kernel,
        (struct((2, D, B), bf16), struct((shards, D, B), bf16)),
        [SMEM] * 4 + [VMEM] * 5,
        tables,
        name="grad_part",
    )(
        edge_slot, edge_count, enc_table, shard_at, arrived_grad, cot_part, unit_part,
        inverse_row, weight_sum,
    )
    arrived_grads = exchange(send_grads, "grid")
    product = call(
        final_kernel,
        struct((shards, C // shards, 2 * D), bf16),
        [SMEM] * 4 + [HBM] + [VMEM] * 7,
        [pltpu.VMEM((own, B, 2 * D), f32)]
        + tables
        + [pltpu.VMEM(grid_norm.shape, bf16), pltpu.SemaphoreType.DMA],
        name="final_part",
        mib=61,
    )(
        send, edge_slot, edge_count, enc_table, grid_norm, own_kv, arrived_early, arrived_grads,
        queries, enc_heads, lse, grads,
    )
    pieces = exchange(product, "grid")
    mesh_out = call(
        output_kernel,
        struct((share, C), bf16),
        [SMEM] + [VMEM] * 4,
        name="output_part",
    )(shard_at, arrived_grad, half_mine, half_other, tail)
    key_grad, value_grad = call(
        sum_kernel,
        (struct((C // shards, D), f32), struct((C // shards, D), f32)),
        [VMEM],
        name="sum_part",
    )(pieces)
    return mesh_out, key_grad, value_grad


def solution(mesh):
    in_specs = (
        P("grid", None),
        P("grid", None),
        P(None, "head"),
        P(None, "head"),
        P(None, "head"),
        P("head", None),
        P(None, "head"),
        P(None, "head"),
        P(None, "head"),
        P("head", None),
        P("grid", None, "head"),
        P("grid", None, "head"),
        P("grid", None),
        P("grid", None),
        P("grid"),
        P(("grid", "head"), None),
    )
    out_specs = (P(("grid", "head"), None), P("grid", "head"), P("grid", "head"))
    return jax.shard_map(
        on_device, mesh=mesh, in_specs=in_specs, out_specs=out_specs, check_vma=False
    )
```

```python
import jax
import jax.numpy as jnp
from jax import lax
from jax.experimental import pallas as pl
from jax.experimental.pallas import tpu as pltpu
from jax.sharding import PartitionSpec as P

D = 64
B = 128
C = 1024
FULL = 30
REST = 9
epsilon = 1e-05
score_scale = 0.125

f32 = jnp.float32
bf16 = jnp.bfloat16

NN = (((1,), (0,)), ((), ()))
NT = (((1,), (1,)), ((), ()))
TN = (((0,), (0,)), ((), ()))

VMEM = pl.BlockSpec(memory_space=pltpu.VMEM)
SMEM = pl.BlockSpec(memory_space=pltpu.SMEM)
HBM = pl.BlockSpec(memory_space=pltpu.HBM)


def dot(left, right, dims=NN):
    return lax.dot_general(left, right, dims, preferred_element_type=f32)


def struct(shape, dtype):
    return jax.ShapeDtypeStruct(shape, dtype)


def call(body, outs, specs, scratch=(), mib=16, flops=1 << 26, data=1 << 22, name=None, **extra):
    return pl.pallas_call(
        body,
        out_shape=outs,
        in_specs=specs,
        scratch_shapes=list(scratch),
        compiler_params=pltpu.CompilerParams(vmem_limit_bytes=mib << 20),
        cost_estimate=pl.CostEstimate(flops=flops, bytes_accessed=data, transcendentals=0),
        name=name,
        **extra,
    )


def normalize(values):
    center = values - jnp.mean(values, axis=-1, keepdims=True)
    inverse = lax.rsqrt(jnp.mean(center * center, axis=-1, keepdims=True) + epsilon)
    return center * inverse, inverse


def grid_kernel(send_ref, feat_ref, wk_ref, wv_ref, norm_ref, kv_ref, out_ref):
    step = pl.program_id(0)
    unit, _ = normalize(feat_ref[...].astype(f32))
    rows = unit.astype(bf16)
    norm_ref[...] = rows
    weight = jnp.concatenate([wk_ref[...], wv_ref[...]], axis=0)
    both = dot(rows, weight, NT).astype(bf16)
    per = both.shape[0] // B
    for i in range(per):
        kv_ref[step * per + i] = both[i * B : (i + 1) * B]

    @pl.when(step == pl.num_programs(0) - 1)
    def _():
        for i in range(out_ref.shape[0]):
            out_ref[i] = kv_ref[send_ref[i]]


def grid_part(send, feat, wk, wv, shards):
    rows = feat.shape[0]
    steps = 4
    return pl.pallas_call(
        grid_kernel,
        grid=(steps,),
        out_shape=(
            struct((rows, C), bf16),
            struct((rows // B, B, 2 * D), bf16),
            struct((shards, B, 2 * D), bf16),
        ),
        in_specs=[
            SMEM,
            pl.BlockSpec((rows // steps, C), lambda i: (i, 0)),
            pl.BlockSpec((D, C), lambda i: (0, 0)),
            pl.BlockSpec((D, C), lambda i: (0, 0)),
        ],
        out_specs=(
            pl.BlockSpec((rows // steps, C), lambda i: (i, 0)),
            pl.BlockSpec((rows // B, B, 2 * D), lambda i: (0, 0, 0)),
            pl.BlockSpec((shards, B, 2 * D), lambda i: (0, 0, 0)),
        ),
        compiler_params=pltpu.CompilerParams(vmem_limit_bytes=60 << 20),
        cost_estimate=pl.CostEstimate(
            flops=1 << 28, bytes_accessed=6 << 20, transcendentals=0
        ),
        name="grid_part",
    )(send, feat, wk, wv)


def rows_kernel(wo_ref, wl_ref, cot_ref, out_ref):
    half = D // 2
    start = pl.multiple_of(lax.rem(lax.axis_index("grid"), 2) * half, half)
    out_ref[0:D] = wo_ref[...]
    out_ref[D : D + half] = wl_ref[pl.ds(start, half)]
    out_ref[D + half :] = cot_ref[...]


def query_kernel(mesh_ref, wq_ref, out_ref):
    for b in range(out_ref.shape[0]):
        unit, _ = normalize(mesh_ref[b * B : (b + 1) * B].astype(f32))
        rows = dot(wq_ref[...], unit.astype(bf16), NT).astype(bf16).astype(f32) * score_scale
        out_ref[b] = rows.astype(bf16)


def fill_pool(pool_ref, own_ref, arrived_ref):
    own = own_ref.shape[0]
    for i in range(own):
        pool_ref[i] = own_ref[i]
    for i in range(arrived_ref.shape[0]):
        pool_ref[own + i] = arrived_ref[i]


def folded(op, values):
    parts = [values[i * 8 : (i + 1) * 8] for i in range(values.shape[0] // 8)]
    while len(parts) > 1:
        parts = [
            op(parts[i], parts[i + 1]) if i + 1 < len(parts) else parts[i]
            for i in range(0, len(parts), 2)
        ]
    return parts[0]


def encoder_kernel(
    slot_ref, count_ref, bias_ref, own_ref, arrived_ref, query_ref,
    wide_ref, out_ref, lse_ref, pool_ref, score_ref,
):
    fill_pool(pool_ref, own_ref, arrived_ref)
    full = jnp.where(count_ref[0] == FULL, 0, 1)
    for m, total in ((full, FULL), (1 - full, REST)):
        stack = jnp.concatenate([query_ref[m], jnp.zeros((D, B), bf16)], axis=0)

        def scores(e, top, m=m, stack=stack):
            value = dot(pool_ref[slot_ref[m, e]], stack) + bias_ref[m, e]
            score_ref[e] = value
            return jnp.maximum(top, folded(jnp.maximum, value))

        top = lax.fori_loop(0, total, scores, jnp.full((8, B), -jnp.inf, f32), unroll=3)
        top = jnp.max(top, axis=0, keepdims=True)

        def mix(e, carry, m=m, top=top):
            low, acc = carry
            raised = jnp.exp(score_ref[e] - top)
            acc = acc + dot(pool_ref[slot_ref[m, e]], raised.astype(bf16), TN)
            return low + folded(jnp.add, raised), acc

        low, acc = lax.fori_loop(
            0, total, mix, (jnp.zeros((8, B), f32), jnp.zeros((2 * D, B), f32)), unroll=3
        )
        low = jnp.sum(low, axis=0, keepdims=True)
        rows = acc[D:] / low
        wide_ref[m] = rows
        out_ref[m] = rows.astype(bf16)
        lse_ref[m] = jnp.broadcast_to(top + jnp.log(low), (8, B))


def middle_kernel(
    at_ref, bias_ref, heads_ref, gathered_ref, mesh_ref, wq_ref, wk_ref, wv_ref, wl_ref,
    pack_ref, tail_ref, unit_ref, enc_ref,
):
    parts = heads_ref.shape[0]
    w_out = gathered_ref[:, 0:D, :].reshape(parts * D, C)
    w_layer = jnp.concatenate([wk_ref[...], wv_ref[...], wq_ref[...]], axis=0)
    half = parts // 2
    height = 2 * B // parts
    tail_ref[height:] = jnp.zeros((8, C), f32)
    queries, grads = [], []
    for b in range(2):
        rows = slice(b * B, (b + 1) * B)
        heads = heads_ref[:, b].reshape(parts * D, B)
        enc = mesh_ref[rows].astype(f32) + dot(heads, w_out, TN)
        enc_ref[rows] = enc
        unit, inverse = normalize(enc)
        unit = unit.astype(bf16)
        unit_ref[rows] = unit
        tail_ref[height:, b * B : (b + 1) * B] = jnp.broadcast_to(inverse, (B, 128)).T[0:8]
        both = dot(unit, w_layer, NT).astype(bf16)
        pack_ref[rows] = both[:, : 2 * D]
        queries.append((both[:, 2 * D :].astype(f32) * score_scale).astype(bf16))
        cot = gathered_ref[half * b : half * (b + 1), D + D // 2 :, :].reshape(B, C)
        grads.append(dot(cot, wl_ref[...], NT).astype(bf16))
    tail_ref[:height] = enc_ref[pl.ds(pl.multiple_of(at_ref[0] * height, height), height), :]
    pack_ref[2 * B : 3 * B] = jnp.concatenate(queries, axis=1)
    pack_ref[3 * B : 4 * B] = jnp.concatenate(grads, axis=1)
    row = lax.broadcasted_iota(jnp.int32, (8, 128), 0)
    table = jnp.zeros((8, 128), f32)
    for b in range(2):
        for n in range(3):
            table = jnp.where(row == 3 * b + n, bias_ref[b, n], table)
    high = table.astype(bf16).astype(f32)
    rest = table - high
    middle = rest.astype(bf16).astype(f32)
    tail = [high, middle, rest - middle, jnp.zeros((8, 128), f32)]
    pack_ref[4 * B : 4 * B + 32] = jnp.concatenate(tail, axis=0).astype(bf16)


def side_kernel(
    gathered_ref, unit_ref, tail_ref, wo_ref,
    cot_ref, unit_out_ref, inv_out_ref, sum_ref, half_ref, sem_ref,
):
    copy = pltpu.make_async_copy(gathered_ref.at[:, D : D + D // 2, :], half_ref, sem_ref)
    copy.start()
    half = gathered_ref.shape[0] // 2
    weight = wo_ref[...]
    for b in range(2):
        rows = slice(b * B, (b + 1) * B)
        cot = gathered_ref[half * b : half * (b + 1), D + D // 2 :, :].reshape(B, C)
        cot_ref[b] = dot(weight, cot, NT)
        unit_out_ref[b] = dot(weight, unit_ref[rows], NT)
        inv_out_ref[b] = tail_ref[tail_ref.shape[0] - 8 :, b * B : (b + 1) * B]
    sum_ref[...] = jnp.broadcast_to(
        jnp.sum(weight.astype(f32), axis=1, keepdims=True), sum_ref.shape
    )
    copy.wait()


def layer_kernel(
    own_ref, left_ref, right_ref, unit_ref, wq_ref, wk_ref, wv_ref, gathered_ref, send_ref
):
    zero = jnp.zeros((B, D), bf16)

    def block(ref, b):
        return ref[b * B : (b + 1) * B]

    def stacked(ref, b):
        lanes = slice(b * D, (b + 1) * D)
        query = ref[2 * B : 3 * B][:, lanes]
        grad = ref[3 * B : 4 * B][:, lanes]
        return jnp.concatenate(
            [jnp.concatenate([query, zero], axis=1), jnp.concatenate([zero, grad], axis=1)], axis=0
        )

    def table(ref):
        tail = ref[4 * B : 4 * B + 32].astype(f32)
        return tail[0:8] + tail[8:16] + tail[16:24]

    kv = [block(ref, b) for ref in (left_ref, own_ref, right_ref) for b in range(2)]
    own_bias = table(own_ref)
    queries = [(left_ref, 1, table(left_ref)), (own_ref, 0, own_bias), (own_ref, 1, own_bias)]
    queries.append((right_ref, 0, table(right_ref)))
    heads = []
    grad_kv = [jnp.zeros((B, 2 * D), f32), jnp.zeros((B, 2 * D), f32)]
    grad_q = []
    for j, (ref, b, bias) in enumerate(queries):
        pair = stacked(ref, b)
        window = kv[j : j + 3]
        both = [dot(rows, pair, NT) for rows in window]
        scores = [both[n][:, :B] + bias[3 * b + n : 3 * b + n + 1] for n in range(3)]
        top = folded(jnp.maximum, jnp.concatenate(scores, axis=0))
        top = jnp.max(top, axis=0, keepdims=True)
        raised = [jnp.exp(s - top) for s in scores]
        low = sum(folded(jnp.add, r) for r in raised)
        scale = 1.0 / jnp.sum(low, axis=0, keepdims=True)
        soft = [r * scale for r in raised]
        inner = sum(folded(jnp.add, soft[n] * both[n][:, B:]) for n in range(3))
        inner = jnp.sum(inner, axis=0, keepdims=True)
        mixed = [
            jnp.concatenate(
                [(soft[n] * (both[n][:, B:] - inner)).astype(bf16), soft[n].astype(bf16)], axis=1
            )
            for n in range(3)
        ]
        for n in range(3):
            own = j + n - 2
            if 0 <= own < 2:
                grad_kv[own] = grad_kv[own] + dot(mixed[n], pair)
        if 1 <= j <= 2:
            back = sum(dot(mixed[n], window[n], TN) for n in range(3))
            grad_q.append((back[:B, :D] * score_scale).astype(bf16))
            heads.append(back[B:, D:].astype(bf16))
    parts = gathered_ref.shape[0]
    w_layer = jnp.concatenate([wk_ref[...], wv_ref[...], wq_ref[...]], axis=0)
    totals, stats = [], jnp.zeros((8, 128), f32)
    lane = lax.broadcasted_iota(jnp.int32, (B, 128), 1)
    for b in range(2):
        grad = jnp.concatenate([grad_kv[b].astype(bf16), grad_q[b]], axis=1)
        total = dot(grad, w_layer)
        first = jnp.mean(total, axis=1, keepdims=True)
        second = jnp.mean(total * unit_ref[b * B : (b + 1) * B].astype(f32), axis=1, keepdims=True)
        first_high = first.astype(bf16).astype(f32)
        second_high = second.astype(bf16).astype(f32)
        columns = (first_high, second_high, first - first_high, second - second_high)
        table_b = jnp.zeros((B, 128), f32)
        for k, column in enumerate(columns):
            table_b = jnp.where(lane == 4 * b + k, column, table_b)
        stats = stats + table_b.T[0:8]
        totals.append(total.astype(bf16))
    stats = jnp.concatenate([stats[:, :D], stats[:, D:]], axis=0).astype(bf16)
    total = jnp.concatenate(totals, axis=0)
    heads = jnp.concatenate(heads, axis=0)
    share = heads.shape[0] // parts
    for z in range(parts):
        piece = dot(gathered_ref[z, 0:D, :], total, NT).astype(bf16)
        for b in range(2):
            send_ref[z, b * D : (b + 1) * D] = piece[:, b * B : (b + 1) * B]
        rows = heads[z * share : (z + 1) * share]
        send_ref[z, 2 * D :] = jnp.concatenate([rows, stats], axis=1)


def back_kernel(
    slot_ref, count_ref, bias_ref, me_ref, arrived_grad_ref, cot_ref, unit_ref, inv_ref, sum_ref,
    wide_ref, lse_ref, query_ref, own_ref, arrived_ref,
    own_out_ref, send_ref, pool_ref, grad_ref, pair_ref, inner_ref,
):
    fill_pool(pool_ref, own_ref, arrived_ref)
    zero = jnp.zeros((D, B), bf16)
    total = arrived_grad_ref[0].astype(f32)
    for z in range(1, arrived_grad_ref.shape[0]):
        total = total + arrived_grad_ref[z].astype(f32)
    stats = total[2 * D :, D:]
    stats = jnp.concatenate([stats[0:8], stats[8:16]], axis=1)
    for b in range(2):
        first = stats[4 * b : 4 * b + 1] + stats[4 * b + 2 : 4 * b + 3]
        second = stats[4 * b + 1 : 4 * b + 2] + stats[4 * b + 3 : 4 * b + 4]
        inside = total[b * D : (b + 1) * D] - first * sum_ref[...] - second * unit_ref[b]
        grad = (cot_ref[b] + inv_ref[b][0:1] * inside).astype(bf16)
        inner = jnp.sum(grad.astype(f32) * wide_ref[b], axis=0, keepdims=True)
        inner_ref[b] = jnp.broadcast_to(inner, (8, B))
        pair_ref[b] = jnp.concatenate(
            [
                jnp.concatenate([query_ref[b], zero], axis=1),
                jnp.concatenate([zero, grad], axis=1),
            ],
            axis=0,
        )
    own = own_ref.shape[0]
    grad_ref[own + me_ref[0]] = jnp.zeros((B, 2 * D), f32)
    full = jnp.where(count_ref[0] == FULL, 0, 1)
    for m, total in ((full, FULL), (1 - full, REST)):
        pair = pair_ref[m]
        lse = lse_ref[m][0:1]
        inner = inner_ref[m][0:1]

        def step(e, carry, m=m, pair=pair, lse=lse, inner=inner):
            slot = slot_ref[m, e]
            both = dot(pool_ref[slot], pair)
            soft = jnp.exp(both[:, :B] + (bias_ref[m, e] - lse))
            mixed = jnp.concatenate(
                [(soft * (both[:, B:] - inner)).astype(bf16), soft.astype(bf16)], axis=1
            )
            grad_ref[slot] = dot(mixed, pair, NT)
            return carry

        lax.fori_loop(0, total, step, 0, unroll=3)
    for i in range(own):
        own_out_ref[i] = grad_ref[i]
    for i in range(send_ref.shape[0]):
        send_ref[i] = grad_ref[own + i].astype(bf16)


def final_kernel(send_ref, norm_ref, own_ref, back_ref, out_ref, acc_ref):
    for i in range(own_ref.shape[0]):
        acc_ref[i] = own_ref[i]

    def add(i, carry):
        slot = send_ref[i]
        acc_ref[slot] = acc_ref[slot] + back_ref[i].astype(f32)
        return carry

    lax.fori_loop(0, back_ref.shape[0], add, 0, unroll=2)
    rows = acc_ref[...].reshape(norm_ref.shape[0], 2 * D).astype(bf16)
    shards, height = out_ref.shape[0], out_ref.shape[1]
    tile = 256
    for c in range(C // tile):
        part = dot(rows, norm_ref[:, c * tile : (c + 1) * tile], TN).T
        per = tile // height
        out_ref[c * per : (c + 1) * per] = part.astype(bf16).reshape(per, height, 2 * D)


def output_kernel(me_ref, heads_ref, mine_ref, other_ref, tail_ref, out_ref):
    total = tail_ref[: out_ref.shape[0]]
    even = lax.rem(me_ref[0], 2) == 0
    half = D // 2
    for h in range(heads_ref.shape[0]):
        rows = heads_ref[h, 2 * D :][:, :D]
        low = jnp.where(even, mine_ref[h], other_ref[h])
        high = jnp.where(even, other_ref[h], mine_ref[h])
        total = total + dot(rows[:, :half], low) + dot(rows[:, half:], high)
    out_ref[...] = total.astype(bf16)


def sum_kernel(parts_ref, key_ref, value_ref):
    total = parts_ref[0].astype(f32)
    for i in range(1, parts_ref.shape[0]):
        total = total + parts_ref[i].astype(f32)
    key_ref[...] = total[:, :D]
    value_ref[...] = total[:, D:]


def exchange(array, axis):
    return lax.all_to_all(array, axis, split_axis=0, concat_axis=0, tiled=True)


def on_device(
    grid_feat,
    mesh_feat,
    query_weight,
    key_weight,
    value_weight,
    enc_out_weight,
    layer_query,
    layer_key,
    layer_value,
    layer_out_weight,
    enc_bias,
    layer_bias,
    send_list,
    edge_slot,
    edge_count,
    cotangent,
):
    shards = lax.axis_size("grid")
    parts = lax.axis_size("head")
    own = grid_feat.shape[0] // B
    share = cotangent.shape[0]
    send = send_list[0]
    enc_table = enc_bias[:, :, 0]
    layer_table = layer_bias[:, :, 0]
    shard_at = lax.axis_index("grid").astype(jnp.int32)[None]
    head_at = lax.axis_index("head").astype(jnp.int32)[None]
    forward = [(i, (i + 1) % shards) for i in range(shards)]
    backward = [(t, s) for s, t in forward]

    half = D // 2
    shared_rows = call(
        rows_kernel, struct((D + half + share, C), bf16), [VMEM] * 3, name="rows_part", mib=61
    )(enc_out_weight, layer_out_weight, cotangent)
    gathered = lax.all_gather(shared_rows, "head", axis=0, tiled=False)
    query_weight, key_weight, value_weight, layer_query, layer_key, layer_value = (
        weight.T
        for weight in (query_weight, key_weight, value_weight, layer_query, layer_key, layer_value)
    )

    grid_norm, own_kv, outgoing = grid_part(send, grid_feat, key_weight, value_weight, shards)
    arrived_kv = exchange(outgoing, "grid")
    queries = call(
        query_kernel, struct((2, D, B), bf16), [VMEM] * 2, name="query_part", data=1 << 20
    )(mesh_feat, query_weight)
    wide_heads, enc_heads, lse = call(
        encoder_kernel,
        (struct((2, D, B), f32), struct((2, D, B), bf16), struct((2, 8, B), f32)),
        [SMEM] * 3 + [VMEM] * 3,
        [pltpu.VMEM((own + shards, B, 2 * D), bf16), pltpu.VMEM((FULL, B, B), f32)],
        name="encoder_part",
    )(edge_slot, edge_count, enc_table, own_kv, arrived_kv, queries)
    all_heads = lax.all_gather(enc_heads, "head", axis=0, tiled=False)
    pack, tail, unit = call(
        middle_kernel,
        (
            struct((4 * B + 32, 2 * D), bf16),
            struct((share + 8, C), f32),
            struct((2 * B, C), bf16),
        ),
        [SMEM] * 2 + [VMEM] * 7,
        [pltpu.VMEM((2 * B, C), f32)],
        name="middle_part",
    )(
        head_at, layer_table, all_heads, gathered, mesh_feat, layer_query, layer_key, layer_value, layer_out_weight
    )
    left = lax.ppermute(pack, "grid", forward)
    right = lax.ppermute(pack, "grid", backward)
    cot_part, unit_part, inverse_row, weight_sum, half_mine = call(
        side_kernel,
        (
            struct((2, D, B), f32),
            struct((2, D, B), f32),
            struct((2, 8, B), f32),
            struct((D, B), f32),
            struct((parts, half, C), bf16),
        ),
        [VMEM] * 4,
        [pltpu.SemaphoreType.DMA],
        out_specs=(VMEM, VMEM, VMEM, VMEM, HBM),
        name="side_part",
    )(gathered, unit, tail, enc_out_weight)
    mixed = call(
        layer_kernel, struct((parts, 2 * D + share, B), bf16), [VMEM] * 8, name="layer_part"
    )(pack, left, right, unit, layer_query, layer_key, layer_value, gathered)
    arrived_grad = exchange(mixed, "head")
    own_grad, send_grad = call(
        back_kernel,
        (struct((own, B, 2 * D), f32), struct((shards, B, 2 * D), bf16)),
        [SMEM] * 4 + [VMEM] * 10,
        [
            pltpu.VMEM((own + shards, B, 2 * D), bf16),
            pltpu.VMEM((own + shards, B, 2 * D), f32),
            pltpu.VMEM((2, 2 * D, 2 * B), bf16),
            pltpu.VMEM((2, 8, B), f32),
        ],
        name="back_part",
    )(
        edge_slot, edge_count, enc_table, shard_at, arrived_grad, cot_part, unit_part,
        inverse_row, weight_sum, wide_heads, lse, queries, own_kv, arrived_kv,
    )
    half_mine, _ = lax.optimization_barrier((half_mine, send_grad))
    half_other = lax.ppermute(half_mine, "grid", [(i, i ^ 1) for i in range(shards)])
    back_grad = exchange(send_grad, "grid")
    back_grad, half_other = lax.optimization_barrier((back_grad, half_other))
    product = call(
        final_kernel,
        struct((shards, C // shards, 2 * D), bf16),
        [SMEM] + [VMEM] * 3,
        [pltpu.VMEM((own, B, 2 * D), f32)],
        name="final_part",
    )(send, grid_norm, own_grad, back_grad)
    pieces = exchange(product, "grid")
    mesh_out = call(
        output_kernel,
        struct((share, C), bf16),
        [SMEM] + [VMEM] * 4,
        name="output_part",
    )(shard_at, arrived_grad, half_mine, half_other, tail)
    key_grad, value_grad = call(
        sum_kernel,
        (struct((C // shards, D), f32), struct((C // shards, D), f32)),
        [VMEM],
        name="sum_part",
    )(pieces)
    return mesh_out, key_grad, value_grad


def solution(mesh):
    in_specs = (
        P("grid", None),
        P("grid", None),
        P(None, "head"),
        P(None, "head"),
        P(None, "head"),
        P("head", None),
        P(None, "head"),
        P(None, "head"),
        P(None, "head"),
        P("head", None),
        P("grid", None, "head"),
        P("grid", None, "head"),
        P("grid", None),
        P("grid", None),
        P("grid"),
        P(("grid", "head"), None),
    )
    out_specs = (P(("grid", "head"), None), P("grid", "head"), P("grid", "head"))
    return jax.shard_map(
        on_device, mesh=mesh, in_specs=in_specs, out_specs=out_specs, check_vma=False
    )
```

```python
import jax
import jax.numpy as jnp
from jax import lax
from jax.experimental import pallas as pl
from jax.experimental.pallas import tpu as pltpu
from jax.sharding import PartitionSpec as P

D = 64
B = 128
C = 1024
FULL = 30
REST = 9
epsilon = 1e-05
score_scale = 0.125

f32 = jnp.float32
bf16 = jnp.bfloat16

NN = (((1,), (0,)), ((), ()))
NT = (((1,), (1,)), ((), ()))
TN = (((0,), (0,)), ((), ()))

VMEM = pl.BlockSpec(memory_space=pltpu.VMEM)
SMEM = pl.BlockSpec(memory_space=pltpu.SMEM)
HBM = pl.BlockSpec(memory_space=pltpu.HBM)


def dot(left, right, dims=NN):
    return lax.dot_general(left, right, dims, preferred_element_type=f32)


def struct(shape, dtype):
    return jax.ShapeDtypeStruct(shape, dtype)


def call(body, outs, specs, scratch=(), mib=16, flops=1 << 26, data=1 << 22, name=None, **extra):
    return pl.pallas_call(
        body,
        out_shape=outs,
        in_specs=specs,
        scratch_shapes=list(scratch),
        compiler_params=pltpu.CompilerParams(vmem_limit_bytes=mib << 20),
        cost_estimate=pl.CostEstimate(flops=flops, bytes_accessed=data, transcendentals=0),
        name=name,
        **extra,
    )


def normalize(values):
    center = values - jnp.mean(values, axis=-1, keepdims=True)
    inverse = lax.rsqrt(jnp.mean(center * center, axis=-1, keepdims=True) + epsilon)
    return center * inverse, inverse


def grid_kernel(send_ref, feat_ref, wk_ref, wv_ref, norm_ref, kv_ref, out_ref):
    step = pl.program_id(0)
    unit, _ = normalize(feat_ref[...].astype(f32))
    rows = unit.astype(bf16)
    norm_ref[...] = rows
    weight = jnp.concatenate([wk_ref[...], wv_ref[...]], axis=0)
    both = dot(rows, weight, NT).astype(bf16)
    per = both.shape[0] // B
    for i in range(per):
        kv_ref[step * per + i] = both[i * B : (i + 1) * B]

    @pl.when(step == pl.num_programs(0) - 1)
    def _():
        for i in range(out_ref.shape[0]):
            out_ref[i] = kv_ref[send_ref[i]]


def grid_part(send, feat, wk, wv, shards):
    rows = feat.shape[0]
    steps = 4
    return pl.pallas_call(
        grid_kernel,
        grid=(steps,),
        out_shape=(
            struct((rows, C), bf16),
            struct((rows // B, B, 2 * D), bf16),
            struct((shards, B, 2 * D), bf16),
        ),
        in_specs=[
            SMEM,
            pl.BlockSpec((rows // steps, C), lambda i: (i, 0)),
            pl.BlockSpec((D, C), lambda i: (0, 0)),
            pl.BlockSpec((D, C), lambda i: (0, 0)),
        ],
        out_specs=(
            pl.BlockSpec((rows // steps, C), lambda i: (i, 0)),
            pl.BlockSpec((rows // B, B, 2 * D), lambda i: (0, 0, 0)),
            pl.BlockSpec((shards, B, 2 * D), lambda i: (0, 0, 0)),
        ),
        compiler_params=pltpu.CompilerParams(vmem_limit_bytes=60 << 20),
        cost_estimate=pl.CostEstimate(
            flops=1 << 28, bytes_accessed=6 << 20, transcendentals=0
        ),
        name="grid_part",
    )(send, feat, wk, wv)


def rows_kernel(wo_ref, wl_ref, cot_ref, out_ref):
    half = D // 2
    start = pl.multiple_of(lax.rem(lax.axis_index("grid"), 2) * half, half)
    out_ref[0:D] = wo_ref[...]
    out_ref[D : D + half] = wl_ref[pl.ds(start, half)]
    out_ref[D + half :] = cot_ref[...]


def query_kernel(mesh_ref, wq_ref, out_ref):
    for b in range(out_ref.shape[0]):
        unit, _ = normalize(mesh_ref[b * B : (b + 1) * B].astype(f32))
        rows = dot(wq_ref[...], unit.astype(bf16), NT).astype(bf16).astype(f32) * score_scale
        out_ref[b] = rows.astype(bf16)


def fill_pool(pool_ref, own_ref, arrived_ref):
    own = own_ref.shape[0]
    for i in range(own):
        pool_ref[i] = own_ref[i]
    for i in range(arrived_ref.shape[0]):
        pool_ref[own + i] = arrived_ref[i]


def folded(op, values):
    parts = [values[i * 8 : (i + 1) * 8] for i in range(values.shape[0] // 8)]
    while len(parts) > 1:
        parts = [
            op(parts[i], parts[i + 1]) if i + 1 < len(parts) else parts[i]
            for i in range(0, len(parts), 2)
        ]
    return parts[0]


def fill_tables(slot_ref, bias_ref, full, reader_ref, edge_ref):
    for i in range(reader_ref.shape[0]):
        reader_ref[i] = 0
        edge_ref[i] = 0.0
    for m, total in ((full, FULL), (1 - full, REST)):

        def put(e, carry, m=m):
            slot = slot_ref[m, e]
            reader_ref[slot] = m
            edge_ref[slot] = bias_ref[m, e]
            return carry

        lax.fori_loop(0, total, put, 0, unroll=3)


def encoder_kernel(
    slot_ref, count_ref, bias_ref, me_ref, own_ref, arrived_ref, query_ref,
    out_ref, lse_ref, early_ref, pool_ref, score_ref, reader_ref, edge_ref,
):
    fill_pool(pool_ref, own_ref, arrived_ref)
    full = jnp.where(count_ref[0] == FULL, 0, 1)
    fill_tables(slot_ref, bias_ref, full, reader_ref, edge_ref)
    for m, total in ((full, FULL), (1 - full, REST)):
        stack = jnp.concatenate([query_ref[m], jnp.zeros((D, B), bf16)], axis=0)

        def scores(e, top, m=m, stack=stack):
            value = dot(pool_ref[slot_ref[m, e]], stack) + bias_ref[m, e]
            score_ref[e] = value
            return jnp.maximum(top, folded(jnp.maximum, value))

        top = lax.fori_loop(0, total, scores, jnp.full((8, B), -jnp.inf, f32), unroll=3)
        top = jnp.max(top, axis=0, keepdims=True)

        def mix(e, carry, m=m, top=top):
            low, acc = carry
            raised = jnp.exp(score_ref[e] - top)
            acc = acc + dot(pool_ref[slot_ref[m, e]], raised.astype(bf16), TN)
            return low + folded(jnp.add, raised), acc

        low, acc = lax.fori_loop(
            0, total, mix, (jnp.zeros((8, B), f32), jnp.zeros((2 * D, B), f32)), unroll=3
        )
        low = jnp.sum(low, axis=0, keepdims=True)
        out_ref[m] = (acc[D:] / low).astype(bf16)
        lse_ref[m] = jnp.broadcast_to(top + jnp.log(low), (8, B))
    own = own_ref.shape[0]
    row = lax.broadcasted_iota(jnp.int32, (16, B), 0)
    for p in range(early_ref.shape[0]):
        m = reader_ref[own + p]
        other = me_ref[0] != p
        early_ref[p, 0:D] = jnp.where(other, query_ref[m], jnp.zeros((D, B), bf16))
        early_ref[p, D : 2 * D] = jnp.where(other, out_ref[m], jnp.zeros((D, B), bf16))
        shift = jnp.concatenate([lse_ref[m], lse_ref[m]], axis=0) - edge_ref[own + p]
        shift = jnp.where(other, shift, 0.0)
        high = shift.astype(bf16).astype(f32)
        middle = (shift - high).astype(bf16).astype(f32)
        rest = shift - high - middle
        tail = jnp.where(row == 0, high, jnp.where(row == 1, middle, jnp.where(row == 2, rest, 0.0)))
        early_ref[p, 2 * D :] = tail.astype(bf16)


def middle_kernel(
    at_ref, bias_ref, heads_ref, gathered_ref, mesh_ref, wq_ref, wk_ref, wv_ref, wl_ref,
    pack_ref, tail_ref, unit_ref, enc_ref,
):
    parts = heads_ref.shape[0]
    w_out = gathered_ref[:, 0:D, :].reshape(parts * D, C)
    w_layer = jnp.concatenate([wk_ref[...], wv_ref[...], wq_ref[...]], axis=0)
    half = parts // 2
    height = 2 * B // parts
    tail_ref[height:] = jnp.zeros((8, C), f32)
    queries, grads = [], []
    for b in range(2):
        rows = slice(b * B, (b + 1) * B)
        heads = heads_ref[:, b].reshape(parts * D, B)
        enc = mesh_ref[rows].astype(f32) + dot(heads, w_out, TN)
        enc_ref[rows] = enc
        unit, inverse = normalize(enc)
        unit = unit.astype(bf16)
        unit_ref[rows] = unit
        tail_ref[height:, b * B : (b + 1) * B] = jnp.broadcast_to(inverse, (B, 128)).T[0:8]
        both = dot(unit, w_layer, NT).astype(bf16)
        pack_ref[rows] = both[:, : 2 * D]
        queries.append((both[:, 2 * D :].astype(f32) * score_scale).astype(bf16))
        cot = gathered_ref[half * b : half * (b + 1), D + D // 2 :, :].reshape(B, C)
        grads.append(dot(cot, wl_ref[...], NT).astype(bf16))
    tail_ref[:height] = enc_ref[pl.ds(pl.multiple_of(at_ref[0] * height, height), height), :]
    pack_ref[2 * B : 3 * B] = jnp.concatenate(queries, axis=1)
    pack_ref[3 * B : 4 * B] = jnp.concatenate(grads, axis=1)
    row = lax.broadcasted_iota(jnp.int32, (8, 128), 0)
    table = jnp.zeros((8, 128), f32)
    for b in range(2):
        for n in range(3):
            table = jnp.where(row == 3 * b + n, bias_ref[b, n], table)
    high = table.astype(bf16).astype(f32)
    rest = table - high
    middle = rest.astype(bf16).astype(f32)
    tail = [high, middle, rest - middle, jnp.zeros((8, 128), f32)]
    pack_ref[4 * B : 4 * B + 32] = jnp.concatenate(tail, axis=0).astype(bf16)


def side_kernel(
    gathered_ref, unit_ref, tail_ref, wo_ref,
    cot_ref, unit_out_ref, inv_out_ref, sum_ref, half_ref, sem_ref,
):
    copy = pltpu.make_async_copy(gathered_ref.at[:, D : D + D // 2, :], half_ref, sem_ref)
    copy.start()
    half = gathered_ref.shape[0] // 2
    weight = wo_ref[...]
    for b in range(2):
        rows = slice(b * B, (b + 1) * B)
        cot = gathered_ref[half * b : half * (b + 1), D + D // 2 :, :].reshape(B, C)
        cot_ref[b] = dot(weight, cot, NT)
        unit_out_ref[b] = dot(weight, unit_ref[rows], NT)
        inv_out_ref[b] = tail_ref[tail_ref.shape[0] - 8 :, b * B : (b + 1) * B]
    sum_ref[...] = jnp.broadcast_to(
        jnp.sum(weight.astype(f32), axis=1, keepdims=True), sum_ref.shape
    )
    copy.wait()


def layer_kernel(
    own_ref, left_ref, right_ref, unit_ref, wq_ref, wk_ref, wv_ref, gathered_ref, send_ref
):
    zero = jnp.zeros((B, D), bf16)

    def block(ref, b):
        return ref[b * B : (b + 1) * B]

    def stacked(ref, b):
        lanes = slice(b * D, (b + 1) * D)
        query = ref[2 * B : 3 * B][:, lanes]
        grad = ref[3 * B : 4 * B][:, lanes]
        return jnp.concatenate(
            [jnp.concatenate([query, zero], axis=1), jnp.concatenate([zero, grad], axis=1)], axis=0
        )

    def table(ref):
        tail = ref[4 * B : 4 * B + 32].astype(f32)
        return tail[0:8] + tail[8:16] + tail[16:24]

    kv = [block(ref, b) for ref in (left_ref, own_ref, right_ref) for b in range(2)]
    own_bias = table(own_ref)
    queries = [(left_ref, 1, table(left_ref)), (own_ref, 0, own_bias), (own_ref, 1, own_bias)]
    queries.append((right_ref, 0, table(right_ref)))
    heads = []
    grad_kv = [jnp.zeros((B, 2 * D), f32), jnp.zeros((B, 2 * D), f32)]
    grad_q = []
    for j, (ref, b, bias) in enumerate(queries):
        pair = stacked(ref, b)
        window = kv[j : j + 3]
        both = [dot(rows, pair, NT) for rows in window]
        scores = [both[n][:, :B] + bias[3 * b + n : 3 * b + n + 1] for n in range(3)]
        top = folded(jnp.maximum, jnp.concatenate(scores, axis=0))
        top = jnp.max(top, axis=0, keepdims=True)
        raised = [jnp.exp(s - top) for s in scores]
        low = sum(folded(jnp.add, r) for r in raised)
        scale = 1.0 / jnp.sum(low, axis=0, keepdims=True)
        soft = [r * scale for r in raised]
        inner = sum(folded(jnp.add, soft[n] * both[n][:, B:]) for n in range(3))
        inner = jnp.sum(inner, axis=0, keepdims=True)
        mixed = [
            jnp.concatenate(
                [(soft[n] * (both[n][:, B:] - inner)).astype(bf16), soft[n].astype(bf16)], axis=1
            )
            for n in range(3)
        ]
        for n in range(3):
            own = j + n - 2
            if 0 <= own < 2:
                grad_kv[own] = grad_kv[own] + dot(mixed[n], pair)
        if 1 <= j <= 2:
            back = sum(dot(mixed[n], window[n], TN) for n in range(3))
            grad_q.append((back[:B, :D] * score_scale).astype(bf16))
            heads.append(back[B:, D:].astype(bf16))
    parts = gathered_ref.shape[0]
    w_layer = jnp.concatenate([wk_ref[...], wv_ref[...], wq_ref[...]], axis=0)
    totals, stats = [], jnp.zeros((8, 128), f32)
    lane = lax.broadcasted_iota(jnp.int32, (B, 128), 1)
    for b in range(2):
        grad = jnp.concatenate([grad_kv[b].astype(bf16), grad_q[b]], axis=1)
        total = dot(grad, w_layer)
        first = jnp.mean(total, axis=1, keepdims=True)
        second = jnp.mean(total * unit_ref[b * B : (b + 1) * B].astype(f32), axis=1, keepdims=True)
        first_high = first.astype(bf16).astype(f32)
        second_high = second.astype(bf16).astype(f32)
        columns = (first_high, second_high, first - first_high, second - second_high)
        table_b = jnp.zeros((B, 128), f32)
        for k, column in enumerate(columns):
            table_b = jnp.where(lane == 4 * b + k, column, table_b)
        stats = stats + table_b.T[0:8]
        totals.append(total.astype(bf16))
    stats = jnp.concatenate([stats[:, :D], stats[:, D:]], axis=0).astype(bf16)
    total = jnp.concatenate(totals, axis=0)
    heads = jnp.concatenate(heads, axis=0)
    share = heads.shape[0] // parts
    for z in range(parts):
        piece = dot(gathered_ref[z, 0:D, :], total, NT).astype(bf16)
        for b in range(2):
            send_ref[z, b * D : (b + 1) * D] = piece[:, b * B : (b + 1) * B]
        rows = heads[z * share : (z + 1) * share]
        send_ref[z, 2 * D :] = jnp.concatenate([rows, stats], axis=1)


def grad_kernel(
    slot_ref, count_ref, bias_ref, me_ref, arrived_ref, cot_ref, unit_ref, inv_ref, sum_ref,
    grad_ref, send_ref, reader_ref, edge_ref,
):
    full = jnp.where(count_ref[0] == FULL, 0, 1)
    fill_tables(slot_ref, bias_ref, full, reader_ref, edge_ref)
    total = arrived_ref[0].astype(f32)
    for z in range(1, arrived_ref.shape[0]):
        total = total + arrived_ref[z].astype(f32)
    stats = total[2 * D :, D:]
    stats = jnp.concatenate([stats[0:8], stats[8:16]], axis=1)
    for b in range(2):
        first = stats[4 * b : 4 * b + 1] + stats[4 * b + 2 : 4 * b + 3]
        second = stats[4 * b + 1 : 4 * b + 2] + stats[4 * b + 3 : 4 * b + 4]
        inside = total[b * D : (b + 1) * D] - first * sum_ref[...] - second * unit_ref[b]
        grad_ref[b] = (cot_ref[b] + inv_ref[b][0:1] * inside).astype(bf16)
    shards = send_ref.shape[0]
    own = reader_ref.shape[0] - shards
    for p in range(shards):
        block = grad_ref[reader_ref[own + p]]
        send_ref[p] = jnp.where(me_ref[0] != p, block, jnp.zeros((D, B), bf16))


def final_kernel(
    send_ref, slot_ref, count_ref, bias_ref, norm_ref, kv_ref, early_ref, grads_ref,
    query_ref, heads_ref, lse_ref, grad_ref, out_ref, acc_ref, reader_ref, edge_ref,
    held_ref, sem_ref,
):
    copy = pltpu.make_async_copy(norm_ref, held_ref, sem_ref)
    copy.start()
    full = jnp.where(count_ref[0] == FULL, 0, 1)
    fill_tables(slot_ref, bias_ref, full, reader_ref, edge_ref)
    zero = jnp.zeros((D, B), bf16)

    def back(keys, query, heads, shift, grad):
        inner = jnp.sum(grad.astype(f32) * heads.astype(f32), axis=0, keepdims=True)
        pair = jnp.concatenate(
            [jnp.concatenate([query, zero], axis=1), jnp.concatenate([zero, grad], axis=1)], axis=0
        )
        both = dot(keys, pair)
        soft = jnp.exp(both[:, :B] - shift)
        mixed = jnp.concatenate(
            [(soft * (both[:, B:] - inner)).astype(bf16), soft.astype(bf16)], axis=1
        )
        return dot(mixed, pair, NT)

    def own_step(v, carry):
        m = reader_ref[v]
        shift = lse_ref[m][0:1] - edge_ref[v]
        acc_ref[v] = back(kv_ref[v], query_ref[m], heads_ref[m], shift, grad_ref[m])
        return carry

    lax.fori_loop(0, kv_ref.shape[0], own_step, 0, unroll=4)

    def sent_step(r, carry):
        slot = send_ref[r]
        block = early_ref[r]
        tail = block[2 * D :].astype(f32)
        shift = tail[0:1] + tail[1:2] + tail[2:3]
        part = back(kv_ref[slot], block[:D], block[D : 2 * D], shift, grads_ref[r])
        acc_ref[slot] = acc_ref[slot] + part
        return carry

    lax.fori_loop(0, early_ref.shape[0], sent_step, 0, unroll=4)
    rows = acc_ref[...].reshape(norm_ref.shape[0], 2 * D).astype(bf16)
    copy.wait()
    shards, height = out_ref.shape[0], out_ref.shape[1]
    tile = 256
    for c in range(C // tile):
        part = dot(rows, held_ref[:, c * tile : (c + 1) * tile], TN).T
        per = tile // height
        out_ref[c * per : (c + 1) * per] = part.astype(bf16).reshape(per, height, 2 * D)


def output_kernel(me_ref, heads_ref, mine_ref, other_ref, tail_ref, out_ref):
    total = tail_ref[: out_ref.shape[0]]
    even = lax.rem(me_ref[0], 2) == 0
    half = D // 2
    for h in range(heads_ref.shape[0]):
        rows = heads_ref[h, 2 * D :][:, :D]
        low = jnp.where(even, mine_ref[h], other_ref[h])
        high = jnp.where(even, other_ref[h], mine_ref[h])
        total = total + dot(rows[:, :half], low) + dot(rows[:, half:], high)
    out_ref[...] = total.astype(bf16)


def sum_kernel(parts_ref, key_ref, value_ref):
    total = parts_ref[0].astype(f32)
    for i in range(1, parts_ref.shape[0]):
        total = total + parts_ref[i].astype(f32)
    key_ref[...] = total[:, :D]
    value_ref[...] = total[:, D:]


def exchange(array, axis):
    return lax.all_to_all(array, axis, split_axis=0, concat_axis=0, tiled=True)


def on_device(
    grid_feat,
    mesh_feat,
    query_weight,
    key_weight,
    value_weight,
    enc_out_weight,
    layer_query,
    layer_key,
    layer_value,
    layer_out_weight,
    enc_bias,
    layer_bias,
    send_list,
    edge_slot,
    edge_count,
    cotangent,
):
    shards = lax.axis_size("grid")
    parts = lax.axis_size("head")
    own = grid_feat.shape[0] // B
    share = cotangent.shape[0]
    send = send_list[0]
    enc_table = enc_bias[:, :, 0]
    layer_table = layer_bias[:, :, 0]
    shard_at = lax.axis_index("grid").astype(jnp.int32)[None]
    head_at = lax.axis_index("head").astype(jnp.int32)[None]
    forward = [(i, (i + 1) % shards) for i in range(shards)]
    backward = [(t, s) for s, t in forward]

    half = D // 2
    shared_rows = call(
        rows_kernel, struct((D + half + share, C), bf16), [VMEM] * 3, name="rows_part", mib=61
    )(enc_out_weight, layer_out_weight, cotangent)
    gathered = lax.all_gather(shared_rows, "head", axis=0, tiled=False)
    query_weight, key_weight, value_weight, layer_query, layer_key, layer_value = (
        weight.T
        for weight in (query_weight, key_weight, value_weight, layer_query, layer_key, layer_value)
    )

    grid_norm, own_kv, outgoing = grid_part(send, grid_feat, key_weight, value_weight, shards)
    arrived_kv = exchange(outgoing, "grid")
    queries = call(
        query_kernel, struct((2, D, B), bf16), [VMEM] * 2, name="query_part", data=1 << 20
    )(mesh_feat, query_weight)
    tables = [pltpu.SMEM((own + shards,), jnp.int32), pltpu.SMEM((own + shards,), f32)]
    enc_heads, lse, early = call(
        encoder_kernel,
        (
            struct((2, D, B), bf16),
            struct((2, 8, B), f32),
            struct((shards, 2 * D + 16, B), bf16),
        ),
        [SMEM] * 4 + [VMEM] * 3,
        [pltpu.VMEM((own + shards, B, 2 * D), bf16), pltpu.VMEM((FULL, B, B), f32)] + tables,
        name="encoder_part",
    )(edge_slot, edge_count, enc_table, shard_at, own_kv, arrived_kv, queries)
    arrived_early = exchange(early, "grid")
    all_heads = lax.all_gather(enc_heads, "head", axis=0, tiled=False)
    pack, tail, unit = call(
        middle_kernel,
        (
            struct((4 * B + 32, 2 * D), bf16),
            struct((share + 8, C), f32),
            struct((2 * B, C), bf16),
        ),
        [SMEM] * 2 + [VMEM] * 7,
        [pltpu.VMEM((2 * B, C), f32)],
        name="middle_part",
    )(
        head_at, layer_table, all_heads, gathered, mesh_feat, layer_query, layer_key, layer_value, layer_out_weight
    )
    left = lax.ppermute(pack, "grid", forward)
    right = lax.ppermute(pack, "grid", backward)
    cot_part, unit_part, inverse_row, weight_sum, half_mine = call(
        side_kernel,
        (
            struct((2, D, B), f32),
            struct((2, D, B), f32),
            struct((2, 8, B), f32),
            struct((D, B), f32),
            struct((parts, half, C), bf16),
        ),
        [VMEM] * 4,
        [pltpu.SemaphoreType.DMA],
        out_specs=(VMEM, VMEM, VMEM, VMEM, HBM),
        name="side_part",
    )(gathered, unit, tail, enc_out_weight)
    mixed = call(
        layer_kernel, struct((parts, 2 * D + share, B), bf16), [VMEM] * 8, name="layer_part"
    )(pack, left, right, unit, layer_query, layer_key, layer_value, gathered)
    arrived_early, mixed = lax.optimization_barrier((arrived_early, mixed))
    arrived_grad = exchange(mixed, "head")
    grads, send_grads = call(
        grad_kernel,
        (struct((2, D, B), bf16), struct((shards, D, B), bf16)),
        [SMEM] * 4 + [VMEM] * 5,
        tables,
        name="grad_part",
    )(
        edge_slot, edge_count, enc_table, shard_at, arrived_grad, cot_part, unit_part,
        inverse_row, weight_sum,
    )
    arrived_grads = exchange(send_grads, "grid")
    half_other = lax.ppermute(half_mine, "grid", [(i, i ^ 1) for i in range(shards)])
    product = call(
        final_kernel,
        struct((shards, C // shards, 2 * D), bf16),
        [SMEM] * 4 + [HBM] + [VMEM] * 7,
        [pltpu.VMEM((own, B, 2 * D), f32)]
        + tables
        + [pltpu.VMEM(grid_norm.shape, bf16), pltpu.SemaphoreType.DMA],
        name="final_part",
        mib=61,
    )(
        send, edge_slot, edge_count, enc_table, grid_norm, own_kv, arrived_early, arrived_grads,
        queries, enc_heads, lse, grads,
    )
    pieces = exchange(product, "grid")
    mesh_out = call(
        output_kernel,
        struct((share, C), bf16),
        [SMEM] + [VMEM] * 4,
        name="output_part",
    )(shard_at, arrived_grad, half_mine, half_other, tail)
    key_grad, value_grad = call(
        sum_kernel,
        (struct((C // shards, D), f32), struct((C // shards, D), f32)),
        [VMEM],
        name="sum_part",
    )(pieces)
    return mesh_out, key_grad, value_grad


def solution(mesh):
    in_specs = (
        P("grid", None),
        P("grid", None),
        P(None, "head"),
        P(None, "head"),
        P(None, "head"),
        P("head", None),
        P(None, "head"),
        P(None, "head"),
        P(None, "head"),
        P("head", None),
        P("grid", None, "head"),
        P("grid", None, "head"),
        P("grid", None),
        P("grid", None),
        P("grid"),
        P(("grid", "head"), None),
    )
    out_specs = (P(("grid", "head"), None), P("grid", "head"), P("grid", "head"))
    return jax.shard_map(
        on_device, mesh=mesh, in_specs=in_specs, out_specs=out_specs, check_vma=False
    )
```

```python
import jax
import jax.numpy as jnp
from jax import lax
from jax.experimental import pallas as pl
from jax.experimental.pallas import tpu as pltpu
from jax.sharding import PartitionSpec as P

D = 64
B = 128
C = 1024
FULL = 30
REST = 9
epsilon = 1e-05
score_scale = 0.125

f32 = jnp.float32
bf16 = jnp.bfloat16

NN = (((1,), (0,)), ((), ()))
NT = (((1,), (1,)), ((), ()))
TN = (((0,), (0,)), ((), ()))

VMEM = pl.BlockSpec(memory_space=pltpu.VMEM)
SMEM = pl.BlockSpec(memory_space=pltpu.SMEM)
HBM = pl.BlockSpec(memory_space=pltpu.HBM)


def dot(left, right, dims=NN):
    return lax.dot_general(left, right, dims, preferred_element_type=f32)


def struct(shape, dtype):
    return jax.ShapeDtypeStruct(shape, dtype)


def call(body, outs, specs, scratch=(), mib=16, flops=1 << 26, data=1 << 22, name=None, **extra):
    return pl.pallas_call(
        body,
        out_shape=outs,
        in_specs=specs,
        scratch_shapes=list(scratch),
        compiler_params=pltpu.CompilerParams(vmem_limit_bytes=mib << 20),
        cost_estimate=pl.CostEstimate(flops=flops, bytes_accessed=data, transcendentals=0),
        name=name,
        **extra,
    )


def normalize(values):
    center = values - jnp.mean(values, axis=-1, keepdims=True)
    inverse = lax.rsqrt(jnp.mean(center * center, axis=-1, keepdims=True) + epsilon)
    return center * inverse, inverse


def grid_kernel(send_ref, feat_ref, wk_ref, wv_ref, norm_ref, kv_ref, out_ref):
    step = pl.program_id(0)
    unit, _ = normalize(feat_ref[...].astype(f32))
    rows = unit.astype(bf16)
    norm_ref[...] = rows
    weight = jnp.concatenate([wk_ref[...], wv_ref[...]], axis=0)
    both = dot(rows, weight, NT).astype(bf16)
    per = both.shape[0] // B
    for i in range(per):
        kv_ref[step * per + i] = both[i * B : (i + 1) * B]

    @pl.when(step == pl.num_programs(0) - 1)
    def _():
        for i in range(out_ref.shape[0]):
            out_ref[i] = kv_ref[send_ref[i]]


def grid_part(send, feat, wk, wv, shards):
    rows = feat.shape[0]
    steps = 4
    return pl.pallas_call(
        grid_kernel,
        grid=(steps,),
        out_shape=(
            struct((rows, C), bf16),
            struct((rows // B, B, 2 * D), bf16),
            struct((shards, B, 2 * D), bf16),
        ),
        in_specs=[
            SMEM,
            pl.BlockSpec((rows // steps, C), lambda i: (i, 0)),
            pl.BlockSpec((D, C), lambda i: (0, 0)),
            pl.BlockSpec((D, C), lambda i: (0, 0)),
        ],
        out_specs=(
            pl.BlockSpec((rows // steps, C), lambda i: (i, 0)),
            pl.BlockSpec((rows // B, B, 2 * D), lambda i: (0, 0, 0)),
            pl.BlockSpec((shards, B, 2 * D), lambda i: (0, 0, 0)),
        ),
        compiler_params=pltpu.CompilerParams(vmem_limit_bytes=60 << 20),
        cost_estimate=pl.CostEstimate(
            flops=1 << 28, bytes_accessed=6 << 20, transcendentals=0
        ),
        name="grid_part",
    )(send, feat, wk, wv)


def rows_kernel(wo_ref, wl_ref, cot_ref, out_ref):
    half = D // 2
    start = pl.multiple_of(lax.rem(lax.axis_index("grid"), 2) * half, half)
    out_ref[0:D] = wo_ref[...]
    out_ref[D : D + half] = wl_ref[pl.ds(start, half)]
    out_ref[D + half :] = cot_ref[...]


def query_kernel(mesh_ref, wq_ref, out_ref):
    for b in range(out_ref.shape[0]):
        unit, _ = normalize(mesh_ref[b * B : (b + 1) * B].astype(f32))
        rows = dot(wq_ref[...], unit.astype(bf16), NT).astype(bf16).astype(f32) * score_scale
        out_ref[b] = rows.astype(bf16)


def fill_pool(pool_ref, own_ref, arrived_ref):
    own = own_ref.shape[0]
    for i in range(own):
        pool_ref[i] = own_ref[i]
    for i in range(arrived_ref.shape[0]):
        pool_ref[own + i] = arrived_ref[i]


def folded(op, values):
    parts = [values[i * 8 : (i + 1) * 8] for i in range(values.shape[0] // 8)]
    while len(parts) > 1:
        parts = [
            op(parts[i], parts[i + 1]) if i + 1 < len(parts) else parts[i]
            for i in range(0, len(parts), 2)
        ]
    return parts[0]


def fill_tables(slot_ref, bias_ref, full, reader_ref, edge_ref):
    for i in range(reader_ref.shape[0]):
        reader_ref[i] = 0
        edge_ref[i] = 0.0
    for m, total in ((full, FULL), (1 - full, REST)):

        def put(e, carry, m=m):
            slot = slot_ref[m, e]
            reader_ref[slot] = m
            edge_ref[slot] = bias_ref[m, e]
            return carry

        lax.fori_loop(0, total, put, 0, unroll=3)


def encoder_kernel(
    slot_ref, count_ref, bias_ref, me_ref, own_ref, arrived_ref, query_ref,
    out_ref, lse_ref, early_ref, pool_ref, score_ref, reader_ref, edge_ref,
):
    fill_pool(pool_ref, own_ref, arrived_ref)
    full = jnp.where(count_ref[0] == FULL, 0, 1)
    fill_tables(slot_ref, bias_ref, full, reader_ref, edge_ref)
    for m, total in ((full, FULL), (1 - full, REST)):
        stack = jnp.concatenate([query_ref[m], jnp.zeros((D, B), bf16)], axis=0)

        def scores(e, top, m=m, stack=stack):
            value = dot(pool_ref[slot_ref[m, e]], stack) + bias_ref[m, e]
            score_ref[e] = value
            return jnp.maximum(top, folded(jnp.maximum, value))

        top = lax.fori_loop(0, total, scores, jnp.full((8, B), -jnp.inf, f32), unroll=3)
        top = jnp.max(top, axis=0, keepdims=True)

        def mix(e, carry, m=m, top=top):
            low, acc = carry
            raised = jnp.exp(score_ref[e] - top)
            acc = acc + dot(pool_ref[slot_ref[m, e]], raised.astype(bf16), TN)
            return low + folded(jnp.add, raised), acc

        low, acc = lax.fori_loop(
            0, total, mix, (jnp.zeros((8, B), f32), jnp.zeros((2 * D, B), f32)), unroll=3
        )
        low = jnp.sum(low, axis=0, keepdims=True)
        out_ref[m] = (acc[D:] / low).astype(bf16)
        lse_ref[m] = jnp.broadcast_to(top + jnp.log(low), (8, B))
    own = own_ref.shape[0]
    row = lax.broadcasted_iota(jnp.int32, (16, B), 0)
    for p in range(early_ref.shape[0]):
        m = reader_ref[own + p]
        other = me_ref[0] != p
        early_ref[p, 0:D] = jnp.where(other, query_ref[m], jnp.zeros((D, B), bf16))
        early_ref[p, D : 2 * D] = jnp.where(other, out_ref[m], jnp.zeros((D, B), bf16))
        shift = jnp.concatenate([lse_ref[m], lse_ref[m]], axis=0) - edge_ref[own + p]
        shift = jnp.where(other, shift, 0.0)
        high = shift.astype(bf16).astype(f32)
        middle = (shift - high).astype(bf16).astype(f32)
        rest = shift - high - middle
        tail = jnp.where(row == 0, high, jnp.where(row == 1, middle, jnp.where(row == 2, rest, 0.0)))
        early_ref[p, 2 * D :] = tail.astype(bf16)


def middle_kernel(
    at_ref, bias_ref, heads_ref, gathered_ref, mesh_ref, wq_ref, wk_ref, wv_ref, wl_ref,
    pack_ref, tail_ref, unit_ref, enc_ref,
):
    parts = heads_ref.shape[0]
    w_out = gathered_ref[:, 0:D, :].reshape(parts * D, C)
    w_layer = jnp.concatenate([wk_ref[...], wv_ref[...], wq_ref[...]], axis=0)
    half = parts // 2
    height = 2 * B // parts
    tail_ref[height:] = jnp.zeros((8, C), f32)
    queries, grads = [], []
    for b in range(2):
        rows = slice(b * B, (b + 1) * B)
        heads = heads_ref[:, b].reshape(parts * D, B)
        enc = mesh_ref[rows].astype(f32) + dot(heads, w_out, TN)
        enc_ref[rows] = enc
        unit, inverse = normalize(enc)
        unit = unit.astype(bf16)
        unit_ref[rows] = unit
        tail_ref[height:, b * B : (b + 1) * B] = jnp.broadcast_to(inverse, (B, 128)).T[0:8]
        both = dot(unit, w_layer, NT).astype(bf16)
        pack_ref[rows] = both[:, : 2 * D]
        queries.append((both[:, 2 * D :].astype(f32) * score_scale).astype(bf16))
        cot = gathered_ref[half * b : half * (b + 1), D + D // 2 :, :].reshape(B, C)
        grads.append(dot(cot, wl_ref[...], NT).astype(bf16))
    tail_ref[:height] = enc_ref[pl.ds(pl.multiple_of(at_ref[0] * height, height), height), :]
    pack_ref[2 * B : 3 * B] = jnp.concatenate(queries, axis=1)
    pack_ref[3 * B : 4 * B] = jnp.concatenate(grads, axis=1)
    row = lax.broadcasted_iota(jnp.int32, (8, 128), 0)
    table = jnp.zeros((8, 128), f32)
    for b in range(2):
        for n in range(3):
            table = jnp.where(row == 3 * b + n, bias_ref[b, n], table)
    high = table.astype(bf16).astype(f32)
    rest = table - high
    middle = rest.astype(bf16).astype(f32)
    tail = [high, middle, rest - middle, jnp.zeros((8, 128), f32)]
    pack_ref[4 * B : 4 * B + 32] = jnp.concatenate(tail, axis=0).astype(bf16)


def side_kernel(
    gathered_ref, unit_ref, tail_ref, wo_ref,
    cot_ref, unit_out_ref, inv_out_ref, sum_ref, half_ref, sem_ref,
):
    copy = pltpu.make_async_copy(gathered_ref.at[:, D : D + D // 2, :], half_ref, sem_ref)
    copy.start()
    half = gathered_ref.shape[0] // 2
    weight = wo_ref[...]
    for b in range(2):
        rows = slice(b * B, (b + 1) * B)
        cot = gathered_ref[half * b : half * (b + 1), D + D // 2 :, :].reshape(B, C)
        cot_ref[b] = dot(weight, cot, NT)
        unit_out_ref[b] = dot(weight, unit_ref[rows], NT)
        inv_out_ref[b] = tail_ref[tail_ref.shape[0] - 8 :, b * B : (b + 1) * B]
    sum_ref[...] = jnp.broadcast_to(
        jnp.sum(weight.astype(f32), axis=1, keepdims=True), sum_ref.shape
    )
    copy.wait()


def layer_kernel(
    own_ref, left_ref, right_ref, unit_ref, wq_ref, wk_ref, wv_ref, gathered_ref, send_ref
):
    zero = jnp.zeros((B, D), bf16)

    def block(ref, b):
        return ref[b * B : (b + 1) * B]

    def stacked(ref, b):
        lanes = slice(b * D, (b + 1) * D)
        query = ref[2 * B : 3 * B][:, lanes]
        grad = ref[3 * B : 4 * B][:, lanes]
        return jnp.concatenate(
            [jnp.concatenate([query, zero], axis=1), jnp.concatenate([zero, grad], axis=1)], axis=0
        )

    def table(ref):
        tail = ref[4 * B : 4 * B + 32].astype(f32)
        return tail[0:8] + tail[8:16] + tail[16:24]

    kv = [block(ref, b) for ref in (left_ref, own_ref, right_ref) for b in range(2)]
    own_bias = table(own_ref)
    queries = [(left_ref, 1, table(left_ref)), (own_ref, 0, own_bias), (own_ref, 1, own_bias)]
    queries.append((right_ref, 0, table(right_ref)))
    heads = []
    grad_kv = [jnp.zeros((B, 2 * D), f32), jnp.zeros((B, 2 * D), f32)]
    grad_q = []
    for j, (ref, b, bias) in enumerate(queries):
        pair = stacked(ref, b)
        window = kv[j : j + 3]
        both = [dot(rows, pair, NT) for rows in window]
        scores = [both[n][:, :B] + bias[3 * b + n : 3 * b + n + 1] for n in range(3)]
        top = folded(jnp.maximum, jnp.concatenate(scores, axis=0))
        top = jnp.max(top, axis=0, keepdims=True)
        raised = [jnp.exp(s - top) for s in scores]
        low = sum(folded(jnp.add, r) for r in raised)
        scale = 1.0 / jnp.sum(low, axis=0, keepdims=True)
        soft = [r * scale for r in raised]
        inner = sum(folded(jnp.add, soft[n] * both[n][:, B:]) for n in range(3))
        inner = jnp.sum(inner, axis=0, keepdims=True)
        mixed = [
            jnp.concatenate(
                [(soft[n] * (both[n][:, B:] - inner)).astype(bf16), soft[n].astype(bf16)], axis=1
            )
            for n in range(3)
        ]
        for n in range(3):
            own = j + n - 2
            if 0 <= own < 2:
                grad_kv[own] = grad_kv[own] + dot(mixed[n], pair)
        if 1 <= j <= 2:
            back = sum(dot(mixed[n], window[n], TN) for n in range(3))
            grad_q.append((back[:B, :D] * score_scale).astype(bf16))
            heads.append(back[B:, D:].astype(bf16))
    parts = gathered_ref.shape[0]
    w_layer = jnp.concatenate([wk_ref[...], wv_ref[...], wq_ref[...]], axis=0)
    totals, stats = [], jnp.zeros((8, 128), f32)
    lane = lax.broadcasted_iota(jnp.int32, (B, 128), 1)
    for b in range(2):
        grad = jnp.concatenate([grad_kv[b].astype(bf16), grad_q[b]], axis=1)
        total = dot(grad, w_layer)
        first = jnp.mean(total, axis=1, keepdims=True)
        second = jnp.mean(total * unit_ref[b * B : (b + 1) * B].astype(f32), axis=1, keepdims=True)
        first_high = first.astype(bf16).astype(f32)
        second_high = second.astype(bf16).astype(f32)
        columns = (first_high, second_high, first - first_high, second - second_high)
        table_b = jnp.zeros((B, 128), f32)
        for k, column in enumerate(columns):
            table_b = jnp.where(lane == 4 * b + k, column, table_b)
        stats = stats + table_b.T[0:8]
        totals.append(total.astype(bf16))
    stats = jnp.concatenate([stats[:, :D], stats[:, D:]], axis=0).astype(bf16)
    total = jnp.concatenate(totals, axis=0)
    heads = jnp.concatenate(heads, axis=0)
    share = heads.shape[0] // parts
    for z in range(parts):
        piece = dot(gathered_ref[z, 0:D, :], total, NT).astype(bf16)
        for b in range(2):
            send_ref[z, b * D : (b + 1) * D] = piece[:, b * B : (b + 1) * B]
        rows = heads[z * share : (z + 1) * share]
        send_ref[z, 2 * D :] = jnp.concatenate([rows, stats], axis=1)


def grad_kernel(
    slot_ref, count_ref, bias_ref, me_ref, arrived_ref, cot_ref, unit_ref, inv_ref, sum_ref,
    grad_ref, send_ref, reader_ref, edge_ref,
):
    full = jnp.where(count_ref[0] == FULL, 0, 1)
    fill_tables(slot_ref, bias_ref, full, reader_ref, edge_ref)
    total = arrived_ref[0].astype(f32)
    for z in range(1, arrived_ref.shape[0]):
        total = total + arrived_ref[z].astype(f32)
    stats = total[2 * D :, D:]
    stats = jnp.concatenate([stats[0:8], stats[8:16]], axis=1)
    for b in range(2):
        first = stats[4 * b : 4 * b + 1] + stats[4 * b + 2 : 4 * b + 3]
        second = stats[4 * b + 1 : 4 * b + 2] + stats[4 * b + 3 : 4 * b + 4]
        inside = total[b * D : (b + 1) * D] - first * sum_ref[...] - second * unit_ref[b]
        grad_ref[b] = (cot_ref[b] + inv_ref[b][0:1] * inside).astype(bf16)
    shards = send_ref.shape[0]
    own = reader_ref.shape[0] - shards
    for p in range(shards):
        block = grad_ref[reader_ref[own + p]]
        send_ref[p] = jnp.where(me_ref[0] != p, block, jnp.zeros((D, B), bf16))


def stacked_pair(query, grad):
    zero = jnp.zeros((D, B), bf16)
    return jnp.concatenate(
        [jnp.concatenate([query, zero], axis=1), jnp.concatenate([zero, grad], axis=1)], axis=0
    )


def row_products(grad, heads):
    return jnp.sum(grad.astype(f32) * heads.astype(f32), axis=0, keepdims=True)


def joined(soft, grad_soft, inner):
    return jnp.concatenate([(soft * (grad_soft - inner)).astype(bf16), soft.astype(bf16)], axis=1)


def ready_kernel(
    send_ref, slot_ref, count_ref, bias_ref, kv_ref, early_ref,
    query_ref, heads_ref, lse_ref, grad_ref, acc_ref, soft_ref, reader_ref, edge_ref,
):
    full = jnp.where(count_ref[0] == FULL, 0, 1)
    fill_tables(slot_ref, bias_ref, full, reader_ref, edge_ref)
    zero = jnp.zeros((D, B), bf16)

    def own_step(v, carry):
        m = reader_ref[v]
        pair = stacked_pair(query_ref[m], grad_ref[m])
        both = dot(kv_ref[v], pair)
        soft = jnp.exp(both[:, :B] - (lse_ref[m][0:1] - edge_ref[v]))
        inner = row_products(grad_ref[m], heads_ref[m])
        acc_ref[v] = dot(joined(soft, both[:, B:], inner), pair, NT)
        return carry

    lax.fori_loop(0, kv_ref.shape[0], own_step, 0, unroll=4)

    def sent_step(r, carry):
        block = early_ref[r]
        tail = block[2 * D :].astype(f32)
        shift = tail[0:1] + tail[1:2] + tail[2:3]
        query = jnp.concatenate([block[:D], zero], axis=0)
        soft_ref[r] = jnp.exp(dot(kv_ref[send_ref[r]], query) - shift)
        return carry

    lax.fori_loop(0, early_ref.shape[0], sent_step, 0, unroll=4)


def final_kernel(
    send_ref, norm_ref, kv_ref, early_ref, grads_ref, own_ref, soft_ref, out_ref, acc_ref,
    held_ref, weight_ref, sem_ref,
):
    pieces = 4
    each = soft_ref.shape[0] // pieces
    copies = [
        pltpu.make_async_copy(
            soft_ref.at[i * each : (i + 1) * each],
            weight_ref.at[i * each : (i + 1) * each],
            sem_ref.at[i],
        )
        for i in range(pieces)
    ]
    copies.append(pltpu.make_async_copy(norm_ref, held_ref, sem_ref.at[pieces]))
    for copy in copies:
        copy.start()
    acc_ref[...] = own_ref[...]

    def sent_step(r, carry):
        slot = send_ref[r]
        pair = stacked_pair(early_ref[r, :D], grads_ref[r])
        inner = row_products(grads_ref[r], early_ref[r, D : 2 * D])
        grad_soft = dot(kv_ref[slot], pair[:, B:])
        part = dot(joined(weight_ref[r], grad_soft, inner), pair, NT)
        acc_ref[slot] = acc_ref[slot] + part
        return carry

    for i in range(pieces):
        copies[i].wait()
        lax.fori_loop(i * each, (i + 1) * each, sent_step, 0, unroll=8)
    copies[pieces].wait()
    rows = acc_ref[...].reshape(norm_ref.shape[0], 2 * D).astype(bf16)
    shards, height = out_ref.shape[0], out_ref.shape[1]
    tile = 256
    for c in range(C // tile):
        part = dot(rows, held_ref[:, c * tile : (c + 1) * tile], TN).T
        per = tile // height
        out_ref[c * per : (c + 1) * per] = part.astype(bf16).reshape(per, height, 2 * D)


def output_kernel(me_ref, heads_ref, mine_ref, other_ref, tail_ref, out_ref):
    total = tail_ref[: out_ref.shape[0]]
    even = lax.rem(me_ref[0], 2) == 0
    half = D // 2
    for h in range(heads_ref.shape[0]):
        rows = heads_ref[h, 2 * D :][:, :D]
        low = jnp.where(even, mine_ref[h], other_ref[h])
        high = jnp.where(even, other_ref[h], mine_ref[h])
        total = total + dot(rows[:, :half], low) + dot(rows[:, half:], high)
    out_ref[...] = total.astype(bf16)


def sum_kernel(parts_ref, key_ref, value_ref):
    total = parts_ref[0].astype(f32)
    for i in range(1, parts_ref.shape[0]):
        total = total + parts_ref[i].astype(f32)
    key_ref[...] = total[:, :D]
    value_ref[...] = total[:, D:]


def exchange(array, axis):
    return lax.all_to_all(array, axis, split_axis=0, concat_axis=0, tiled=True)


def on_device(
    grid_feat,
    mesh_feat,
    query_weight,
    key_weight,
    value_weight,
    enc_out_weight,
    layer_query,
    layer_key,
    layer_value,
    layer_out_weight,
    enc_bias,
    layer_bias,
    send_list,
    edge_slot,
    edge_count,
    cotangent,
):
    shards = lax.axis_size("grid")
    parts = lax.axis_size("head")
    own = grid_feat.shape[0] // B
    share = cotangent.shape[0]
    send = send_list[0]
    enc_table = enc_bias[:, :, 0]
    layer_table = layer_bias[:, :, 0]
    shard_at = lax.axis_index("grid").astype(jnp.int32)[None]
    head_at = lax.axis_index("head").astype(jnp.int32)[None]
    forward = [(i, (i + 1) % shards) for i in range(shards)]
    backward = [(t, s) for s, t in forward]

    half = D // 2
    shared_rows = call(
        rows_kernel, struct((D + half + share, C), bf16), [VMEM] * 3, name="rows_part", mib=61
    )(enc_out_weight, layer_out_weight, cotangent)
    gathered = lax.all_gather(shared_rows, "head", axis=0, tiled=False)
    query_weight, key_weight, value_weight, layer_query, layer_key, layer_value = (
        weight.T
        for weight in (query_weight, key_weight, value_weight, layer_query, layer_key, layer_value)
    )

    grid_norm, own_kv, outgoing = grid_part(send, grid_feat, key_weight, value_weight, shards)
    arrived_kv = exchange(outgoing, "grid")
    queries = call(
        query_kernel, struct((2, D, B), bf16), [VMEM] * 2, name="query_part", data=1 << 20
    )(mesh_feat, query_weight)
    tables = [pltpu.SMEM((own + shards,), jnp.int32), pltpu.SMEM((own + shards,), f32)]
    enc_heads, lse, early = call(
        encoder_kernel,
        (
            struct((2, D, B), bf16),
            struct((2, 8, B), f32),
            struct((shards, 2 * D + 16, B), bf16),
        ),
        [SMEM] * 4 + [VMEM] * 3,
        [pltpu.VMEM((own + shards, B, 2 * D), bf16), pltpu.VMEM((FULL, B, B), f32)] + tables,
        name="encoder_part",
    )(edge_slot, edge_count, enc_table, shard_at, own_kv, arrived_kv, queries)
    arrived_early = exchange(early, "grid")
    all_heads = lax.all_gather(enc_heads, "head", axis=0, tiled=False)
    pack, tail, unit = call(
        middle_kernel,
        (
            struct((4 * B + 32, 2 * D), bf16),
            struct((share + 8, C), f32),
            struct((2 * B, C), bf16),
        ),
        [SMEM] * 2 + [VMEM] * 7,
        [pltpu.VMEM((2 * B, C), f32)],
        name="middle_part",
    )(
        head_at, layer_table, all_heads, gathered, mesh_feat, layer_query, layer_key, layer_value, layer_out_weight
    )
    left = lax.ppermute(pack, "grid", forward)
    right = lax.ppermute(pack, "grid", backward)
    cot_part, unit_part, inverse_row, weight_sum, half_mine = call(
        side_kernel,
        (
            struct((2, D, B), f32),
            struct((2, D, B), f32),
            struct((2, 8, B), f32),
            struct((D, B), f32),
            struct((parts, half, C), bf16),
        ),
        [VMEM] * 4,
        [pltpu.SemaphoreType.DMA],
        out_specs=(VMEM, VMEM, VMEM, VMEM, HBM),
        name="side_part",
    )(gathered, unit, tail, enc_out_weight)
    mixed = call(
        layer_kernel, struct((parts, 2 * D + share, B), bf16), [VMEM] * 8, name="layer_part"
    )(pack, left, right, unit, layer_query, layer_key, layer_value, gathered)
    arrived_early, mixed = lax.optimization_barrier((arrived_early, mixed))
    arrived_grad = exchange(mixed, "head")
    grads, send_grads = call(
        grad_kernel,
        (struct((2, D, B), bf16), struct((shards, D, B), bf16)),
        [SMEM] * 4 + [VMEM] * 5,
        tables,
        name="grad_part",
    )(
        edge_slot, edge_count, enc_table, shard_at, arrived_grad, cot_part, unit_part,
        inverse_row, weight_sum,
    )
    arrived_grads = exchange(send_grads, "grid")
    half_other = lax.ppermute(half_mine, "grid", [(i, i ^ 1) for i in range(shards)])
    own_grad, soft = call(
        ready_kernel,
        (struct((own, B, 2 * D), f32), struct((shards, B, B), f32)),
        [SMEM] * 4 + [VMEM] * 6,
        tables,
        name="ready_part",
    )(
        send, edge_slot, edge_count, enc_table, own_kv, arrived_early,
        queries, enc_heads, lse, grads,
    )
    product = call(
        final_kernel,
        struct((shards, C // shards, 2 * D), bf16),
        [SMEM, HBM] + [VMEM] * 4 + [HBM],
        [
            pltpu.VMEM((own, B, 2 * D), f32),
            pltpu.VMEM(grid_norm.shape, bf16),
            pltpu.VMEM((shards, B, B), f32),
            pltpu.SemaphoreType.DMA((5,)),
        ],
        name="final_part",
        mib=61,
    )(send, grid_norm, own_kv, arrived_early, arrived_grads, own_grad, soft)
    pieces = exchange(product, "grid")
    mesh_out = call(
        output_kernel,
        struct((share, C), bf16),
        [SMEM] + [VMEM] * 4,
        name="output_part",
    )(shard_at, arrived_grad, half_mine, half_other, tail)
    key_grad, value_grad = call(
        sum_kernel,
        (struct((C // shards, D), f32), struct((C // shards, D), f32)),
        [VMEM],
        name="sum_part",
    )(pieces)
    return mesh_out, key_grad, value_grad


def solution(mesh):
    in_specs = (
        P("grid", None),
        P("grid", None),
        P(None, "head"),
        P(None, "head"),
        P(None, "head"),
        P("head", None),
        P(None, "head"),
        P(None, "head"),
        P(None, "head"),
        P("head", None),
        P("grid", None, "head"),
        P("grid", None, "head"),
        P("grid", None),
        P("grid", None),
        P("grid"),
        P(("grid", "head"), None),
    )
    out_specs = (P(("grid", "head"), None), P("grid", "head"), P("grid", "head"))
    return jax.shard_map(
        on_device, mesh=mesh, in_specs=in_specs, out_specs=out_specs, check_vma=False
    )
```

```python
import jax
import jax.numpy as jnp
from jax import lax
from jax.experimental import pallas as pl
from jax.experimental.pallas import tpu as pltpu
from jax.sharding import PartitionSpec as P

D = 64
B = 128
C = 1024
FULL = 30
REST = 9
epsilon = 1e-05
score_scale = 0.125

f32 = jnp.float32
bf16 = jnp.bfloat16

NN = (((1,), (0,)), ((), ()))
NT = (((1,), (1,)), ((), ()))
TN = (((0,), (0,)), ((), ()))

VMEM = pl.BlockSpec(memory_space=pltpu.VMEM)
SMEM = pl.BlockSpec(memory_space=pltpu.SMEM)
HBM = pl.BlockSpec(memory_space=pltpu.HBM)


def dot(left, right, dims=NN):
    return lax.dot_general(left, right, dims, preferred_element_type=f32)


def struct(shape, dtype):
    return jax.ShapeDtypeStruct(shape, dtype)


def call(body, outs, specs, scratch=(), mib=16, flops=1 << 26, data=1 << 22, name=None, **extra):
    return pl.pallas_call(
        body,
        out_shape=outs,
        in_specs=specs,
        scratch_shapes=list(scratch),
        compiler_params=pltpu.CompilerParams(vmem_limit_bytes=mib << 20),
        cost_estimate=pl.CostEstimate(flops=flops, bytes_accessed=data, transcendentals=0),
        name=name,
        **extra,
    )


def normalize(values):
    center = values - jnp.mean(values, axis=-1, keepdims=True)
    inverse = lax.rsqrt(jnp.mean(center * center, axis=-1, keepdims=True) + epsilon)
    return center * inverse, inverse


def grid_kernel(send_ref, feat_ref, wk_ref, wv_ref, norm_ref, kv_ref, out_ref):
    step = pl.program_id(0)
    unit, _ = normalize(feat_ref[...].astype(f32))
    rows = unit.astype(bf16)
    norm_ref[...] = rows
    weight = jnp.concatenate([wk_ref[...], wv_ref[...]], axis=0)
    both = dot(rows, weight, NT).astype(bf16)
    per = both.shape[0] // B
    for i in range(per):
        kv_ref[step * per + i] = both[i * B : (i + 1) * B]

    @pl.when(step == pl.num_programs(0) - 1)
    def _():
        for i in range(out_ref.shape[0]):
            out_ref[i] = kv_ref[send_ref[i]]


def grid_part(send, feat, wk, wv, shards):
    rows = feat.shape[0]
    steps = 4
    return pl.pallas_call(
        grid_kernel,
        grid=(steps,),
        out_shape=(
            struct((rows, C), bf16),
            struct((rows // B, B, 2 * D), bf16),
            struct((shards, B, 2 * D), bf16),
        ),
        in_specs=[
            SMEM,
            pl.BlockSpec((rows // steps, C), lambda i: (i, 0)),
            pl.BlockSpec((D, C), lambda i: (0, 0)),
            pl.BlockSpec((D, C), lambda i: (0, 0)),
        ],
        out_specs=(
            pl.BlockSpec((rows // steps, C), lambda i: (i, 0)),
            pl.BlockSpec((rows // B, B, 2 * D), lambda i: (0, 0, 0)),
            pl.BlockSpec((shards, B, 2 * D), lambda i: (0, 0, 0)),
        ),
        compiler_params=pltpu.CompilerParams(vmem_limit_bytes=60 << 20),
        cost_estimate=pl.CostEstimate(
            flops=1 << 28, bytes_accessed=6 << 20, transcendentals=0
        ),
        name="grid_part",
    )(send, feat, wk, wv)


def rows_kernel(wo_ref, wl_ref, cot_ref, out_ref):
    half = D // 2
    start = pl.multiple_of(lax.rem(lax.axis_index("grid"), 2) * half, half)
    out_ref[0:D] = wo_ref[...]
    out_ref[D : D + half] = wl_ref[pl.ds(start, half)]
    out_ref[D + half :] = cot_ref[...]


def query_kernel(mesh_ref, wq_ref, out_ref):
    for b in range(out_ref.shape[0]):
        unit, _ = normalize(mesh_ref[b * B : (b + 1) * B].astype(f32))
        rows = dot(wq_ref[...], unit.astype(bf16), NT).astype(bf16).astype(f32) * score_scale
        out_ref[b] = rows.astype(bf16)


def fill_pool(pool_ref, own_ref, arrived_ref):
    own = own_ref.shape[0]
    for i in range(own):
        pool_ref[i] = own_ref[i]
    for i in range(arrived_ref.shape[0]):
        pool_ref[own + i] = arrived_ref[i]


def folded(op, values):
    parts = [values[i * 8 : (i + 1) * 8] for i in range(values.shape[0] // 8)]
    while len(parts) > 1:
        parts = [
            op(parts[i], parts[i + 1]) if i + 1 < len(parts) else parts[i]
            for i in range(0, len(parts), 2)
        ]
    return parts[0]


def fill_tables(slot_ref, bias_ref, full, reader_ref, edge_ref):
    for i in range(reader_ref.shape[0]):
        reader_ref[i] = 0
        edge_ref[i] = 0.0
    for m, total in ((full, FULL), (1 - full, REST)):

        def put(e, carry, m=m):
            slot = slot_ref[m, e]
            reader_ref[slot] = m
            edge_ref[slot] = bias_ref[m, e]
            return carry

        lax.fori_loop(0, total, put, 0, unroll=3)


def encoder_kernel(
    slot_ref, count_ref, bias_ref, me_ref, own_ref, arrived_ref, query_ref,
    out_ref, lse_ref, early_ref, pool_ref, score_ref, reader_ref, edge_ref,
):
    fill_pool(pool_ref, own_ref, arrived_ref)
    full = jnp.where(count_ref[0] == FULL, 0, 1)
    fill_tables(slot_ref, bias_ref, full, reader_ref, edge_ref)
    for m, total in ((full, FULL), (1 - full, REST)):
        stack = jnp.concatenate([query_ref[m], jnp.zeros((D, B), bf16)], axis=0)

        def scores(e, top, m=m, stack=stack):
            value = dot(pool_ref[slot_ref[m, e]], stack) + bias_ref[m, e]
            score_ref[e] = value
            return jnp.maximum(top, folded(jnp.maximum, value))

        top = lax.fori_loop(0, total, scores, jnp.full((8, B), -jnp.inf, f32), unroll=3)
        top = jnp.max(top, axis=0, keepdims=True)

        def mix(e, carry, m=m, top=top):
            low, acc = carry
            raised = jnp.exp(score_ref[e] - top)
            acc = acc + dot(pool_ref[slot_ref[m, e]], raised.astype(bf16), TN)
            return low + folded(jnp.add, raised), acc

        low, acc = lax.fori_loop(
            0, total, mix, (jnp.zeros((8, B), f32), jnp.zeros((2 * D, B), f32)), unroll=3
        )
        low = jnp.sum(low, axis=0, keepdims=True)
        out_ref[m] = (acc[D:] / low).astype(bf16)
        lse_ref[m] = jnp.broadcast_to(top + jnp.log(low), (8, B))
    own = own_ref.shape[0]
    row = lax.broadcasted_iota(jnp.int32, (16, B), 0)
    for p in range(early_ref.shape[0]):
        m = reader_ref[own + p]
        other = me_ref[0] != p
        early_ref[p, 0:D] = jnp.where(other, query_ref[m], jnp.zeros((D, B), bf16))
        early_ref[p, D : 2 * D] = jnp.where(other, out_ref[m], jnp.zeros((D, B), bf16))
        shift = jnp.concatenate([lse_ref[m], lse_ref[m]], axis=0) - edge_ref[own + p]
        shift = jnp.where(other, shift, 0.0)
        high = shift.astype(bf16).astype(f32)
        middle = (shift - high).astype(bf16).astype(f32)
        rest = shift - high - middle
        tail = jnp.where(row == 0, high, jnp.where(row == 1, middle, jnp.where(row == 2, rest, 0.0)))
        early_ref[p, 2 * D :] = tail.astype(bf16)


def middle_kernel(
    at_ref, bias_ref, heads_ref, gathered_ref, mesh_ref, wq_ref, wk_ref, wv_ref, wl_ref,
    left_ref, right_ref, tail_ref, unit_ref, enc_ref,
):
    parts = heads_ref.shape[0]
    w_out = gathered_ref[:, 0:D, :].reshape(parts * D, C)
    w_layer = jnp.concatenate([wk_ref[...], wv_ref[...], wq_ref[...]], axis=0)
    half = parts // 2
    height = 2 * B // parts
    tail_ref[height:] = jnp.zeros((8, C), f32)
    messages = (left_ref, right_ref)
    for b in range(2):
        rows = slice(b * B, (b + 1) * B)
        heads = heads_ref[:, b].reshape(parts * D, B)
        enc = mesh_ref[rows].astype(f32) + dot(heads, w_out, TN)
        enc_ref[rows] = enc
        unit, inverse = normalize(enc)
        unit = unit.astype(bf16)
        unit_ref[rows] = unit
        tail_ref[height:, b * B : (b + 1) * B] = jnp.broadcast_to(inverse, (B, 128)).T[0:8]
        both = dot(unit, w_layer, NT).astype(bf16)
        for message in messages:
            message[rows] = both[:, : 2 * D]
        queries = (both[:, 2 * D :].astype(f32) * score_scale).astype(bf16)
        cot = gathered_ref[half * b : half * (b + 1), D + D // 2 :, :].reshape(B, C)
        grads = dot(cot, wl_ref[...], NT).astype(bf16)
        messages[b][2 * B : 3 * B] = jnp.concatenate([queries, grads], axis=1)
    tail_ref[:height] = enc_ref[pl.ds(pl.multiple_of(at_ref[0] * height, height), height), :]
    row = lax.broadcasted_iota(jnp.int32, (8, 128), 0)
    table = jnp.zeros((8, 128), f32)
    for b in range(2):
        for n in range(3):
            table = jnp.where(row == 3 * b + n, bias_ref[b, n], table)
    high = table.astype(bf16).astype(f32)
    rest = table - high
    middle = rest.astype(bf16).astype(f32)
    tail = [high, middle, rest - middle, jnp.zeros((8, 128), f32)]
    for message in messages:
        message[3 * B : 3 * B + 32] = jnp.concatenate(tail, axis=0).astype(bf16)


def side_kernel(
    gathered_ref, unit_ref, tail_ref, wo_ref,
    cot_ref, unit_out_ref, inv_out_ref, sum_ref, half_ref, sem_ref,
):
    copy = pltpu.make_async_copy(gathered_ref.at[:, D : D + D // 2, :], half_ref, sem_ref)
    copy.start()
    half = gathered_ref.shape[0] // 2
    weight = wo_ref[...]
    for b in range(2):
        rows = slice(b * B, (b + 1) * B)
        cot = gathered_ref[half * b : half * (b + 1), D + D // 2 :, :].reshape(B, C)
        cot_ref[b] = dot(weight, cot, NT)
        unit_out_ref[b] = dot(weight, unit_ref[rows], NT)
        inv_out_ref[b] = tail_ref[tail_ref.shape[0] - 8 :, b * B : (b + 1) * B]
    sum_ref[...] = jnp.broadcast_to(
        jnp.sum(weight.astype(f32), axis=1, keepdims=True), sum_ref.shape
    )
    copy.wait()


def layer_kernel(
    low_ref, high_ref, left_ref, right_ref, unit_ref, wq_ref, wk_ref, wv_ref, gathered_ref,
    send_ref,
):
    zero = jnp.zeros((B, 2 * D), bf16)
    first = lax.broadcasted_iota(jnp.int32, (B, 2 * D), 1) < D

    def block(ref, b):
        return ref[b * B : (b + 1) * B]

    def stacked(ref):
        rows = block(ref, 2)
        return jnp.concatenate([jnp.where(first, rows, zero), jnp.where(first, zero, rows)], axis=0)

    def table(ref):
        tail = ref[3 * B : 3 * B + 32].astype(f32)
        return tail[0:8] + tail[8:16] + tail[16:24]

    kv = [block(ref, b) for ref in (left_ref, low_ref, right_ref) for b in range(2)]
    own_bias = table(low_ref)
    queries = [(left_ref, 1, table(left_ref)), (low_ref, 0, own_bias), (high_ref, 1, own_bias)]
    queries.append((right_ref, 0, table(right_ref)))
    heads = []
    grad_kv = [jnp.zeros((B, 2 * D), f32), jnp.zeros((B, 2 * D), f32)]
    grad_q = []
    for j, (ref, b, bias) in enumerate(queries):
        pair = stacked(ref)
        window = kv[j : j + 3]
        both = [dot(rows, pair, NT) for rows in window]
        scores = [both[n][:, :B] + bias[3 * b + n : 3 * b + n + 1] for n in range(3)]
        top = folded(jnp.maximum, jnp.concatenate(scores, axis=0))
        top = jnp.max(top, axis=0, keepdims=True)
        raised = [jnp.exp(s - top) for s in scores]
        low = sum(folded(jnp.add, r) for r in raised)
        scale = 1.0 / jnp.sum(low, axis=0, keepdims=True)
        soft = [r * scale for r in raised]
        inner = sum(folded(jnp.add, soft[n] * both[n][:, B:]) for n in range(3))
        inner = jnp.sum(inner, axis=0, keepdims=True)
        mixed = [
            jnp.concatenate(
                [(soft[n] * (both[n][:, B:] - inner)).astype(bf16), soft[n].astype(bf16)], axis=1
            )
            for n in range(3)
        ]
        for n in range(3):
            own = j + n - 2
            if 0 <= own < 2:
                grad_kv[own] = grad_kv[own] + dot(mixed[n], pair)
        if 1 <= j <= 2:
            back = sum(dot(mixed[n], window[n], TN) for n in range(3))
            grad_q.append((back[:B, :D] * score_scale).astype(bf16))
            heads.append(back[B:, D:].astype(bf16))
    parts = gathered_ref.shape[0]
    w_layer = jnp.concatenate([wk_ref[...], wv_ref[...], wq_ref[...]], axis=0)
    totals, stats = [], jnp.zeros((8, 128), f32)
    lane = lax.broadcasted_iota(jnp.int32, (B, 128), 1)
    for b in range(2):
        grad = jnp.concatenate([grad_kv[b].astype(bf16), grad_q[b]], axis=1)
        total = dot(grad, w_layer)
        first = jnp.mean(total, axis=1, keepdims=True)
        second = jnp.mean(total * unit_ref[b * B : (b + 1) * B].astype(f32), axis=1, keepdims=True)
        first_high = first.astype(bf16).astype(f32)
        second_high = second.astype(bf16).astype(f32)
        columns = (first_high, second_high, first - first_high, second - second_high)
        table_b = jnp.zeros((B, 128), f32)
        for k, column in enumerate(columns):
            table_b = jnp.where(lane == 4 * b + k, column, table_b)
        stats = stats + table_b.T[0:8]
        totals.append(total.astype(bf16))
    stats = jnp.concatenate([stats[:, :D], stats[:, D:]], axis=0).astype(bf16)
    total = jnp.concatenate(totals, axis=0)
    heads = jnp.concatenate(heads, axis=0)
    share = heads.shape[0] // parts
    for z in range(parts):
        piece = dot(gathered_ref[z, 0:D, :], total, NT).astype(bf16)
        for b in range(2):
            send_ref[z, b * D : (b + 1) * D] = piece[:, b * B : (b + 1) * B]
        rows = heads[z * share : (z + 1) * share]
        send_ref[z, 2 * D :] = jnp.concatenate([rows, stats], axis=1)


def grad_kernel(
    slot_ref, count_ref, bias_ref, me_ref, arrived_ref, cot_ref, unit_ref, inv_ref, sum_ref,
    grad_ref, send_ref, reader_ref, edge_ref,
):
    full = jnp.where(count_ref[0] == FULL, 0, 1)
    fill_tables(slot_ref, bias_ref, full, reader_ref, edge_ref)
    total = arrived_ref[0].astype(f32)
    for z in range(1, arrived_ref.shape[0]):
        total = total + arrived_ref[z].astype(f32)
    stats = total[2 * D :, D:]
    stats = jnp.concatenate([stats[0:8], stats[8:16]], axis=1)
    for b in range(2):
        first = stats[4 * b : 4 * b + 1] + stats[4 * b + 2 : 4 * b + 3]
        second = stats[4 * b + 1 : 4 * b + 2] + stats[4 * b + 3 : 4 * b + 4]
        inside = total[b * D : (b + 1) * D] - first * sum_ref[...] - second * unit_ref[b]
        grad_ref[b] = (cot_ref[b] + inv_ref[b][0:1] * inside).astype(bf16)
    shards = send_ref.shape[0]
    own = reader_ref.shape[0] - shards
    for p in range(shards):
        block = grad_ref[reader_ref[own + p]]
        send_ref[p] = jnp.where(me_ref[0] != p, block, jnp.zeros((D, B), bf16))


def final_kernel(
    send_ref, slot_ref, count_ref, bias_ref, norm_ref, kv_ref, early_ref, grads_ref,
    query_ref, heads_ref, lse_ref, grad_ref, out_ref, acc_ref, reader_ref, edge_ref,
    held_ref, block_ref, part_ref, sem_ref,
):
    copies = [
        pltpu.make_async_copy(early_ref, block_ref, sem_ref.at[0]),
        pltpu.make_async_copy(grads_ref, part_ref, sem_ref.at[1]),
        pltpu.make_async_copy(norm_ref, held_ref, sem_ref.at[2]),
    ]
    for copy in copies:
        copy.start()
    full = jnp.where(count_ref[0] == FULL, 0, 1)
    fill_tables(slot_ref, bias_ref, full, reader_ref, edge_ref)
    zero = jnp.zeros((D, B), bf16)

    def back(keys, query, heads, shift, grad):
        inner = jnp.sum(grad.astype(f32) * heads.astype(f32), axis=0, keepdims=True)
        pair = jnp.concatenate(
            [jnp.concatenate([query, zero], axis=1), jnp.concatenate([zero, grad], axis=1)], axis=0
        )
        both = dot(keys, pair)
        soft = jnp.exp(both[:, :B] - shift)
        mixed = jnp.concatenate(
            [(soft * (both[:, B:] - inner)).astype(bf16), soft.astype(bf16)], axis=1
        )
        return dot(mixed, pair, NT)

    def own_step(v, carry):
        m = reader_ref[v]
        shift = lse_ref[m][0:1] - edge_ref[v]
        acc_ref[v] = back(kv_ref[v], query_ref[m], heads_ref[m], shift, grad_ref[m])
        return carry

    lax.fori_loop(0, kv_ref.shape[0], own_step, 0, unroll=4)

    def sent_step(r, carry):
        slot = send_ref[r]
        block = block_ref[r]
        tail = block[2 * D :].astype(f32)
        shift = tail[0:1] + tail[1:2] + tail[2:3]
        part = back(kv_ref[slot], block[:D], block[D : 2 * D], shift, part_ref[r])
        acc_ref[slot] = acc_ref[slot] + part
        return carry

    copies[0].wait()
    copies[1].wait()
    lax.fori_loop(0, block_ref.shape[0], sent_step, 0, unroll=4)
    rows = acc_ref[...].reshape(norm_ref.shape[0], 2 * D).astype(bf16)
    copies[2].wait()
    shards, height = out_ref.shape[0], out_ref.shape[1]
    tile = 256
    for c in range(C // tile):
        part = dot(rows, held_ref[:, c * tile : (c + 1) * tile], TN).T
        per = tile // height
        out_ref[c * per : (c + 1) * per] = part.astype(bf16).reshape(per, height, 2 * D)


def output_kernel(me_ref, heads_ref, mine_ref, other_ref, tail_ref, out_ref):
    total = tail_ref[: out_ref.shape[0]]
    even = lax.rem(me_ref[0], 2) == 0
    half = D // 2
    for h in range(heads_ref.shape[0]):
        rows = heads_ref[h, 2 * D :][:, :D]
        low = jnp.where(even, mine_ref[h], other_ref[h])
        high = jnp.where(even, other_ref[h], mine_ref[h])
        total = total + dot(rows[:, :half], low) + dot(rows[:, half:], high)
    out_ref[...] = total.astype(bf16)


def sum_kernel(parts_ref, key_ref, value_ref):
    total = parts_ref[0].astype(f32)
    for i in range(1, parts_ref.shape[0]):
        total = total + parts_ref[i].astype(f32)
    key_ref[...] = total[:, :D]
    value_ref[...] = total[:, D:]


def exchange(array, axis):
    return lax.all_to_all(array, axis, split_axis=0, concat_axis=0, tiled=True)


def on_device(
    grid_feat,
    mesh_feat,
    query_weight,
    key_weight,
    value_weight,
    enc_out_weight,
    layer_query,
    layer_key,
    layer_value,
    layer_out_weight,
    enc_bias,
    layer_bias,
    send_list,
    edge_slot,
    edge_count,
    cotangent,
):
    shards = lax.axis_size("grid")
    parts = lax.axis_size("head")
    own = grid_feat.shape[0] // B
    share = cotangent.shape[0]
    send = send_list[0]
    enc_table = enc_bias[:, :, 0]
    layer_table = layer_bias[:, :, 0]
    shard_at = lax.axis_index("grid").astype(jnp.int32)[None]
    head_at = lax.axis_index("head").astype(jnp.int32)[None]
    forward = [(i, (i + 1) % shards) for i in range(shards)]
    backward = [(t, s) for s, t in forward]

    half = D // 2
    shared_rows = call(
        rows_kernel, struct((D + half + share, C), bf16), [VMEM] * 3, name="rows_part", mib=61
    )(enc_out_weight, layer_out_weight, cotangent)
    gathered = lax.all_gather(shared_rows, "head", axis=0, tiled=False)
    query_weight, key_weight, value_weight, layer_query, layer_key, layer_value = (
        weight.T
        for weight in (query_weight, key_weight, value_weight, layer_query, layer_key, layer_value)
    )

    grid_norm, own_kv, outgoing = grid_part(send, grid_feat, key_weight, value_weight, shards)
    arrived_kv = exchange(outgoing, "grid")
    queries = call(
        query_kernel, struct((2, D, B), bf16), [VMEM] * 2, name="query_part", data=1 << 20
    )(mesh_feat, query_weight)
    tables = [pltpu.SMEM((own + shards,), jnp.int32), pltpu.SMEM((own + shards,), f32)]
    enc_heads, lse, early = call(
        encoder_kernel,
        (
            struct((2, D, B), bf16),
            struct((2, 8, B), f32),
            struct((shards, 2 * D + 16, B), bf16),
        ),
        [SMEM] * 4 + [VMEM] * 3,
        [pltpu.VMEM((own + shards, B, 2 * D), bf16), pltpu.VMEM((FULL, B, B), f32)] + tables,
        name="encoder_part",
    )(edge_slot, edge_count, enc_table, shard_at, own_kv, arrived_kv, queries)
    arrived_early = exchange(early, "grid")
    all_heads = lax.all_gather(enc_heads, "head", axis=0, tiled=False)
    low, high, tail, unit = call(
        middle_kernel,
        (
            struct((3 * B + 32, 2 * D), bf16),
            struct((3 * B + 32, 2 * D), bf16),
            struct((share + 8, C), f32),
            struct((2 * B, C), bf16),
        ),
        [SMEM] * 2 + [VMEM] * 7,
        [pltpu.VMEM((2 * B, C), f32)],
        name="middle_part",
    )(
        head_at, layer_table, all_heads, gathered, mesh_feat, layer_query, layer_key, layer_value, layer_out_weight
    )
    left = lax.ppermute(high, "grid", forward)
    right = lax.ppermute(low, "grid", backward)
    cot_part, unit_part, inverse_row, weight_sum, half_mine = call(
        side_kernel,
        (
            struct((2, D, B), f32),
            struct((2, D, B), f32),
            struct((2, 8, B), f32),
            struct((D, B), f32),
            struct((parts, half, C), bf16),
        ),
        [VMEM] * 4,
        [pltpu.SemaphoreType.DMA],
        out_specs=(VMEM, VMEM, VMEM, VMEM, HBM),
        name="side_part",
    )(gathered, unit, tail, enc_out_weight)
    mixed = call(
        layer_kernel, struct((parts, 2 * D + share, B), bf16), [VMEM] * 9, name="layer_part"
    )(low, high, left, right, unit, layer_query, layer_key, layer_value, gathered)
    arrived_early, mixed = lax.optimization_barrier((arrived_early, mixed))
    arrived_grad = exchange(mixed, "head")
    grads, send_grads = call(
        grad_kernel,
        (struct((2, D, B), bf16), struct((shards, D, B), bf16)),
        [SMEM] * 4 + [VMEM] * 5,
        tables,
        name="grad_part",
    )(
        edge_slot, edge_count, enc_table, shard_at, arrived_grad, cot_part, unit_part,
        inverse_row, weight_sum,
    )
    arrived_grads = exchange(send_grads, "grid")
    half_other = lax.ppermute(half_mine, "grid", [(i, i ^ 1) for i in range(shards)])
    product = call(
        final_kernel,
        struct((shards, C // shards, 2 * D), bf16),
        [SMEM] * 4 + [HBM, VMEM, HBM, HBM] + [VMEM] * 4,
        [pltpu.VMEM((own, B, 2 * D), f32)]
        + tables
        + [
            pltpu.VMEM(grid_norm.shape, bf16),
            pltpu.VMEM((shards, 2 * D + 16, B), bf16),
            pltpu.VMEM((shards, D, B), bf16),
            pltpu.SemaphoreType.DMA((3,)),
        ],
        name="final_part",
        mib=61,
    )(
        send, edge_slot, edge_count, enc_table, grid_norm, own_kv, arrived_early, arrived_grads,
        queries, enc_heads, lse, grads,
    )
    pieces = exchange(product, "grid")
    mesh_out = call(
        output_kernel,
        struct((share, C), bf16),
        [SMEM] + [VMEM] * 4,
        name="output_part",
    )(shard_at, arrived_grad, half_mine, half_other, tail)
    key_grad, value_grad = call(
        sum_kernel,
        (struct((C // shards, D), f32), struct((C // shards, D), f32)),
        [VMEM],
        name="sum_part",
    )(pieces)
    return mesh_out, key_grad, value_grad


def solution(mesh):
    in_specs = (
        P("grid", None),
        P("grid", None),
        P(None, "head"),
        P(None, "head"),
        P(None, "head"),
        P("head", None),
        P(None, "head"),
        P(None, "head"),
        P(None, "head"),
        P("head", None),
        P("grid", None, "head"),
        P("grid", None, "head"),
        P("grid", None),
        P("grid", None),
        P("grid"),
        P(("grid", "head"), None),
    )
    out_specs = (P(("grid", "head"), None), P("grid", "head"), P("grid", "head"))
    return jax.shard_map(
        on_device, mesh=mesh, in_specs=in_specs, out_specs=out_specs, check_vma=False
    )
```

```python
import jax
import jax.numpy as jnp
from jax import lax
from jax.experimental import pallas as pl
from jax.experimental.pallas import tpu as pltpu
from jax.sharding import PartitionSpec as P

D = 64
B = 128
C = 1024
FULL = 30
REST = 9
epsilon = 1e-05
score_scale = 0.125

f32 = jnp.float32
bf16 = jnp.bfloat16

NN = (((1,), (0,)), ((), ()))
NT = (((1,), (1,)), ((), ()))
TN = (((0,), (0,)), ((), ()))

VMEM = pl.BlockSpec(memory_space=pltpu.VMEM)
SMEM = pl.BlockSpec(memory_space=pltpu.SMEM)
HBM = pl.BlockSpec(memory_space=pltpu.HBM)


def dot(left, right, dims=NN):
    return lax.dot_general(left, right, dims, preferred_element_type=f32)


def struct(shape, dtype):
    return jax.ShapeDtypeStruct(shape, dtype)


def call(body, outs, specs, scratch=(), mib=16, flops=1 << 26, data=1 << 22, name=None, **extra):
    return pl.pallas_call(
        body,
        out_shape=outs,
        in_specs=specs,
        scratch_shapes=list(scratch),
        compiler_params=pltpu.CompilerParams(vmem_limit_bytes=mib << 20),
        cost_estimate=pl.CostEstimate(flops=flops, bytes_accessed=data, transcendentals=0),
        name=name,
        **extra,
    )


def normalize(values):
    center = values - jnp.mean(values, axis=-1, keepdims=True)
    inverse = lax.rsqrt(jnp.mean(center * center, axis=-1, keepdims=True) + epsilon)
    return center * inverse, inverse


def grid_kernel(send_ref, feat_ref, wk_ref, wv_ref, norm_ref, kv_ref, out_ref):
    step = pl.program_id(0)
    unit, _ = normalize(feat_ref[...].astype(f32))
    rows = unit.astype(bf16)
    norm_ref[...] = rows
    weight = jnp.concatenate([wk_ref[...], wv_ref[...]], axis=0)
    both = dot(rows, weight, NT).astype(bf16)
    per = both.shape[0] // B
    for i in range(per):
        kv_ref[step * per + i] = both[i * B : (i + 1) * B]

    @pl.when(step == pl.num_programs(0) - 1)
    def _():
        for i in range(out_ref.shape[0]):
            out_ref[i] = kv_ref[send_ref[i]]


def grid_part(send, feat, wk, wv, shards):
    rows = feat.shape[0]
    steps = 4
    return pl.pallas_call(
        grid_kernel,
        grid=(steps,),
        out_shape=(
            struct((rows, C), bf16),
            struct((rows // B, B, 2 * D), bf16),
            struct((shards, B, 2 * D), bf16),
        ),
        in_specs=[
            SMEM,
            pl.BlockSpec((rows // steps, C), lambda i: (i, 0)),
            pl.BlockSpec((D, C), lambda i: (0, 0)),
            pl.BlockSpec((D, C), lambda i: (0, 0)),
        ],
        out_specs=(
            pl.BlockSpec((rows // steps, C), lambda i: (i, 0)),
            pl.BlockSpec((rows // B, B, 2 * D), lambda i: (0, 0, 0)),
            pl.BlockSpec((shards, B, 2 * D), lambda i: (0, 0, 0)),
        ),
        compiler_params=pltpu.CompilerParams(vmem_limit_bytes=60 << 20),
        cost_estimate=pl.CostEstimate(
            flops=1 << 28, bytes_accessed=6 << 20, transcendentals=0
        ),
        name="grid_part",
    )(send, feat, wk, wv)


def rows_kernel(wo_ref, wl_ref, cot_ref, out_ref):
    half = D // 2
    start = pl.multiple_of(lax.rem(lax.axis_index("grid"), 2) * half, half)
    out_ref[0:D] = wo_ref[...]
    out_ref[D : D + half] = wl_ref[pl.ds(start, half)]
    out_ref[D + half :] = cot_ref[...]


def query_kernel(mesh_ref, wq_ref, out_ref):
    for b in range(out_ref.shape[0]):
        unit, _ = normalize(mesh_ref[b * B : (b + 1) * B].astype(f32))
        rows = dot(wq_ref[...], unit.astype(bf16), NT).astype(bf16).astype(f32) * score_scale
        out_ref[b] = rows.astype(bf16)


def fill_pool(pool_ref, own_ref, arrived_ref):
    own = own_ref.shape[0]
    for i in range(own):
        pool_ref[i] = own_ref[i]
    for i in range(arrived_ref.shape[0]):
        pool_ref[own + i] = arrived_ref[i]


def folded(op, values):
    parts = [values[i * 8 : (i + 1) * 8] for i in range(values.shape[0] // 8)]
    while len(parts) > 1:
        parts = [
            op(parts[i], parts[i + 1]) if i + 1 < len(parts) else parts[i]
            for i in range(0, len(parts), 2)
        ]
    return parts[0]


def fill_tables(slot_ref, bias_ref, full, reader_ref, edge_ref):
    for i in range(reader_ref.shape[0]):
        reader_ref[i] = 0
        edge_ref[i] = 0.0
    for m, total in ((full, FULL), (1 - full, REST)):

        def put(e, carry, m=m):
            slot = slot_ref[m, e]
            reader_ref[slot] = m
            edge_ref[slot] = bias_ref[m, e]
            return carry

        lax.fori_loop(0, total, put, 0, unroll=3)


def encoder_kernel(
    slot_ref, count_ref, bias_ref, me_ref, own_ref, arrived_ref, query_ref,
    out_ref, lse_ref, early_ref, pool_ref, score_ref, reader_ref, edge_ref,
):
    fill_pool(pool_ref, own_ref, arrived_ref)
    full = jnp.where(count_ref[0] == FULL, 0, 1)
    fill_tables(slot_ref, bias_ref, full, reader_ref, edge_ref)
    for m, total in ((full, FULL), (1 - full, REST)):
        stack = jnp.concatenate([query_ref[m], jnp.zeros((D, B), bf16)], axis=0)

        def scores(i, top, m=m, stack=stack):
            values = []
            for k in range(3):
                e = 3 * i + k
                values.append(dot(pool_ref[slot_ref[m, e]], stack) + bias_ref[m, e])
            for k in range(3):
                score_ref[3 * i + k] = values[k]
                top = jnp.maximum(top, folded(jnp.maximum, values[k]))
            return top

        top = lax.fori_loop(0, total // 3, scores, jnp.full((8, B), -jnp.inf, f32))
        top = jnp.max(top, axis=0, keepdims=True)

        def mix(e, carry, m=m, top=top):
            low, acc = carry
            raised = jnp.exp(score_ref[e] - top)
            acc = acc + dot(pool_ref[slot_ref[m, e]], raised.astype(bf16), TN)
            return low + folded(jnp.add, raised), acc

        low, acc = lax.fori_loop(
            0, total, mix, (jnp.zeros((8, B), f32), jnp.zeros((2 * D, B), f32)), unroll=3
        )
        low = jnp.sum(low, axis=0, keepdims=True)
        out_ref[m] = (acc[D:] / low).astype(bf16)
        lse_ref[m] = jnp.broadcast_to(top + jnp.log(low), (8, B))
    own = own_ref.shape[0]
    row = lax.broadcasted_iota(jnp.int32, (16, B), 0)
    for p in range(early_ref.shape[0]):
        m = reader_ref[own + p]
        other = me_ref[0] != p
        early_ref[p, 0:D] = jnp.where(other, query_ref[m], jnp.zeros((D, B), bf16))
        early_ref[p, D : 2 * D] = jnp.where(other, out_ref[m], jnp.zeros((D, B), bf16))
        shift = jnp.concatenate([lse_ref[m], lse_ref[m]], axis=0) - edge_ref[own + p]
        shift = jnp.where(other, shift, 0.0)
        high = shift.astype(bf16).astype(f32)
        middle = (shift - high).astype(bf16).astype(f32)
        rest = shift - high - middle
        tail = jnp.where(row == 0, high, jnp.where(row == 1, middle, jnp.where(row == 2, rest, 0.0)))
        early_ref[p, 2 * D :] = tail.astype(bf16)


def middle_kernel(
    at_ref, bias_ref, heads_ref, gathered_ref, mesh_ref, wq_ref, wk_ref, wv_ref, wl_ref,
    left_ref, right_ref, tail_ref, unit_ref, enc_ref,
):
    parts = heads_ref.shape[0]
    w_out = gathered_ref[:, 0:D, :].reshape(parts * D, C)
    w_layer = jnp.concatenate([wk_ref[...], wv_ref[...], wq_ref[...]], axis=0)
    half = parts // 2
    height = 2 * B // parts
    tail_ref[height:] = jnp.zeros((8, C), f32)
    messages = (left_ref, right_ref)
    for b in range(2):
        rows = slice(b * B, (b + 1) * B)
        heads = heads_ref[:, b].reshape(parts * D, B)
        enc = mesh_ref[rows].astype(f32) + dot(heads, w_out, TN)
        enc_ref[rows] = enc
        unit, inverse = normalize(enc)
        unit = unit.astype(bf16)
        unit_ref[rows] = unit
        tail_ref[height:, b * B : (b + 1) * B] = jnp.broadcast_to(inverse, (B, 128)).T[0:8]
        both = dot(unit, w_layer, NT).astype(bf16)
        for message in messages:
            message[rows] = both[:, : 2 * D]
        queries = (both[:, 2 * D :].astype(f32) * score_scale).astype(bf16)
        cot = gathered_ref[half * b : half * (b + 1), D + D // 2 :, :].reshape(B, C)
        grads = dot(cot, wl_ref[...], NT).astype(bf16)
        messages[b][2 * B : 3 * B] = jnp.concatenate([queries, grads], axis=1)
    tail_ref[:height] = enc_ref[pl.ds(pl.multiple_of(at_ref[0] * height, height), height), :]
    row = lax.broadcasted_iota(jnp.int32, (8, 128), 0)
    table = jnp.zeros((8, 128), f32)
    for b in range(2):
        for n in range(3):
            table = jnp.where(row == 3 * b + n, bias_ref[b, n], table)
    high = table.astype(bf16).astype(f32)
    rest = table - high
    middle = rest.astype(bf16).astype(f32)
    tail = [high, middle, rest - middle, jnp.zeros((8, 128), f32)]
    for message in messages:
        message[3 * B : 3 * B + 32] = jnp.concatenate(tail, axis=0).astype(bf16)


def side_kernel(
    gathered_ref, unit_ref, tail_ref, wo_ref,
    cot_ref, unit_out_ref, inv_out_ref, sum_ref, half_ref, sem_ref,
):
    copy = pltpu.make_async_copy(gathered_ref.at[:, D : D + D // 2, :], half_ref, sem_ref)
    copy.start()
    half = gathered_ref.shape[0] // 2
    weight = wo_ref[...]
    for b in range(2):
        rows = slice(b * B, (b + 1) * B)
        cot = gathered_ref[half * b : half * (b + 1), D + D // 2 :, :].reshape(B, C)
        cot_ref[b] = dot(weight, cot, NT)
        unit_out_ref[b] = dot(weight, unit_ref[rows], NT)
        inv_out_ref[b] = tail_ref[tail_ref.shape[0] - 8 :, b * B : (b + 1) * B]
    sum_ref[...] = jnp.broadcast_to(
        jnp.sum(weight.astype(f32), axis=1, keepdims=True), sum_ref.shape
    )
    copy.wait()


def layer_kernel(
    low_ref, high_ref, left_ref, right_ref, unit_ref, wq_ref, wk_ref, wv_ref, gathered_ref,
    send_ref,
):
    zero = jnp.zeros((B, 2 * D), bf16)
    first = lax.broadcasted_iota(jnp.int32, (B, 2 * D), 1) < D

    def block(ref, b):
        return ref[b * B : (b + 1) * B]

    def stacked(ref):
        rows = block(ref, 2)
        return jnp.concatenate([jnp.where(first, rows, zero), jnp.where(first, zero, rows)], axis=0)

    def table(ref):
        tail = ref[3 * B : 3 * B + 32].astype(f32)
        return tail[0:8] + tail[8:16] + tail[16:24]

    kv = [block(ref, b) for ref in (left_ref, low_ref, right_ref) for b in range(2)]
    own_bias = table(low_ref)
    queries = [(left_ref, 1, table(left_ref)), (low_ref, 0, own_bias), (high_ref, 1, own_bias)]
    queries.append((right_ref, 0, table(right_ref)))
    heads = []
    grad_kv = [jnp.zeros((B, 2 * D), f32), jnp.zeros((B, 2 * D), f32)]
    grad_q = []
    for j, (ref, b, bias) in enumerate(queries):
        pair = stacked(ref)
        window = kv[j : j + 3]
        both = [dot(rows, pair, NT) for rows in window]
        scores = [both[n][:, :B] + bias[3 * b + n : 3 * b + n + 1] for n in range(3)]
        top = folded(jnp.maximum, jnp.concatenate(scores, axis=0))
        top = jnp.max(top, axis=0, keepdims=True)
        raised = [jnp.exp(s - top) for s in scores]
        low = sum(folded(jnp.add, r) for r in raised)
        scale = 1.0 / jnp.sum(low, axis=0, keepdims=True)
        soft = [r * scale for r in raised]
        inner = sum(folded(jnp.add, soft[n] * both[n][:, B:]) for n in range(3))
        inner = jnp.sum(inner, axis=0, keepdims=True)
        mixed = [
            jnp.concatenate(
                [(soft[n] * (both[n][:, B:] - inner)).astype(bf16), soft[n].astype(bf16)], axis=1
            )
            for n in range(3)
        ]
        for n in range(3):
            own = j + n - 2
            if 0 <= own < 2:
                grad_kv[own] = grad_kv[own] + dot(mixed[n], pair)
        if 1 <= j <= 2:
            back = sum(dot(mixed[n], window[n], TN) for n in range(3))
            grad_q.append((back[:B, :D] * score_scale).astype(bf16))
            heads.append(back[B:, D:].astype(bf16))
    parts = gathered_ref.shape[0]
    w_layer = jnp.concatenate([wk_ref[...], wv_ref[...], wq_ref[...]], axis=0)
    totals, stats = [], jnp.zeros((8, 128), f32)
    lane = lax.broadcasted_iota(jnp.int32, (B, 128), 1)
    for b in range(2):
        grad = jnp.concatenate([grad_kv[b].astype(bf16), grad_q[b]], axis=1)
        total = dot(grad, w_layer)
        first = jnp.mean(total, axis=1, keepdims=True)
        second = jnp.mean(total * unit_ref[b * B : (b + 1) * B].astype(f32), axis=1, keepdims=True)
        first_high = first.astype(bf16).astype(f32)
        second_high = second.astype(bf16).astype(f32)
        columns = (first_high, second_high, first - first_high, second - second_high)
        table_b = jnp.zeros((B, 128), f32)
        for k, column in enumerate(columns):
            table_b = jnp.where(lane == 4 * b + k, column, table_b)
        stats = stats + table_b.T[0:8]
        totals.append(total.astype(bf16))
    stats = jnp.concatenate([stats[:, :D], stats[:, D:]], axis=0).astype(bf16)
    total = jnp.concatenate(totals, axis=0)
    heads = jnp.concatenate(heads, axis=0)
    share = heads.shape[0] // parts
    for z in range(parts):
        piece = dot(gathered_ref[z, 0:D, :], total, NT).astype(bf16)
        for b in range(2):
            send_ref[z, b * D : (b + 1) * D] = piece[:, b * B : (b + 1) * B]
        rows = heads[z * share : (z + 1) * share]
        send_ref[z, 2 * D :] = jnp.concatenate([rows, stats], axis=1)


def grad_kernel(
    slot_ref, count_ref, bias_ref, me_ref, arrived_ref, cot_ref, unit_ref, inv_ref, sum_ref,
    grad_ref, send_ref, reader_ref, edge_ref,
):
    full = jnp.where(count_ref[0] == FULL, 0, 1)
    fill_tables(slot_ref, bias_ref, full, reader_ref, edge_ref)
    total = arrived_ref[0].astype(f32)
    for z in range(1, arrived_ref.shape[0]):
        total = total + arrived_ref[z].astype(f32)
    stats = total[2 * D :, D:]
    stats = jnp.concatenate([stats[0:8], stats[8:16]], axis=1)
    for b in range(2):
        first = stats[4 * b : 4 * b + 1] + stats[4 * b + 2 : 4 * b + 3]
        second = stats[4 * b + 1 : 4 * b + 2] + stats[4 * b + 3 : 4 * b + 4]
        inside = total[b * D : (b + 1) * D] - first * sum_ref[...] - second * unit_ref[b]
        grad_ref[b] = (cot_ref[b] + inv_ref[b][0:1] * inside).astype(bf16)
    shards = send_ref.shape[0]
    own = reader_ref.shape[0] - shards
    for p in range(shards):
        block = grad_ref[reader_ref[own + p]]
        send_ref[p] = jnp.where(me_ref[0] != p, block, jnp.zeros((D, B), bf16))


def final_kernel(
    send_ref, slot_ref, count_ref, bias_ref, norm_ref, kv_ref, early_ref, grads_ref,
    query_ref, heads_ref, lse_ref, grad_ref, out_ref, acc_ref, reader_ref, edge_ref,
    held_ref, block_ref, part_ref, sem_ref,
):
    copies = [
        pltpu.make_async_copy(early_ref, block_ref, sem_ref.at[0]),
        pltpu.make_async_copy(grads_ref, part_ref, sem_ref.at[1]),
        pltpu.make_async_copy(norm_ref, held_ref, sem_ref.at[2]),
    ]
    for copy in copies:
        copy.start()
    full = jnp.where(count_ref[0] == FULL, 0, 1)
    fill_tables(slot_ref, bias_ref, full, reader_ref, edge_ref)
    zero = jnp.zeros((D, B), bf16)

    def back(keys, query, heads, shift, grad):
        inner = jnp.sum(grad.astype(f32) * heads.astype(f32), axis=0, keepdims=True)
        pair = jnp.concatenate(
            [jnp.concatenate([query, zero], axis=1), jnp.concatenate([zero, grad], axis=1)], axis=0
        )
        both = dot(keys, pair)
        soft = jnp.exp(both[:, :B] - shift)
        mixed = jnp.concatenate(
            [(soft * (both[:, B:] - inner)).astype(bf16), soft.astype(bf16)], axis=1
        )
        return dot(mixed, pair, NT)

    group = 4

    def own_step(i, carry):
        parts = []
        for k in range(group):
            v = i * group + k
            m = reader_ref[v]
            shift = lse_ref[m][0:1] - edge_ref[v]
            parts.append(back(kv_ref[v], query_ref[m], heads_ref[m], shift, grad_ref[m]))
        for k in range(group):
            acc_ref[i * group + k] = parts[k]
        return carry

    lax.fori_loop(0, kv_ref.shape[0] // group, own_step, 0)

    def sent_step(i, carry):
        parts = []
        for k in range(group):
            r = i * group + k
            block = block_ref[r]
            tail = block[2 * D :].astype(f32)
            shift = tail[0:1] + tail[1:2] + tail[2:3]
            keys = kv_ref[send_ref[r]]
            parts.append(back(keys, block[:D], block[D : 2 * D], shift, part_ref[r]))
        for k in range(group):
            slot = send_ref[i * group + k]
            acc_ref[slot] = acc_ref[slot] + parts[k]
        return carry

    copies[0].wait()
    copies[1].wait()
    lax.fori_loop(0, block_ref.shape[0] // group, sent_step, 0)
    rows = acc_ref[...].reshape(norm_ref.shape[0], 2 * D).astype(bf16)
    copies[2].wait()
    shards, height = out_ref.shape[0], out_ref.shape[1]
    tile = 256
    for c in range(C // tile):
        part = dot(rows, held_ref[:, c * tile : (c + 1) * tile], TN).T
        per = tile // height
        out_ref[c * per : (c + 1) * per] = part.astype(bf16).reshape(per, height, 2 * D)


def output_kernel(me_ref, heads_ref, mine_ref, other_ref, tail_ref, out_ref):
    total = tail_ref[: out_ref.shape[0]]
    even = lax.rem(me_ref[0], 2) == 0
    half = D // 2
    for h in range(heads_ref.shape[0]):
        rows = heads_ref[h, 2 * D :][:, :D]
        low = jnp.where(even, mine_ref[h], other_ref[h])
        high = jnp.where(even, other_ref[h], mine_ref[h])
        total = total + dot(rows[:, :half], low) + dot(rows[:, half:], high)
    out_ref[...] = total.astype(bf16)


def sum_kernel(parts_ref, key_ref, value_ref):
    total = parts_ref[0].astype(f32)
    for i in range(1, parts_ref.shape[0]):
        total = total + parts_ref[i].astype(f32)
    key_ref[...] = total[:, :D]
    value_ref[...] = total[:, D:]


def exchange(array, axis):
    return lax.all_to_all(array, axis, split_axis=0, concat_axis=0, tiled=True)


def on_device(
    grid_feat,
    mesh_feat,
    query_weight,
    key_weight,
    value_weight,
    enc_out_weight,
    layer_query,
    layer_key,
    layer_value,
    layer_out_weight,
    enc_bias,
    layer_bias,
    send_list,
    edge_slot,
    edge_count,
    cotangent,
):
    shards = lax.axis_size("grid")
    parts = lax.axis_size("head")
    own = grid_feat.shape[0] // B
    share = cotangent.shape[0]
    send = send_list[0]
    enc_table = enc_bias[:, :, 0]
    layer_table = layer_bias[:, :, 0]
    shard_at = lax.axis_index("grid").astype(jnp.int32)[None]
    head_at = lax.axis_index("head").astype(jnp.int32)[None]
    forward = [(i, (i + 1) % shards) for i in range(shards)]
    backward = [(t, s) for s, t in forward]

    half = D // 2
    shared_rows = call(
        rows_kernel, struct((D + half + share, C), bf16), [VMEM] * 3, name="rows_part", mib=61
    )(enc_out_weight, layer_out_weight, cotangent)
    gathered = lax.all_gather(shared_rows, "head", axis=0, tiled=False)
    query_weight, key_weight, value_weight, layer_query, layer_key, layer_value = (
        weight.T
        for weight in (query_weight, key_weight, value_weight, layer_query, layer_key, layer_value)
    )

    grid_norm, own_kv, outgoing = grid_part(send, grid_feat, key_weight, value_weight, shards)
    arrived_kv = exchange(outgoing, "grid")
    queries = call(
        query_kernel, struct((2, D, B), bf16), [VMEM] * 2, name="query_part", data=1 << 20
    )(mesh_feat, query_weight)
    tables = [pltpu.SMEM((own + shards,), jnp.int32), pltpu.SMEM((own + shards,), f32)]
    enc_heads, lse, early = call(
        encoder_kernel,
        (
            struct((2, D, B), bf16),
            struct((2, 8, B), f32),
            struct((shards, 2 * D + 16, B), bf16),
        ),
        [SMEM] * 4 + [VMEM] * 3,
        [pltpu.VMEM((own + shards, B, 2 * D), bf16), pltpu.VMEM((FULL, B, B), f32)] + tables,
        name="encoder_part",
    )(edge_slot, edge_count, enc_table, shard_at, own_kv, arrived_kv, queries)
    arrived_early = exchange(early, "grid")
    all_heads = lax.all_gather(enc_heads, "head", axis=0, tiled=False)
    low, high, tail, unit = call(
        middle_kernel,
        (
            struct((3 * B + 32, 2 * D), bf16),
            struct((3 * B + 32, 2 * D), bf16),
            struct((share + 8, C), f32),
            struct((2 * B, C), bf16),
        ),
        [SMEM] * 2 + [VMEM] * 7,
        [pltpu.VMEM((2 * B, C), f32)],
        name="middle_part",
    )(
        head_at, layer_table, all_heads, gathered, mesh_feat, layer_query, layer_key, layer_value, layer_out_weight
    )
    left = lax.ppermute(high, "grid", forward)
    right = lax.ppermute(low, "grid", backward)
    cot_part, unit_part, inverse_row, weight_sum, half_mine = call(
        side_kernel,
        (
            struct((2, D, B), f32),
            struct((2, D, B), f32),
            struct((2, 8, B), f32),
            struct((D, B), f32),
            struct((parts, half, C), bf16),
        ),
        [VMEM] * 4,
        [pltpu.SemaphoreType.DMA],
        out_specs=(VMEM, VMEM, VMEM, VMEM, HBM),
        name="side_part",
    )(gathered, unit, tail, enc_out_weight)
    mixed = call(
        layer_kernel, struct((parts, 2 * D + share, B), bf16), [VMEM] * 9, name="layer_part"
    )(low, high, left, right, unit, layer_query, layer_key, layer_value, gathered)
    arrived_early, mixed = lax.optimization_barrier((arrived_early, mixed))
    arrived_grad = exchange(mixed, "head")
    grads, send_grads = call(
        grad_kernel,
        (struct((2, D, B), bf16), struct((shards, D, B), bf16)),
        [SMEM] * 4 + [VMEM] * 5,
        tables,
        name="grad_part",
    )(
        edge_slot, edge_count, enc_table, shard_at, arrived_grad, cot_part, unit_part,
        inverse_row, weight_sum,
    )
    arrived_grads = exchange(send_grads, "grid")
    half_other = lax.ppermute(half_mine, "grid", [(i, i ^ 1) for i in range(shards)])
    product = call(
        final_kernel,
        struct((shards, C // shards, 2 * D), bf16),
        [SMEM] * 4 + [HBM, VMEM, HBM, HBM] + [VMEM] * 4,
        [pltpu.VMEM((own, B, 2 * D), f32)]
        + tables
        + [
            pltpu.VMEM(grid_norm.shape, bf16),
            pltpu.VMEM((shards, 2 * D + 16, B), bf16),
            pltpu.VMEM((shards, D, B), bf16),
            pltpu.SemaphoreType.DMA((3,)),
        ],
        name="final_part",
        mib=61,
    )(
        send, edge_slot, edge_count, enc_table, grid_norm, own_kv, arrived_early, arrived_grads,
        queries, enc_heads, lse, grads,
    )
    pieces = exchange(product, "grid")
    mesh_out = call(
        output_kernel,
        struct((share, C), bf16),
        [SMEM] + [VMEM] * 4,
        name="output_part",
    )(shard_at, arrived_grad, half_mine, half_other, tail)
    key_grad, value_grad = call(
        sum_kernel,
        (struct((C // shards, D), f32), struct((C // shards, D), f32)),
        [VMEM],
        name="sum_part",
    )(pieces)
    return mesh_out, key_grad, value_grad


def solution(mesh):
    in_specs = (
        P("grid", None),
        P("grid", None),
        P(None, "head"),
        P(None, "head"),
        P(None, "head"),
        P("head", None),
        P(None, "head"),
        P(None, "head"),
        P(None, "head"),
        P("head", None),
        P("grid", None, "head"),
        P("grid", None, "head"),
        P("grid", None),
        P("grid", None),
        P("grid"),
        P(("grid", "head"), None),
    )
    out_specs = (P(("grid", "head"), None), P("grid", "head"), P("grid", "head"))
    return jax.shard_map(
        on_device, mesh=mesh, in_specs=in_specs, out_specs=out_specs, check_vma=False
    )
```

```python
import jax
import jax.numpy as jnp
from jax import lax
from jax.experimental import pallas as pl
from jax.experimental.pallas import tpu as pltpu
from jax.sharding import PartitionSpec as P

D = 64
B = 128
C = 1024
FULL = 30
REST = 9
epsilon = 1e-05
score_scale = 0.125

f32 = jnp.float32
bf16 = jnp.bfloat16

NN = (((1,), (0,)), ((), ()))
NT = (((1,), (1,)), ((), ()))
TN = (((0,), (0,)), ((), ()))

VMEM = pl.BlockSpec(memory_space=pltpu.VMEM)
SMEM = pl.BlockSpec(memory_space=pltpu.SMEM)
HBM = pl.BlockSpec(memory_space=pltpu.HBM)


def dot(left, right, dims=NN):
    return lax.dot_general(left, right, dims, preferred_element_type=f32)


def struct(shape, dtype):
    return jax.ShapeDtypeStruct(shape, dtype)


def call(body, outs, specs, scratch=(), mib=16, flops=1 << 26, data=1 << 22, name=None, **extra):
    return pl.pallas_call(
        body,
        out_shape=outs,
        in_specs=specs,
        scratch_shapes=list(scratch),
        compiler_params=pltpu.CompilerParams(vmem_limit_bytes=mib << 20),
        cost_estimate=pl.CostEstimate(flops=flops, bytes_accessed=data, transcendentals=0),
        name=name,
        **extra,
    )


def normalize(values):
    center = values - jnp.mean(values, axis=-1, keepdims=True)
    inverse = lax.rsqrt(jnp.mean(center * center, axis=-1, keepdims=True) + epsilon)
    return center * inverse, inverse


def grid_kernel(send_ref, feat_ref, wk_ref, wv_ref, norm_ref, kv_ref, out_ref):
    step = pl.program_id(0)
    unit, _ = normalize(feat_ref[...].astype(f32))
    rows = unit.astype(bf16)
    norm_ref[...] = rows
    weight = jnp.concatenate([wk_ref[...], wv_ref[...]], axis=0)
    both = dot(rows, weight, NT).astype(bf16)
    per = both.shape[0] // B
    for i in range(per):
        kv_ref[step * per + i] = both[i * B : (i + 1) * B]

    @pl.when(step == pl.num_programs(0) - 1)
    def _():
        for i in range(out_ref.shape[0]):
            out_ref[i] = kv_ref[send_ref[i]]


def grid_part(send, feat, wk, wv, shards):
    rows = feat.shape[0]
    steps = 4
    return pl.pallas_call(
        grid_kernel,
        grid=(steps,),
        out_shape=(
            struct((rows, C), bf16),
            struct((rows // B, B, 2 * D), bf16),
            struct((shards, B, 2 * D), bf16),
        ),
        in_specs=[
            SMEM,
            pl.BlockSpec((rows // steps, C), lambda i: (i, 0)),
            pl.BlockSpec((D, C), lambda i: (0, 0)),
            pl.BlockSpec((D, C), lambda i: (0, 0)),
        ],
        out_specs=(
            pl.BlockSpec((rows // steps, C), lambda i: (i, 0)),
            pl.BlockSpec((rows // B, B, 2 * D), lambda i: (0, 0, 0)),
            pl.BlockSpec((shards, B, 2 * D), lambda i: (0, 0, 0)),
        ),
        compiler_params=pltpu.CompilerParams(vmem_limit_bytes=60 << 20),
        cost_estimate=pl.CostEstimate(
            flops=1 << 28, bytes_accessed=6 << 20, transcendentals=0
        ),
        name="grid_part",
    )(send, feat, wk, wv)


def rows_kernel(wo_ref, wl_ref, cot_ref, out_ref):
    half = D // 2
    start = pl.multiple_of(lax.rem(lax.axis_index("grid"), 2) * half, half)
    out_ref[0:D] = wo_ref[...]
    out_ref[D : D + half] = wl_ref[pl.ds(start, half)]
    out_ref[D + half :] = cot_ref[...]


def query_kernel(mesh_ref, wq_ref, out_ref):
    for b in range(out_ref.shape[0]):
        unit, _ = normalize(mesh_ref[b * B : (b + 1) * B].astype(f32))
        rows = dot(wq_ref[...], unit.astype(bf16), NT).astype(bf16).astype(f32) * score_scale
        out_ref[b] = rows.astype(bf16)


def fill_pool(pool_ref, own_ref, arrived_ref):
    own = own_ref.shape[0]
    for i in range(own):
        pool_ref[i] = own_ref[i]
    for i in range(arrived_ref.shape[0]):
        pool_ref[own + i] = arrived_ref[i]


def folded(op, values):
    parts = [values[i * 8 : (i + 1) * 8] for i in range(values.shape[0] // 8)]
    while len(parts) > 1:
        parts = [
            op(parts[i], parts[i + 1]) if i + 1 < len(parts) else parts[i]
            for i in range(0, len(parts), 2)
        ]
    return parts[0]


def fill_tables(slot_ref, bias_ref, full, reader_ref, edge_ref):
    for i in range(reader_ref.shape[0]):
        reader_ref[i] = 0
        edge_ref[i] = 0.0
    for m, total in ((full, FULL), (1 - full, REST)):

        def put(e, carry, m=m):
            slot = slot_ref[m, e]
            reader_ref[slot] = m
            edge_ref[slot] = bias_ref[m, e]
            return carry

        lax.fori_loop(0, total, put, 0, unroll=3)


def encoder_kernel(
    slot_ref, count_ref, bias_ref, me_ref, own_ref, arrived_ref, query_ref,
    out_ref, lse_ref, early_ref, pool_ref, score_ref, reader_ref, edge_ref,
):
    fill_pool(pool_ref, own_ref, arrived_ref)
    full = jnp.where(count_ref[0] == FULL, 0, 1)
    fill_tables(slot_ref, bias_ref, full, reader_ref, edge_ref)
    for m, total in ((full, FULL), (1 - full, REST)):
        stack = jnp.concatenate([query_ref[m], jnp.zeros((D, B), bf16)], axis=0)

        def scores(e, top, m=m, stack=stack):
            value = dot(pool_ref[slot_ref[m, e]], stack) + bias_ref[m, e]
            score_ref[e] = value
            return jnp.maximum(top, folded(jnp.maximum, value))

        top = lax.fori_loop(0, total, scores, jnp.full((8, B), -jnp.inf, f32), unroll=3)
        top = jnp.max(top, axis=0, keepdims=True)

        def mix(e, carry, m=m, top=top):
            low, acc = carry
            raised = jnp.exp(score_ref[e] - top)
            acc = acc + dot(pool_ref[slot_ref[m, e]], raised.astype(bf16), TN)
            return low + folded(jnp.add, raised), acc

        low, acc = lax.fori_loop(
            0, total, mix, (jnp.zeros((8, B), f32), jnp.zeros((2 * D, B), f32)), unroll=3
        )
        low = jnp.sum(low, axis=0, keepdims=True)
        out_ref[m] = (acc[D:] / low).astype(bf16)
        lse_ref[m] = jnp.broadcast_to(top + jnp.log(low), (8, B))
    own = own_ref.shape[0]
    row = lax.broadcasted_iota(jnp.int32, (16, B), 0)
    for p in range(early_ref.shape[0]):
        m = reader_ref[own + p]
        other = me_ref[0] != p
        early_ref[p, 0:D] = jnp.where(other, query_ref[m], jnp.zeros((D, B), bf16))
        early_ref[p, D : 2 * D] = jnp.where(other, out_ref[m], jnp.zeros((D, B), bf16))
        shift = jnp.concatenate([lse_ref[m], lse_ref[m]], axis=0) - edge_ref[own + p]
        shift = jnp.where(other, shift, 0.0)
        high = shift.astype(bf16).astype(f32)
        middle = (shift - high).astype(bf16).astype(f32)
        rest = shift - high - middle
        tail = jnp.where(row == 0, high, jnp.where(row == 1, middle, jnp.where(row == 2, rest, 0.0)))
        early_ref[p, 2 * D :] = tail.astype(bf16)


def middle_kernel(
    at_ref, bias_ref, heads_ref, gathered_ref, mesh_ref, wq_ref, wk_ref, wv_ref, wl_ref,
    left_ref, right_ref, tail_ref, unit_ref, enc_ref,
):
    parts = heads_ref.shape[0]
    w_out = gathered_ref[:, 0:D, :].reshape(parts * D, C)
    w_layer = jnp.concatenate([wk_ref[...], wv_ref[...], wq_ref[...]], axis=0)
    half = parts // 2
    height = 2 * B // parts
    tail_ref[height:] = jnp.zeros((8, C), f32)
    messages = (left_ref, right_ref)
    heads = jnp.concatenate([heads_ref[:, b].reshape(parts * D, B) for b in range(2)], axis=1)
    enc_ref[...] = mesh_ref[...].astype(f32) + dot(heads, w_out, TN)
    for b in range(2):
        rows = slice(b * B, (b + 1) * B)
        enc = enc_ref[rows]
        unit, inverse = normalize(enc)
        unit = unit.astype(bf16)
        unit_ref[rows] = unit
        tail_ref[height:, b * B : (b + 1) * B] = jnp.broadcast_to(inverse, (B, 128)).T[0:8]
        both = dot(unit, w_layer, NT).astype(bf16)
        for message in messages:
            message[rows] = both[:, : 2 * D]
        queries = (both[:, 2 * D :].astype(f32) * score_scale).astype(bf16)
        cot = gathered_ref[half * b : half * (b + 1), D + D // 2 :, :].reshape(B, C)
        grads = dot(cot, wl_ref[...], NT).astype(bf16)
        messages[b][2 * B : 3 * B] = jnp.concatenate([queries, grads], axis=1)
    tail_ref[:height] = enc_ref[pl.ds(pl.multiple_of(at_ref[0] * height, height), height), :]
    row = lax.broadcasted_iota(jnp.int32, (8, 128), 0)
    table = jnp.zeros((8, 128), f32)
    for b in range(2):
        for n in range(3):
            table = jnp.where(row == 3 * b + n, bias_ref[b, n], table)
    high = table.astype(bf16).astype(f32)
    rest = table - high
    middle = rest.astype(bf16).astype(f32)
    tail = [high, middle, rest - middle, jnp.zeros((8, 128), f32)]
    for message in messages:
        message[3 * B : 3 * B + 32] = jnp.concatenate(tail, axis=0).astype(bf16)


def side_kernel(
    gathered_ref, unit_ref, tail_ref, wo_ref,
    cot_ref, unit_out_ref, inv_out_ref, sum_ref, half_ref, sem_ref,
):
    copy = pltpu.make_async_copy(gathered_ref.at[:, D : D + D // 2, :], half_ref, sem_ref)
    copy.start()
    half = gathered_ref.shape[0] // 2
    weight = wo_ref[...]
    for b in range(2):
        rows = slice(b * B, (b + 1) * B)
        cot = gathered_ref[half * b : half * (b + 1), D + D // 2 :, :].reshape(B, C)
        cot_ref[b] = dot(weight, cot, NT)
        unit_out_ref[b] = dot(weight, unit_ref[rows], NT)
        inv_out_ref[b] = tail_ref[tail_ref.shape[0] - 8 :, b * B : (b + 1) * B]
    sum_ref[...] = jnp.broadcast_to(
        jnp.sum(weight.astype(f32), axis=1, keepdims=True), sum_ref.shape
    )
    copy.wait()


def layer_kernel(
    low_ref, high_ref, left_ref, right_ref, unit_ref, wq_ref, wk_ref, wv_ref, gathered_ref,
    send_ref,
):
    zero = jnp.zeros((B, 2 * D), bf16)
    first = lax.broadcasted_iota(jnp.int32, (B, 2 * D), 1) < D

    def block(ref, b):
        return ref[b * B : (b + 1) * B]

    def stacked(ref):
        rows = block(ref, 2)
        return jnp.concatenate([jnp.where(first, rows, zero), jnp.where(first, zero, rows)], axis=0)

    def table(ref):
        tail = ref[3 * B : 3 * B + 32].astype(f32)
        return tail[0:8] + tail[8:16] + tail[16:24]

    kv = [block(ref, b) for ref in (left_ref, low_ref, right_ref) for b in range(2)]
    own_bias = table(low_ref)
    queries = [(left_ref, 1, table(left_ref)), (low_ref, 0, own_bias), (high_ref, 1, own_bias)]
    queries.append((right_ref, 0, table(right_ref)))
    heads = []
    grad_kv = [jnp.zeros((B, 2 * D), f32), jnp.zeros((B, 2 * D), f32)]
    grad_q = []
    for j, (ref, b, bias) in enumerate(queries):
        pair = stacked(ref)
        window = kv[j : j + 3]
        both = [dot(rows, pair, NT) for rows in window]
        scores = [both[n][:, :B] + bias[3 * b + n : 3 * b + n + 1] for n in range(3)]
        top = folded(jnp.maximum, jnp.concatenate(scores, axis=0))
        top = jnp.max(top, axis=0, keepdims=True)
        raised = [jnp.exp(s - top) for s in scores]
        low = sum(folded(jnp.add, r) for r in raised)
        scale = 1.0 / jnp.sum(low, axis=0, keepdims=True)
        soft = [r * scale for r in raised]
        inner = sum(folded(jnp.add, soft[n] * both[n][:, B:]) for n in range(3))
        inner = jnp.sum(inner, axis=0, keepdims=True)
        mixed = [
            jnp.concatenate(
                [(soft[n] * (both[n][:, B:] - inner)).astype(bf16), soft[n].astype(bf16)], axis=1
            )
            for n in range(3)
        ]
        for n in range(3):
            own = j + n - 2
            if 0 <= own < 2:
                grad_kv[own] = grad_kv[own] + dot(mixed[n], pair)
        if 1 <= j <= 2:
            back = sum(dot(mixed[n], window[n], TN) for n in range(3))
            grad_q.append((back[:B, :D] * score_scale).astype(bf16))
            heads.append(back[B:, D:].astype(bf16))
    parts = gathered_ref.shape[0]
    w_layer = jnp.concatenate([wk_ref[...], wv_ref[...], wq_ref[...]], axis=0)
    totals, stats = [], jnp.zeros((8, 128), f32)
    lane = lax.broadcasted_iota(jnp.int32, (B, 128), 1)
    for b in range(2):
        grad = jnp.concatenate([grad_kv[b].astype(bf16), grad_q[b]], axis=1)
        total = dot(grad, w_layer)
        first = jnp.mean(total, axis=1, keepdims=True)
        second = jnp.mean(total * unit_ref[b * B : (b + 1) * B].astype(f32), axis=1, keepdims=True)
        first_high = first.astype(bf16).astype(f32)
        second_high = second.astype(bf16).astype(f32)
        columns = (first_high, second_high, first - first_high, second - second_high)
        table_b = jnp.zeros((B, 128), f32)
        for k, column in enumerate(columns):
            table_b = jnp.where(lane == 4 * b + k, column, table_b)
        stats = stats + table_b.T[0:8]
        totals.append(total.astype(bf16))
    stats = jnp.concatenate([stats[:, :D], stats[:, D:]], axis=0).astype(bf16)
    total = jnp.concatenate(totals, axis=0)
    heads = jnp.concatenate(heads, axis=0)
    share = heads.shape[0] // parts
    group = 4
    for start in range(0, parts, group):
        weight = gathered_ref[start : start + group, 0:D, :].reshape(group * D, C)
        pieces = dot(weight, total, NT).astype(bf16)
        for k in range(group):
            for b in range(2):
                block = pieces[k * D : (k + 1) * D, b * B : (b + 1) * B]
                send_ref[start + k, b * D : (b + 1) * D] = block
    for z in range(parts):
        rows = heads[z * share : (z + 1) * share]
        send_ref[z, 2 * D :] = jnp.concatenate([rows, stats], axis=1)


def grad_kernel(
    slot_ref, count_ref, bias_ref, me_ref, arrived_ref, cot_ref, unit_ref, inv_ref, sum_ref,
    grad_ref, send_ref, reader_ref, edge_ref,
):
    full = jnp.where(count_ref[0] == FULL, 0, 1)
    fill_tables(slot_ref, bias_ref, full, reader_ref, edge_ref)
    total = arrived_ref[0].astype(f32)
    for z in range(1, arrived_ref.shape[0]):
        total = total + arrived_ref[z].astype(f32)
    stats = total[2 * D :, D:]
    stats = jnp.concatenate([stats[0:8], stats[8:16]], axis=1)
    for b in range(2):
        first = stats[4 * b : 4 * b + 1] + stats[4 * b + 2 : 4 * b + 3]
        second = stats[4 * b + 1 : 4 * b + 2] + stats[4 * b + 3 : 4 * b + 4]
        inside = total[b * D : (b + 1) * D] - first * sum_ref[...] - second * unit_ref[b]
        grad_ref[b] = (cot_ref[b] + inv_ref[b][0:1] * inside).astype(bf16)
    shards = send_ref.shape[0]
    own = reader_ref.shape[0] - shards
    for p in range(shards):
        block = grad_ref[reader_ref[own + p]]
        send_ref[p] = jnp.where(me_ref[0] != p, block, jnp.zeros((D, B), bf16))


def final_kernel(
    send_ref, slot_ref, count_ref, bias_ref, norm_ref, kv_ref, early_ref, grads_ref,
    query_ref, heads_ref, lse_ref, grad_ref, out_ref, acc_ref, reader_ref, edge_ref,
    held_ref, block_ref, part_ref, sem_ref,
):
    copies = [
        pltpu.make_async_copy(early_ref, block_ref, sem_ref.at[0]),
        pltpu.make_async_copy(grads_ref, part_ref, sem_ref.at[1]),
        pltpu.make_async_copy(norm_ref, held_ref, sem_ref.at[2]),
    ]
    for copy in copies:
        copy.start()
    full = jnp.where(count_ref[0] == FULL, 0, 1)
    fill_tables(slot_ref, bias_ref, full, reader_ref, edge_ref)
    zero = jnp.zeros((D, B), bf16)

    def back(keys, query, heads, shift, grad):
        inner = jnp.sum(grad.astype(f32) * heads.astype(f32), axis=0, keepdims=True)
        pair = jnp.concatenate(
            [jnp.concatenate([query, zero], axis=1), jnp.concatenate([zero, grad], axis=1)], axis=0
        )
        both = dot(keys, pair)
        soft = jnp.exp(both[:, :B] - shift)
        mixed = jnp.concatenate(
            [(soft * (both[:, B:] - inner)).astype(bf16), soft.astype(bf16)], axis=1
        )
        return dot(mixed, pair, NT)

    def own_step(v, carry):
        m = reader_ref[v]
        shift = lse_ref[m][0:1] - edge_ref[v]
        acc_ref[v] = back(kv_ref[v], query_ref[m], heads_ref[m], shift, grad_ref[m])
        return carry

    lax.fori_loop(0, kv_ref.shape[0], own_step, 0, unroll=4)

    def sent_step(r, carry):
        slot = send_ref[r]
        block = block_ref[r]
        tail = block[2 * D :].astype(f32)
        shift = tail[0:1] + tail[1:2] + tail[2:3]
        part = back(kv_ref[slot], block[:D], block[D : 2 * D], shift, part_ref[r])
        acc_ref[slot] = acc_ref[slot] + part
        return carry

    copies[0].wait()
    copies[1].wait()
    lax.fori_loop(0, block_ref.shape[0], sent_step, 0, unroll=4)
    rows = acc_ref[...].reshape(norm_ref.shape[0], 2 * D).astype(bf16)
    copies[2].wait()
    shards, height = out_ref.shape[0], out_ref.shape[1]
    tile = 512
    for c in range(C // tile):
        part = dot(rows, held_ref[:, c * tile : (c + 1) * tile], TN).T
        per = tile // height
        out_ref[c * per : (c + 1) * per] = part.astype(bf16).reshape(per, height, 2 * D)


def output_kernel(me_ref, heads_ref, mine_ref, other_ref, tail_ref, out_ref):
    total = tail_ref[: out_ref.shape[0]]
    even = lax.rem(me_ref[0], 2) == 0
    half = D // 2
    for h in range(heads_ref.shape[0]):
        rows = heads_ref[h, 2 * D :][:, :D]
        low = jnp.where(even, mine_ref[h], other_ref[h])
        high = jnp.where(even, other_ref[h], mine_ref[h])
        total = total + dot(rows[:, :half], low) + dot(rows[:, half:], high)
    out_ref[...] = total.astype(bf16)


def sum_kernel(parts_ref, key_ref, value_ref):
    total = parts_ref[0].astype(f32)
    for i in range(1, parts_ref.shape[0]):
        total = total + parts_ref[i].astype(f32)
    key_ref[...] = total[:, :D]
    value_ref[...] = total[:, D:]


def exchange(array, axis):
    return lax.all_to_all(array, axis, split_axis=0, concat_axis=0, tiled=True)


def on_device(
    grid_feat,
    mesh_feat,
    query_weight,
    key_weight,
    value_weight,
    enc_out_weight,
    layer_query,
    layer_key,
    layer_value,
    layer_out_weight,
    enc_bias,
    layer_bias,
    send_list,
    edge_slot,
    edge_count,
    cotangent,
):
    shards = lax.axis_size("grid")
    parts = lax.axis_size("head")
    own = grid_feat.shape[0] // B
    share = cotangent.shape[0]
    send = send_list[0]
    enc_table = enc_bias[:, :, 0]
    layer_table = layer_bias[:, :, 0]
    shard_at = lax.axis_index("grid").astype(jnp.int32)[None]
    head_at = lax.axis_index("head").astype(jnp.int32)[None]
    forward = [(i, (i + 1) % shards) for i in range(shards)]
    backward = [(t, s) for s, t in forward]

    half = D // 2
    shared_rows = call(
        rows_kernel, struct((D + half + share, C), bf16), [VMEM] * 3, name="rows_part", mib=61
    )(enc_out_weight, layer_out_weight, cotangent)
    gathered = lax.all_gather(shared_rows, "head", axis=0, tiled=False)
    query_weight, key_weight, value_weight, layer_query, layer_key, layer_value = (
        weight.T
        for weight in (query_weight, key_weight, value_weight, layer_query, layer_key, layer_value)
    )

    grid_norm, own_kv, outgoing = grid_part(send, grid_feat, key_weight, value_weight, shards)
    arrived_kv = exchange(outgoing, "grid")
    queries = call(
        query_kernel, struct((2, D, B), bf16), [VMEM] * 2, name="query_part", data=1 << 20
    )(mesh_feat, query_weight)
    tables = [pltpu.SMEM((own + shards,), jnp.int32), pltpu.SMEM((own + shards,), f32)]
    enc_heads, lse, early = call(
        encoder_kernel,
        (
            struct((2, D, B), bf16),
            struct((2, 8, B), f32),
            struct((shards, 2 * D + 16, B), bf16),
        ),
        [SMEM] * 4 + [VMEM] * 3,
        [pltpu.VMEM((own + shards, B, 2 * D), bf16), pltpu.VMEM((FULL, B, B), f32)] + tables,
        name="encoder_part",
    )(edge_slot, edge_count, enc_table, shard_at, own_kv, arrived_kv, queries)
    arrived_early = exchange(early, "grid")
    all_heads = lax.all_gather(enc_heads, "head", axis=0, tiled=False)
    low, high, tail, unit = call(
        middle_kernel,
        (
            struct((3 * B + 32, 2 * D), bf16),
            struct((3 * B + 32, 2 * D), bf16),
            struct((share + 8, C), f32),
            struct((2 * B, C), bf16),
        ),
        [SMEM] * 2 + [VMEM] * 7,
        [pltpu.VMEM((2 * B, C), f32)],
        name="middle_part",
    )(
        head_at, layer_table, all_heads, gathered, mesh_feat, layer_query, layer_key, layer_value, layer_out_weight
    )
    left = lax.ppermute(high, "grid", forward)
    right = lax.ppermute(low, "grid", backward)
    cot_part, unit_part, inverse_row, weight_sum, half_mine = call(
        side_kernel,
        (
            struct((2, D, B), f32),
            struct((2, D, B), f32),
            struct((2, 8, B), f32),
            struct((D, B), f32),
            struct((parts, half, C), bf16),
        ),
        [VMEM] * 4,
        [pltpu.SemaphoreType.DMA],
        out_specs=(VMEM, VMEM, VMEM, VMEM, HBM),
        name="side_part",
    )(gathered, unit, tail, enc_out_weight)
    mixed = call(
        layer_kernel, struct((parts, 2 * D + share, B), bf16), [VMEM] * 9, name="layer_part"
    )(low, high, left, right, unit, layer_query, layer_key, layer_value, gathered)
    arrived_early, mixed = lax.optimization_barrier((arrived_early, mixed))
    arrived_grad = exchange(mixed, "head")
    grads, send_grads = call(
        grad_kernel,
        (struct((2, D, B), bf16), struct((shards, D, B), bf16)),
        [SMEM] * 4 + [VMEM] * 5,
        tables,
        name="grad_part",
    )(
        edge_slot, edge_count, enc_table, shard_at, arrived_grad, cot_part, unit_part,
        inverse_row, weight_sum,
    )
    arrived_grads = exchange(send_grads, "grid")
    half_other = lax.ppermute(half_mine, "grid", [(i, i ^ 1) for i in range(shards)])
    product = call(
        final_kernel,
        struct((shards, C // shards, 2 * D), bf16),
        [SMEM] * 4 + [HBM, VMEM, HBM, HBM] + [VMEM] * 4,
        [pltpu.VMEM((own, B, 2 * D), f32)]
        + tables
        + [
            pltpu.VMEM(grid_norm.shape, bf16),
            pltpu.VMEM((shards, 2 * D + 16, B), bf16),
            pltpu.VMEM((shards, D, B), bf16),
            pltpu.SemaphoreType.DMA((3,)),
        ],
        name="final_part",
        mib=61,
    )(
        send, edge_slot, edge_count, enc_table, grid_norm, own_kv, arrived_early, arrived_grads,
        queries, enc_heads, lse, grads,
    )
    pieces = exchange(product, "grid")
    mesh_out = call(
        output_kernel,
        struct((share, C), bf16),
        [SMEM] + [VMEM] * 4,
        name="output_part",
    )(shard_at, arrived_grad, half_mine, half_other, tail)
    key_grad, value_grad = call(
        sum_kernel,
        (struct((C // shards, D), f32), struct((C // shards, D), f32)),
        [VMEM],
        name="sum_part",
    )(pieces)
    return mesh_out, key_grad, value_grad


def solution(mesh):
    in_specs = (
        P("grid", None),
        P("grid", None),
        P(None, "head"),
        P(None, "head"),
        P(None, "head"),
        P("head", None),
        P(None, "head"),
        P(None, "head"),
        P(None, "head"),
        P("head", None),
        P("grid", None, "head"),
        P("grid", None, "head"),
        P("grid", None),
        P("grid", None),
        P("grid"),
        P(("grid", "head"), None),
    )
    out_specs = (P(("grid", "head"), None), P("grid", "head"), P("grid", "head"))
    return jax.shard_map(
        on_device, mesh=mesh, in_specs=in_specs, out_specs=out_specs, check_vma=False
    )
```

```python
import jax
import jax.numpy as jnp
from jax import lax
from jax.experimental import pallas as pl
from jax.experimental.pallas import tpu as pltpu
from jax.sharding import PartitionSpec as P

D = 64
B = 128
C = 1024
FULL = 30
REST = 9
epsilon = 1e-05
score_scale = 0.125

f32 = jnp.float32
bf16 = jnp.bfloat16

NN = (((1,), (0,)), ((), ()))
NT = (((1,), (1,)), ((), ()))
TN = (((0,), (0,)), ((), ()))

VMEM = pl.BlockSpec(memory_space=pltpu.VMEM)
SMEM = pl.BlockSpec(memory_space=pltpu.SMEM)
HBM = pl.BlockSpec(memory_space=pltpu.HBM)


def dot(left, right, dims=NN):
    return lax.dot_general(left, right, dims, preferred_element_type=f32)


def struct(shape, dtype):
    return jax.ShapeDtypeStruct(shape, dtype)


def call(body, outs, specs, scratch=(), mib=16, flops=1 << 26, data=1 << 22, name=None, **extra):
    return pl.pallas_call(
        body,
        out_shape=outs,
        in_specs=specs,
        scratch_shapes=list(scratch),
        compiler_params=pltpu.CompilerParams(vmem_limit_bytes=mib << 20),
        cost_estimate=pl.CostEstimate(flops=flops, bytes_accessed=data, transcendentals=0),
        name=name,
        **extra,
    )


def normalize(values):
    center = values - jnp.mean(values, axis=-1, keepdims=True)
    inverse = lax.rsqrt(jnp.mean(center * center, axis=-1, keepdims=True) + epsilon)
    return center * inverse, inverse


def grid_kernel(send_ref, feat_ref, wk_ref, wv_ref, norm_ref, kv_ref, out_ref):
    step = pl.program_id(0)
    unit, _ = normalize(feat_ref[...].astype(f32))
    rows = unit.astype(bf16)
    norm_ref[...] = rows
    weight = jnp.concatenate([wk_ref[...], wv_ref[...]], axis=0)
    both = dot(rows, weight, NT).astype(bf16)
    per = both.shape[0] // B
    for i in range(per):
        kv_ref[step * per + i] = both[i * B : (i + 1) * B]

    @pl.when(step == pl.num_programs(0) - 1)
    def _():
        for i in range(out_ref.shape[0]):
            out_ref[i] = kv_ref[send_ref[i]]


def grid_part(send, feat, wk, wv, shards):
    rows = feat.shape[0]
    steps = 4
    return pl.pallas_call(
        grid_kernel,
        grid=(steps,),
        out_shape=(
            struct((rows, C), bf16),
            struct((rows // B, B, 2 * D), bf16),
            struct((shards, B, 2 * D), bf16),
        ),
        in_specs=[
            SMEM,
            pl.BlockSpec((rows // steps, C), lambda i: (i, 0)),
            pl.BlockSpec((D, C), lambda i: (0, 0)),
            pl.BlockSpec((D, C), lambda i: (0, 0)),
        ],
        out_specs=(
            pl.BlockSpec((rows // steps, C), lambda i: (i, 0)),
            pl.BlockSpec((rows // B, B, 2 * D), lambda i: (0, 0, 0)),
            pl.BlockSpec((shards, B, 2 * D), lambda i: (0, 0, 0)),
        ),
        compiler_params=pltpu.CompilerParams(vmem_limit_bytes=60 << 20),
        cost_estimate=pl.CostEstimate(
            flops=1 << 28, bytes_accessed=6 << 20, transcendentals=0
        ),
        name="grid_part",
    )(send, feat, wk, wv)


def rows_kernel(wo_ref, wl_ref, cot_ref, out_ref):
    half = D // 2
    start = pl.multiple_of(lax.rem(lax.axis_index("grid"), 2) * half, half)
    out_ref[0:D] = wo_ref[...]
    out_ref[D : D + half] = wl_ref[pl.ds(start, half)]
    out_ref[D + half :] = cot_ref[...]


def query_kernel(mesh_ref, wq_ref, out_ref):
    for b in range(out_ref.shape[0]):
        unit, _ = normalize(mesh_ref[b * B : (b + 1) * B].astype(f32))
        rows = dot(wq_ref[...], unit.astype(bf16), NT).astype(bf16).astype(f32) * score_scale
        out_ref[b] = rows.astype(bf16)


def fill_pool(pool_ref, own_ref, arrived_ref):
    own = own_ref.shape[0]
    for i in range(own):
        pool_ref[i] = own_ref[i]
    for i in range(arrived_ref.shape[0]):
        pool_ref[own + i] = arrived_ref[i]


def folded(op, values):
    parts = [values[i * 8 : (i + 1) * 8] for i in range(values.shape[0] // 8)]
    while len(parts) > 1:
        parts = [
            op(parts[i], parts[i + 1]) if i + 1 < len(parts) else parts[i]
            for i in range(0, len(parts), 2)
        ]
    return parts[0]


def fill_tables(slot_ref, bias_ref, full, reader_ref, edge_ref):
    for i in range(reader_ref.shape[0]):
        reader_ref[i] = 0
        edge_ref[i] = 0.0
    for m, total in ((full, FULL), (1 - full, REST)):

        def put(e, carry, m=m):
            slot = slot_ref[m, e]
            reader_ref[slot] = m
            edge_ref[slot] = bias_ref[m, e]
            return carry

        lax.fori_loop(0, total, put, 0, unroll=3)


def encoder_kernel(
    slot_ref, count_ref, bias_ref, me_ref, own_ref, arrived_ref, query_ref,
    out_ref, lse_ref, early_ref, pool_ref, score_ref, reader_ref, edge_ref,
):
    fill_pool(pool_ref, own_ref, arrived_ref)
    full = jnp.where(count_ref[0] == FULL, 0, 1)
    fill_tables(slot_ref, bias_ref, full, reader_ref, edge_ref)
    for m, total in ((full, FULL), (1 - full, REST)):
        stack = jnp.concatenate([query_ref[m], jnp.zeros((D, B), bf16)], axis=0)

        def scores(e, top, m=m, stack=stack):
            value = dot(pool_ref[slot_ref[m, e]], stack) + bias_ref[m, e]
            score_ref[e] = value
            return jnp.maximum(top, folded(jnp.maximum, value))

        top = lax.fori_loop(0, total, scores, jnp.full((8, B), -jnp.inf, f32), unroll=3)
        top = jnp.max(top, axis=0, keepdims=True)

        def mix(e, carry, m=m, top=top):
            low, acc = carry
            raised = jnp.exp(score_ref[e] - top)
            acc = acc + dot(pool_ref[slot_ref[m, e]], raised.astype(bf16), TN)
            return low + folded(jnp.add, raised), acc

        low, acc = lax.fori_loop(
            0, total, mix, (jnp.zeros((8, B), f32), jnp.zeros((2 * D, B), f32)), unroll=3
        )
        low = jnp.sum(low, axis=0, keepdims=True)
        out_ref[m] = (acc[D:] / low).astype(bf16)
        lse_ref[m] = jnp.broadcast_to(top + jnp.log(low), (8, B))
    own = own_ref.shape[0]
    row = lax.broadcasted_iota(jnp.int32, (16, B), 0)
    for p in range(early_ref.shape[0]):
        m = reader_ref[own + p]
        other = me_ref[0] != p
        early_ref[p, 0:D] = jnp.where(other, query_ref[m], jnp.zeros((D, B), bf16))
        early_ref[p, D : 2 * D] = jnp.where(other, out_ref[m], jnp.zeros((D, B), bf16))
        shift = jnp.concatenate([lse_ref[m], lse_ref[m]], axis=0) - edge_ref[own + p]
        shift = jnp.where(other, shift, 0.0)
        high = shift.astype(bf16).astype(f32)
        middle = (shift - high).astype(bf16).astype(f32)
        rest = shift - high - middle
        tail = jnp.where(row == 0, high, jnp.where(row == 1, middle, jnp.where(row == 2, rest, 0.0)))
        early_ref[p, 2 * D :] = tail.astype(bf16)


def middle_kernel(
    at_ref, bias_ref, heads_ref, gathered_ref, mesh_ref, wq_ref, wk_ref, wv_ref, wl_ref,
    left_ref, right_ref, tail_ref, unit_ref, enc_ref,
):
    parts = heads_ref.shape[0]
    w_out = gathered_ref[:, 0:D, :].reshape(parts * D, C)
    w_layer = jnp.concatenate([wk_ref[...], wv_ref[...], wq_ref[...]], axis=0)
    height = 2 * B // parts
    tail_ref[height:] = jnp.zeros((8, C), f32)
    messages = (left_ref, right_ref)
    heads = jnp.concatenate([heads_ref[:, b].reshape(parts * D, B) for b in range(2)], axis=1)
    enc_ref[...] = mesh_ref[...].astype(f32) + dot(heads, w_out, TN)
    for b in range(2):
        rows = slice(b * B, (b + 1) * B)
        enc = enc_ref[rows]
        unit, inverse = normalize(enc)
        unit = unit.astype(bf16)
        unit_ref[rows] = unit
        tail_ref[height:, b * B : (b + 1) * B] = jnp.broadcast_to(inverse, (B, 128)).T[0:8]
    both = dot(unit_ref[...], w_layer, NT).astype(bf16)
    cot = gathered_ref[:, D + D // 2 :, :].reshape(2 * B, C)
    grads = dot(cot, wl_ref[...], NT).astype(bf16)
    queries = (both[:, 2 * D :].astype(f32) * score_scale).astype(bf16)
    for b in range(2):
        rows = slice(b * B, (b + 1) * B)
        messages[b][0 : 2 * B] = both[:, : 2 * D]
        messages[b][2 * B : 3 * B] = jnp.concatenate([queries[rows], grads[rows]], axis=1)
    tail_ref[:height] = enc_ref[pl.ds(pl.multiple_of(at_ref[0] * height, height), height), :]
    row = lax.broadcasted_iota(jnp.int32, (8, 128), 0)
    table = jnp.zeros((8, 128), f32)
    for b in range(2):
        for n in range(3):
            table = jnp.where(row == 3 * b + n, bias_ref[b, n], table)
    high = table.astype(bf16).astype(f32)
    rest = table - high
    middle = rest.astype(bf16).astype(f32)
    tail = [high, middle, rest - middle, jnp.zeros((8, 128), f32)]
    for message in messages:
        message[3 * B : 3 * B + 32] = jnp.concatenate(tail, axis=0).astype(bf16)


def side_kernel(
    gathered_ref, unit_ref, tail_ref, wo_ref,
    cot_ref, unit_out_ref, inv_out_ref, sum_ref, half_ref, sem_ref,
):
    copy = pltpu.make_async_copy(gathered_ref.at[:, D : D + D // 2, :], half_ref, sem_ref)
    copy.start()
    half = gathered_ref.shape[0] // 2
    weight = wo_ref[...]
    for b in range(2):
        rows = slice(b * B, (b + 1) * B)
        cot = gathered_ref[half * b : half * (b + 1), D + D // 2 :, :].reshape(B, C)
        cot_ref[b] = dot(weight, cot, NT)
        unit_out_ref[b] = dot(weight, unit_ref[rows], NT)
        inv_out_ref[b] = tail_ref[tail_ref.shape[0] - 8 :, b * B : (b + 1) * B]
    sum_ref[...] = jnp.broadcast_to(
        jnp.sum(weight.astype(f32), axis=1, keepdims=True), sum_ref.shape
    )
    copy.wait()


def layer_kernel(
    low_ref, high_ref, left_ref, right_ref, unit_ref, wq_ref, wk_ref, wv_ref, gathered_ref,
    send_ref,
):
    zero = jnp.zeros((B, 2 * D), bf16)
    first = lax.broadcasted_iota(jnp.int32, (B, 2 * D), 1) < D

    def block(ref, b):
        return ref[b * B : (b + 1) * B]

    def stacked(ref):
        rows = block(ref, 2)
        return jnp.concatenate([jnp.where(first, rows, zero), jnp.where(first, zero, rows)], axis=0)

    def table(ref):
        tail = ref[3 * B : 3 * B + 32].astype(f32)
        return tail[0:8] + tail[8:16] + tail[16:24]

    kv = [block(ref, b) for ref in (left_ref, low_ref, right_ref) for b in range(2)]
    own_bias = table(low_ref)
    queries = [(left_ref, 1, table(left_ref)), (low_ref, 0, own_bias), (high_ref, 1, own_bias)]
    queries.append((right_ref, 0, table(right_ref)))
    heads = []
    grad_kv = [jnp.zeros((B, 2 * D), f32), jnp.zeros((B, 2 * D), f32)]
    grad_q = []
    for j, (ref, b, bias) in enumerate(queries):
        pair = stacked(ref)
        window = kv[j : j + 3]
        both = [dot(rows, pair, NT) for rows in window]
        scores = [both[n][:, :B] + bias[3 * b + n : 3 * b + n + 1] for n in range(3)]
        top = folded(jnp.maximum, jnp.concatenate(scores, axis=0))
        top = jnp.max(top, axis=0, keepdims=True)
        raised = [jnp.exp(s - top) for s in scores]
        low = sum(folded(jnp.add, r) for r in raised)
        scale = 1.0 / jnp.sum(low, axis=0, keepdims=True)
        soft = [r * scale for r in raised]
        inner = sum(folded(jnp.add, soft[n] * both[n][:, B:]) for n in range(3))
        inner = jnp.sum(inner, axis=0, keepdims=True)
        mixed = [
            jnp.concatenate(
                [(soft[n] * (both[n][:, B:] - inner)).astype(bf16), soft[n].astype(bf16)], axis=1
            )
            for n in range(3)
        ]
        for n in range(3):
            own = j + n - 2
            if 0 <= own < 2:
                grad_kv[own] = grad_kv[own] + dot(mixed[n], pair)
        if 1 <= j <= 2:
            back = sum(dot(mixed[n], window[n], TN) for n in range(3))
            grad_q.append((back[:B, :D] * score_scale).astype(bf16))
            heads.append(back[B:, D:].astype(bf16))
    parts = gathered_ref.shape[0]
    w_layer = jnp.concatenate([wk_ref[...], wv_ref[...], wq_ref[...]], axis=0)
    totals, stats = [], jnp.zeros((8, 128), f32)
    lane = lax.broadcasted_iota(jnp.int32, (B, 128), 1)
    for b in range(2):
        grad = jnp.concatenate([grad_kv[b].astype(bf16), grad_q[b]], axis=1)
        total = dot(grad, w_layer)
        first = jnp.mean(total, axis=1, keepdims=True)
        second = jnp.mean(total * unit_ref[b * B : (b + 1) * B].astype(f32), axis=1, keepdims=True)
        first_high = first.astype(bf16).astype(f32)
        second_high = second.astype(bf16).astype(f32)
        columns = (first_high, second_high, first - first_high, second - second_high)
        table_b = jnp.zeros((B, 128), f32)
        for k, column in enumerate(columns):
            table_b = jnp.where(lane == 4 * b + k, column, table_b)
        stats = stats + table_b.T[0:8]
        totals.append(total.astype(bf16))
    stats = jnp.concatenate([stats[:, :D], stats[:, D:]], axis=0).astype(bf16)
    total = jnp.concatenate(totals, axis=0)
    heads = jnp.concatenate(heads, axis=0)
    share = heads.shape[0] // parts
    group = 8
    for start in range(0, parts, group):
        weight = gathered_ref[start : start + group, 0:D, :].reshape(group * D, C)
        pieces = dot(weight, total, NT).astype(bf16)
        for k in range(group):
            for b in range(2):
                block = pieces[k * D : (k + 1) * D, b * B : (b + 1) * B]
                send_ref[start + k, b * D : (b + 1) * D] = block
    for z in range(parts):
        rows = heads[z * share : (z + 1) * share]
        send_ref[z, 2 * D :] = jnp.concatenate([rows, stats], axis=1)


def grad_kernel(
    slot_ref, count_ref, bias_ref, me_ref, arrived_ref, cot_ref, unit_ref, inv_ref, sum_ref,
    grad_ref, send_ref, reader_ref, edge_ref,
):
    full = jnp.where(count_ref[0] == FULL, 0, 1)
    fill_tables(slot_ref, bias_ref, full, reader_ref, edge_ref)
    total = arrived_ref[0].astype(f32)
    for z in range(1, arrived_ref.shape[0]):
        total = total + arrived_ref[z].astype(f32)
    stats = total[2 * D :, D:]
    stats = jnp.concatenate([stats[0:8], stats[8:16]], axis=1)
    for b in range(2):
        first = stats[4 * b : 4 * b + 1] + stats[4 * b + 2 : 4 * b + 3]
        second = stats[4 * b + 1 : 4 * b + 2] + stats[4 * b + 3 : 4 * b + 4]
        inside = total[b * D : (b + 1) * D] - first * sum_ref[...] - second * unit_ref[b]
        grad_ref[b] = (cot_ref[b] + inv_ref[b][0:1] * inside).astype(bf16)
    shards = send_ref.shape[0]
    own = reader_ref.shape[0] - shards
    for p in range(shards):
        block = grad_ref[reader_ref[own + p]]
        send_ref[p] = jnp.where(me_ref[0] != p, block, jnp.zeros((D, B), bf16))


def final_kernel(
    send_ref, slot_ref, count_ref, bias_ref, norm_ref, kv_ref, early_ref, grads_ref,
    query_ref, heads_ref, lse_ref, grad_ref, out_ref, acc_ref, reader_ref, edge_ref,
    held_ref, block_ref, part_ref, sem_ref,
):
    copies = [
        pltpu.make_async_copy(early_ref, block_ref, sem_ref.at[0]),
        pltpu.make_async_copy(grads_ref, part_ref, sem_ref.at[1]),
        pltpu.make_async_copy(norm_ref, held_ref, sem_ref.at[2]),
    ]
    for copy in copies:
        copy.start()
    full = jnp.where(count_ref[0] == FULL, 0, 1)
    fill_tables(slot_ref, bias_ref, full, reader_ref, edge_ref)
    zero = jnp.zeros((D, B), bf16)

    def back(keys, query, heads, shift, grad):
        inner = jnp.sum(grad.astype(f32) * heads.astype(f32), axis=0, keepdims=True)
        pair = jnp.concatenate(
            [jnp.concatenate([query, zero], axis=1), jnp.concatenate([zero, grad], axis=1)], axis=0
        )
        both = dot(keys, pair)
        soft = jnp.exp(both[:, :B] - shift)
        mixed = jnp.concatenate(
            [(soft * (both[:, B:] - inner)).astype(bf16), soft.astype(bf16)], axis=1
        )
        return dot(mixed, pair, NT)

    def own_step(v, carry):
        m = reader_ref[v]
        shift = lse_ref[m][0:1] - edge_ref[v]
        acc_ref[v] = back(kv_ref[v], query_ref[m], heads_ref[m], shift, grad_ref[m])
        return carry

    lax.fori_loop(0, kv_ref.shape[0], own_step, 0, unroll=4)

    def sent_step(r, carry):
        slot = send_ref[r]
        block = block_ref[r]
        tail = block[2 * D :].astype(f32)
        shift = tail[0:1] + tail[1:2] + tail[2:3]
        part = back(kv_ref[slot], block[:D], block[D : 2 * D], shift, part_ref[r])
        acc_ref[slot] = acc_ref[slot] + part
        return carry

    copies[0].wait()
    copies[1].wait()
    lax.fori_loop(0, block_ref.shape[0], sent_step, 0, unroll=4)
    rows = acc_ref[...].reshape(norm_ref.shape[0], 2 * D).astype(bf16)
    copies[2].wait()
    shards, height = out_ref.shape[0], out_ref.shape[1]
    tile = 512
    for c in range(C // tile):
        part = dot(rows, held_ref[:, c * tile : (c + 1) * tile], TN).T
        per = tile // height
        out_ref[c * per : (c + 1) * per] = part.astype(bf16).reshape(per, height, 2 * D)


def output_kernel(me_ref, heads_ref, mine_ref, other_ref, tail_ref, out_ref):
    total = tail_ref[: out_ref.shape[0]]
    even = lax.rem(me_ref[0], 2) == 0
    half = D // 2
    for h in range(heads_ref.shape[0]):
        rows = heads_ref[h, 2 * D :][:, :D]
        low = jnp.where(even, mine_ref[h], other_ref[h])
        high = jnp.where(even, other_ref[h], mine_ref[h])
        total = total + dot(rows[:, :half], low) + dot(rows[:, half:], high)
    out_ref[...] = total.astype(bf16)


def sum_kernel(parts_ref, key_ref, value_ref):
    total = parts_ref[0].astype(f32)
    for i in range(1, parts_ref.shape[0]):
        total = total + parts_ref[i].astype(f32)
    key_ref[...] = total[:, :D]
    value_ref[...] = total[:, D:]


def exchange(array, axis):
    return lax.all_to_all(array, axis, split_axis=0, concat_axis=0, tiled=True)


def on_device(
    grid_feat,
    mesh_feat,
    query_weight,
    key_weight,
    value_weight,
    enc_out_weight,
    layer_query,
    layer_key,
    layer_value,
    layer_out_weight,
    enc_bias,
    layer_bias,
    send_list,
    edge_slot,
    edge_count,
    cotangent,
):
    shards = lax.axis_size("grid")
    parts = lax.axis_size("head")
    own = grid_feat.shape[0] // B
    share = cotangent.shape[0]
    send = send_list[0]
    enc_table = enc_bias[:, :, 0]
    layer_table = layer_bias[:, :, 0]
    shard_at = lax.axis_index("grid").astype(jnp.int32)[None]
    head_at = lax.axis_index("head").astype(jnp.int32)[None]
    forward = [(i, (i + 1) % shards) for i in range(shards)]
    backward = [(t, s) for s, t in forward]

    half = D // 2
    shared_rows = call(
        rows_kernel, struct((D + half + share, C), bf16), [VMEM] * 3, name="rows_part", mib=61
    )(enc_out_weight, layer_out_weight, cotangent)
    gathered = lax.all_gather(shared_rows, "head", axis=0, tiled=False)
    query_weight, key_weight, value_weight, layer_query, layer_key, layer_value = (
        weight.T
        for weight in (query_weight, key_weight, value_weight, layer_query, layer_key, layer_value)
    )

    grid_norm, own_kv, outgoing = grid_part(send, grid_feat, key_weight, value_weight, shards)
    arrived_kv = exchange(outgoing, "grid")
    queries = call(
        query_kernel, struct((2, D, B), bf16), [VMEM] * 2, name="query_part", data=1 << 20
    )(mesh_feat, query_weight)
    tables = [pltpu.SMEM((own + shards,), jnp.int32), pltpu.SMEM((own + shards,), f32)]
    enc_heads, lse, early = call(
        encoder_kernel,
        (
            struct((2, D, B), bf16),
            struct((2, 8, B), f32),
            struct((shards, 2 * D + 16, B), bf16),
        ),
        [SMEM] * 4 + [VMEM] * 3,
        [pltpu.VMEM((own + shards, B, 2 * D), bf16), pltpu.VMEM((FULL, B, B), f32)] + tables,
        name="encoder_part",
    )(edge_slot, edge_count, enc_table, shard_at, own_kv, arrived_kv, queries)
    arrived_early = exchange(early, "grid")
    all_heads = lax.all_gather(enc_heads, "head", axis=0, tiled=False)
    low, high, tail, unit = call(
        middle_kernel,
        (
            struct((3 * B + 32, 2 * D), bf16),
            struct((3 * B + 32, 2 * D), bf16),
            struct((share + 8, C), f32),
            struct((2 * B, C), bf16),
        ),
        [SMEM] * 2 + [VMEM] * 7,
        [pltpu.VMEM((2 * B, C), f32)],
        name="middle_part",
    )(
        head_at, layer_table, all_heads, gathered, mesh_feat, layer_query, layer_key, layer_value, layer_out_weight
    )
    left = lax.ppermute(high, "grid", forward)
    right = lax.ppermute(low, "grid", backward)
    cot_part, unit_part, inverse_row, weight_sum, half_mine = call(
        side_kernel,
        (
            struct((2, D, B), f32),
            struct((2, D, B), f32),
            struct((2, 8, B), f32),
            struct((D, B), f32),
            struct((parts, half, C), bf16),
        ),
        [VMEM] * 4,
        [pltpu.SemaphoreType.DMA],
        out_specs=(VMEM, VMEM, VMEM, VMEM, HBM),
        name="side_part",
    )(gathered, unit, tail, enc_out_weight)
    mixed = call(
        layer_kernel, struct((parts, 2 * D + share, B), bf16), [VMEM] * 9, name="layer_part"
    )(low, high, left, right, unit, layer_query, layer_key, layer_value, gathered)
    arrived_early, mixed = lax.optimization_barrier((arrived_early, mixed))
    arrived_grad = exchange(mixed, "head")
    grads, send_grads = call(
        grad_kernel,
        (struct((2, D, B), bf16), struct((shards, D, B), bf16)),
        [SMEM] * 4 + [VMEM] * 5,
        tables,
        name="grad_part",
    )(
        edge_slot, edge_count, enc_table, shard_at, arrived_grad, cot_part, unit_part,
        inverse_row, weight_sum,
    )
    arrived_grads = exchange(send_grads, "grid")
    half_other = lax.ppermute(half_mine, "grid", [(i, i ^ 1) for i in range(shards)])
    product = call(
        final_kernel,
        struct((shards, C // shards, 2 * D), bf16),
        [SMEM] * 4 + [HBM, VMEM, HBM, HBM] + [VMEM] * 4,
        [pltpu.VMEM((own, B, 2 * D), f32)]
        + tables
        + [
            pltpu.VMEM(grid_norm.shape, bf16),
            pltpu.VMEM((shards, 2 * D + 16, B), bf16),
            pltpu.VMEM((shards, D, B), bf16),
            pltpu.SemaphoreType.DMA((3,)),
        ],
        name="final_part",
        mib=61,
    )(
        send, edge_slot, edge_count, enc_table, grid_norm, own_kv, arrived_early, arrived_grads,
        queries, enc_heads, lse, grads,
    )
    pieces = exchange(product, "grid")
    mesh_out = call(
        output_kernel,
        struct((share, C), bf16),
        [SMEM] + [VMEM] * 4,
        name="output_part",
    )(shard_at, arrived_grad, half_mine, half_other, tail)
    key_grad, value_grad = call(
        sum_kernel,
        (struct((C // shards, D), f32), struct((C // shards, D), f32)),
        [VMEM],
        name="sum_part",
    )(pieces)
    return mesh_out, key_grad, value_grad


def solution(mesh):
    in_specs = (
        P("grid", None),
        P("grid", None),
        P(None, "head"),
        P(None, "head"),
        P(None, "head"),
        P("head", None),
        P(None, "head"),
        P(None, "head"),
        P(None, "head"),
        P("head", None),
        P("grid", None, "head"),
        P("grid", None, "head"),
        P("grid", None),
        P("grid", None),
        P("grid"),
        P(("grid", "head"), None),
    )
    out_specs = (P(("grid", "head"), None), P("grid", "head"), P("grid", "head"))
    return jax.shard_map(
        on_device, mesh=mesh, in_specs=in_specs, out_specs=out_specs, check_vma=False
    )
```
